32 devices in a mesh: gx: 4 (over z), gy: 2 (over x), gz: 4 (over y, core).
Axes of the slice: x: 2, y: 2, z: 4, core: 2. Of those that a mesh axis runs over, the one named last changes fastest.
Arguments:
- elevation: int32 [64, 512], P('gy', ('gx', 'gz')), may hold values from 0 to 499
- layer_base: float32 [64], P('gz'), may hold values from 0.6 to 1.6
- stretch: float32 [64], P('gz'), may hold values from -0.5 to 0.5
- material: int32 [64, 64, 512], P('gz', 'gy', 'gx'), may hold values from 0 to 15
- buoyancy: float32 [16], replicated, may hold values from 0.5 to 2
- lame_lambda: float32 [16], replicated, may hold values from 0.5 to 2
- shear_modulus: float32 [16], replicated, may hold values from 0.3 to 1.5
- relax_time: float32 [16], replicated, may hold values from 0.2 to 30
- anelastic_weight: float32 [16], replicated, may hold values from 0.05 to 0.5
- velocity: float32 [3, 64, 64, 512], P(None, 'gz', 'gy', 'gx'), may hold values from -6 to 6
- stress: float32 [6, 64, 64, 512], P(None, 'gz', 'gy', 'gx'), may hold values from -6 to 6
- memory: float32 [6, 64, 64, 512], P(None, 'gz', 'gy', 'gx'), may hold values from -4 to 4
Outputs:
- velocity_next: float32 [3, 64, 64, 512], P(None, 'gz', 'gy', 'gx')
- stress_next: float32 [6, 64, 64, 512], P(None, 'gz', 'gy', 'gx')
- memory_next: float32 [6, 64, 64, 512], P(None, 'gz', 'gy', 'gx')
The draws below stay inside these ranges and needn't reach their ends.
All inputs are finite; a program needn't handle non-finite values.
Results may differ from the reference program's by a relative error of at most 0.00002.
Values sent between devices are 32-bit elements; how exact they have to be, the bound alone decides.
No kernel may reach another device: no remote copies, remote signals or barrier semaphores. Data moves between devices by JAX's collectives and lax.ppermute only.
A program may use at most 64 MiB of HBM per device.

```python
import math
import jax
import jax.numpy as jnp
from jax import lax

NMAT = 16
NX = 512
NY = 64
NZ = 64


def place_ends(array, stream_key, least, high):
    spot = [jax.random.randint(jax.random.fold_in(stream_key, axis), (), 0, length) for axis, length in enumerate(array.shape)]
    main_axis = array.shape.index(max(array.shape))
    neighbour = spot[:main_axis] + [(spot[main_axis] + 1) % array.shape[main_axis]] + spot[main_axis + 1:]
    return array.at[tuple(spot)].set(least).at[tuple(neighbour)].set(high)


def level_of(rng, extent, cuts, low, largest):
    def one(dim, shards_of):
        steps = jax.random.uniform(jax.random.fold_in(jax.random.fold_in(rng, 6), dim), (shards_of,), jnp.float32, low / len(cuts), largest / len(cuts))
        return jnp.repeat(jnp.exp(steps), extent[dim] // shards_of).reshape((-1,) + (1,) * (len(extent) - dim - 1))

    level = one(*cuts[0])
    for cut in cuts[1:]:
        level = level * one(*cut)
    return level


def scatter_about(stream_key, dims, width, most, cuts=(), held_as=jnp.bfloat16):
    array = jax.random.normal(stream_key, dims, jnp.float32) * width
    if len(cuts) > 0:
        array = level_of(stream_key, dims, cuts, -0.22, 0.18) * array
    return jnp.clip(array, min=-most, max=most).astype(held_as)


def setup_inputs(seed: int = 0) -> dict:
    streams_of = jax.random.split(jax.random.key(seed), 13)
    elevation = place_ends(jax.random.randint(streams_of[0], (NY, NX), 0, 500), jax.random.fold_in(streams_of[0], 1), 0, 499).astype(jnp.int32)
    layer_base = jnp.clip(jnp.exp(math.log(1.6) - 0.98082923 * jax.random.uniform(streams_of[1], (NZ,), jnp.float32) ** level_of(streams_of[1], (NZ,), ((0, 4),), -0.2, 0.2)), 0.6, 1.6)
    stretch = jnp.clip(jax.random.uniform(streams_of[2], (NZ,), jnp.float32, -0.5, 0.5) * level_of(streams_of[2], (NZ,), ((0, 4),), -0.4, 0.0), -0.5, 0.5)
    material = place_ends(jax.random.randint(streams_of[3], (NZ, NY, NX), 0, NMAT), jax.random.fold_in(streams_of[3], 1), 0, NMAT - 1).astype(jnp.int32)
    buoyancy = jnp.clip(jnp.exp(jax.random.uniform(streams_of[4], (NMAT,), jnp.float32, math.log(0.5), math.log(2.0))), 0.5, 2.0)
    lame_lambda = jnp.clip(jnp.exp(jax.random.uniform(streams_of[5], (NMAT,), jnp.float32, math.log(0.5), math.log(2.0))), 0.5, 2.0)
    shear_modulus = jnp.clip(jnp.exp(jax.random.uniform(streams_of[6], (NMAT,), jnp.float32, math.log(0.3), math.log(1.5))), 0.3, 1.5)
    relax_time = jnp.clip(jnp.exp(jax.random.uniform(streams_of[7], (NMAT,), jnp.float32, math.log(0.2), math.log(30.0))), 0.2, 30.0)
    anelastic_weight = jnp.clip(jax.random.uniform(streams_of[8], (NMAT,), jnp.float32, 0.05, 0.5), 0.05, 0.5)
    velocity = scatter_about(streams_of[9], (3, NZ, NY, NX), 1.0, 6.0, ((1, 4), (2, 2), (3, 4)), jnp.float32)
    stress = scatter_about(streams_of[10], (6, NZ, NY, NX), 1.0, 6.0, ((1, 4), (2, 2), (3, 4)), jnp.float32)
    memory = scatter_about(streams_of[11], (6, NZ, NY, NX), 0.5, 4.0, ((1, 4), (2, 2), (3, 4)), jnp.float32)
    return dict(elevation=elevation, layer_base=layer_base, stretch=stretch, material=material, buoyancy=buoyancy, lame_lambda=lame_lambda, shear_modulus=shear_modulus, relax_time=relax_time, anelastic_weight=anelastic_weight, velocity=velocity, stress=stress, memory=memory)


step_size = 0.3
binomial = (1.0, 4.0, 6.0, 4.0, 1.0)


def smooth_axis(values_in, dimension):
    length_out = values_in.shape[dimension] - 4
    summed = jnp.zeros_like(lax.slice_in_dim(values_in, 0, length_out, axis=dimension))
    for offset, weight in enumerate(binomial):
        summed = summed + weight * lax.slice_in_dim(values_in, offset, offset + length_out, axis=dimension)
    return summed / 16.0


def centred(values_in, dimension):
    length_out = values_in.shape[dimension] - 4
    closer = lax.slice_in_dim(values_in, 3, 3 + length_out, axis=dimension) - lax.slice_in_dim(values_in, 1, 1 + length_out, axis=dimension)
    farther = lax.slice_in_dim(values_in, 4, 4 + length_out, axis=dimension) - lax.slice_in_dim(values_in, 0, length_out, axis=dimension)
    return (8.0 * closer - farther) / 12.0


def new_velocity(velocity, grad_x, grad_y, grad_k, metric_x, metric_y, metric_z, buoy_cell):
    accel_x = (grad_x[0] - metric_x * grad_k[0]) + (grad_y[0] - metric_y * grad_k[3]) + metric_z * grad_k[4]
    accel_y = (grad_x[1] - metric_x * grad_k[3]) + (grad_y[1] - metric_y * grad_k[1]) + metric_z * grad_k[5]
    accel_z = (grad_x[2] - metric_x * grad_k[4]) + (grad_y[2] - metric_y * grad_k[5]) + metric_z * grad_k[2]
    return velocity + step_size * buoy_cell[None] * jnp.stack([accel_x, accel_y, accel_z])


def new_stress(stress, memory, vel_x, vel_y, vel_k, metric_x, metric_y, metric_z, properties):
    along_x = vel_x - metric_x[None] * vel_k
    along_y = vel_y - metric_y[None] * vel_k
    along_z = metric_z[None] * vel_k
    lame_cell = properties[1]
    shear_cell = properties[2]
    volume_rate = along_x[0] + along_y[1] + along_z[2]
    elastic_rate = jnp.stack([
        lame_cell * volume_rate + 2.0 * shear_cell * along_x[0],
        lame_cell * volume_rate + 2.0 * shear_cell * along_y[1],
        lame_cell * volume_rate + 2.0 * shear_cell * along_z[2],
        shear_cell * (along_y[0] + along_x[1]),
        shear_cell * (along_z[0] + along_x[2]),
        shear_cell * (along_z[1] + along_y[2]),
    ])
    keep_factor = properties[3][None]
    memory_next = keep_factor * memory + (1.0 - keep_factor) * properties[4][None] * elastic_rate
    stress_next = stress + step_size * (elastic_rate - memory_next)
    return stress_next, memory_next


def reference(elevation, layer_base, stretch, material, buoyancy, lame_lambda, shear_modulus, relax_time, anelastic_weight, velocity, stress, memory):
    height = elevation.astype(jnp.float32) / 200.0
    rimmed = jnp.pad(height, 4)
    surface = smooth_axis(smooth_axis(rimmed, 0), 1)
    slope_x = centred(surface[2:-2, :], 1)
    slope_y = centred(surface[:, 2:-2], 0)
    surface_own = surface[2:-2, 2:-2]
    thickness = layer_base[:, None, None] * jnp.exp(stretch[:, None, None] * surface_own[None])
    weighted = stretch[:, None, None] * thickness
    lift = jnp.cumsum(weighted, axis=0) - 0.5 * weighted
    factor = (lift - 1.0) / thickness
    metric_x = slope_x[None] * factor
    metric_y = slope_y[None] * factor
    metric_z = 1.0 / thickness
    tables = jnp.stack([buoyancy, lame_lambda, shear_modulus, jnp.exp(-step_size / relax_time), anelastic_weight])
    properties = tables[:, material]
    padded = jnp.pad(stress, ((0, 0), (2, 2), (2, 2), (2, 2)))
    stress_x = jnp.concatenate([padded[0:1], padded[3:5]])[:, 2:-2, 2:-2, :]
    stress_y = jnp.concatenate([padded[3:4], padded[1:2], padded[5:6]])[:, 2:-2, :, 2:-2]
    stress_z = padded[:, :, 2:-2, 2:-2]
    velocity_next = new_velocity(velocity, centred(stress_x, 3), centred(stress_y, 2), centred(stress_z, 1), metric_x, metric_y, metric_z, properties[0])
    vel_pad = jnp.pad(velocity_next, ((0, 0), (2, 2), (2, 2), (2, 2)))
    vel_x = centred(vel_pad[:, 2:-2, 2:-2, :], 3)
    vel_y = centred(vel_pad[:, 2:-2, :, 2:-2], 2)
    vel_k = centred(vel_pad[:, :, 2:-2, 2:-2], 1)
    stress_next, memory_next = new_stress(stress, memory, vel_x, vel_y, vel_k, metric_x, metric_y, metric_z, properties)
    return velocity_next, stress_next, memory_next
```

```python
import functools
import jax
import jax.numpy as jnp
from jax import lax
from jax.experimental import pallas as pl
from jax.experimental.pallas import tpu as pltpu
from jax.sharding import PartitionSpec as P

step_size = 0.3
SUB = 8
PAD = 8
F32 = jnp.float32
params = functools.partial(pltpu.CompilerParams, vmem_limit_bytes=48 * 1024 * 1024)
VM = pl.BlockSpec(memory_space=pltpu.VMEM)
SM = pl.BlockSpec(memory_space=pltpu.SMEM)


def ring(n, step):
    return [(i, (i + step) % n) for i in range(n)]


def exchange(axis, n, to_after, to_before):
    if n == 1:
        return to_after, to_before
    if n == 2:
        mine = lax.axis_index(axis)
        got = lax.ppermute(jnp.where(mine == 0, to_after, to_before), axis, ring(2, 1))
        return got, got
    return lax.ppermute(to_after, axis, ring(n, 1)), lax.ppermute(to_before, axis, ring(n, -1))


def lanes_of(shape):
    return lax.broadcasted_iota(jnp.int32, shape, len(shape) - 1)


def terrain_piece_kernel(gz_axis, elev_ref, base_ref, stretch_ref, out_ref):
    mine = lax.axis_index(gz_axis)
    ny, width = elev_ref.shape
    nx = out_ref.shape[1]
    nz = base_ref.shape[1]
    height = elev_ref[...].astype(F32) / 200.0
    wide = jnp.concatenate([height, jnp.zeros((ny, nx - width), F32)], axis=1)
    out_ref[:ny, :] = pltpu.roll(wide, mine * width, 1)
    row = lax.broadcasted_iota(jnp.int32, (SUB, nx), 0)
    fill = jnp.zeros((1, nx - nz), F32)
    base = jnp.concatenate([base_ref[...], fill], axis=1)
    stretch = jnp.concatenate([stretch_ref[...], fill], axis=1)
    both = jnp.where(row == 0, base, jnp.where(row == 1, stretch, 0.0))
    out_ref[ny:, :] = pltpu.roll(both, mine * nz, 1)


def pack_sides(field, nz, ny, nx):
    tiles = ny // SUB
    lane2 = lanes_of((SUB, nx)) // 2
    low, high = [], []
    for c in range(3):
        lo = jnp.zeros((SUB, nx), F32)
        hi = jnp.zeros((SUB, nx), F32)
        for k in range(nz):
            for t in range(tiles):
                m = k * tiles + t
                turned = pltpu.roll(field(c, k, t), (2 * m + 2) % nx, 1)
                hi = jnp.where(lane2 == m, turned, hi)
                lo = jnp.where(lane2 == (m + 1) % (nx // 2), turned, lo)
        low.append(lo)
        high.append(hi)
    return low, high


def pack_kernel(rows_out, stress_ref, low_ref, high_ref, *y_refs):
    _, nz, ny, nx = stress_ref.shape
    of_x = (0, 3, 4)
    of_y = (3, 1, 5)
    low, high = pack_sides(
        lambda c, k, t: stress_ref[of_x[c], k, SUB * t : SUB * t + SUB, :], nz, ny, nx
    )
    for c in range(3):
        low_ref[SUB * c : SUB * c + SUB, :] = low[c]
        high_ref[SUB * c : SUB * c + SUB, :] = high[c]
    for c in range(3):
        for k in range(nz):
            j = 2 * (c * nz + k)
            y_refs[0][j : j + 2, :] = stress_ref[of_y[c], k, ny - 2 : ny, :]
            y_refs[1][j : j + 2, :] = stress_ref[of_y[c], k, 0:2, :]


def y_terrain_kernel(sizes, slab_ref, left_ref, right_ref, after_ref, before_ref):
    n = sizes[0]
    mine = lax.axis_index("gx")
    nx = slab_ref.shape[1]
    ny = slab_ref.shape[0] - SUB
    lane = lanes_of((4, nx))
    for ref, start in ((after_ref, ny - 4), (before_ref, 0)):
        left = jnp.where(mine > 0, left_ref[start : start + 4, :], 0.0)
        right = jnp.where(mine < n - 1, right_ref[start : start + 4, :], 0.0)
        ref[0:4, :] = slab_ref[start : start + 4, :]
        ref[4:8, :] = jnp.where(lane < nx // 2, right, left)


def binomial(at):
    return (at(-2) + at(2) + 4.0 * (at(-1) + at(1)) + 6.0 * at(0)) / 16.0


def centred12(at):
    return 8.0 * (at(1) - at(-1)) - (at(2) - at(-2))


def metric_kernel(
    sizes, layers_ref, slab_ref, left_ref, right_ref, yb_ref, ya_ref, factor_ref, mz_ref, slope_ref,
    own, rim, sown,
):
    n_gx, n_gy = sizes
    gx, gy, gz = lax.axis_index("gx"), lax.axis_index("gy"), lax.axis_index("gz")
    nz, ny, nx = factor_ref.shape
    lane = lanes_of((ny, nx))
    own[PAD : PAD + ny, :] = slab_ref[:ny, :]
    left = jnp.where(gx > 0, left_ref[...], 0.0)
    right = jnp.where(gx < n_gx - 1, right_ref[...], 0.0)
    rim[PAD : PAD + ny, :] = jnp.where(lane < nx // 2, right, left)
    for ref, at in ((own, 0), (rim, 4)):
        ref[PAD - 4 : PAD, :] = jnp.where(gy > 0, yb_ref[at : at + 4, :], 0.0)
        ref[PAD + ny : PAD + ny + 4, :] = jnp.where(gy < n_gy - 1, ya_ref[at : at + 4, :], 0.0)
    rows = ny + 4
    tall_own = binomial(lambda s: own[PAD - 2 + s : PAD - 2 + s + rows, :])
    tall_rim = binomial(lambda s: rim[PAD - 2 + s : PAD - 2 + s + rows, :])

    def shifted(a, b, s):
        ln = lanes_of(a.shape)
        cut = (ln < s) if s > 0 else (ln >= nx + s)
        if s > 0:
            mixed_a, mixed_b = jnp.where(cut, b, a), jnp.where(cut, a, b)
        elif s < 0:
            mixed_a, mixed_b = jnp.where(cut, b, a), jnp.where(cut, a, b)
        else:
            return a, b
        return pltpu.roll(mixed_a, (-s) % nx, 1), pltpu.roll(mixed_b, (-s) % nx, 1)

    def padded_rows(a):
        return jnp.concatenate([a, jnp.zeros((SUB - rows % SUB, nx), F32)], axis=0)

    tall_own, tall_rim = padded_rows(tall_own), padded_rows(tall_rim)
    pairs = {s: shifted(tall_own, tall_rim, s) for s in (-2, -1, 0, 1, 2)}
    surf_own = binomial(lambda s: pairs[s][0])
    surf_rim = binomial(lambda s: pairs[s][1])
    sown[...] = surf_own
    slope_ref[1] = centred12(lambda s: sown[2 + s : 2 + s + ny, :]) / 12.0
    pairs2 = {s: shifted(surf_own, surf_rim, s)[0] for s in (-2, -1, 1, 2)}
    along = centred12(lambda s: pairs2[s]) / 12.0
    surface = sown[2 : 2 + ny, :]
    sown[...] = along
    slope_ref[0] = sown[2 : 2 + ny, :]

    def above(k, total):
        s = layers_ref[1, k]
        return total + (s * layers_ref[0, k]) * jnp.exp(s * surface)

    total = lax.fori_loop(0, gz * nz, above, jnp.zeros((ny, nx), F32))
    for k in range(nz):
        s = layers_ref[1, gz * nz + k]
        thickness = layers_ref[0, gz * nz + k] * jnp.exp(s * surface)
        weighted = s * thickness
        mz = 1.0 / thickness
        lift = total + 0.5 * weighted
        total = total + weighted
        mz_ref[k] = mz
        factor_ref[k] = (lift - 1.0) * mz


def edge_terms(got_left, got_right, low, high):
    dl = got_left - high
    dr = got_right - low
    nx = dl.shape[-1]
    lane = lanes_of(dl.shape)
    even = lane % 2 == 0
    dl = pltpu.roll(dl, 2, 1)
    dr = pltpu.roll(dr, nx - 2, 1)
    to_low = jnp.where(even, dl - 8.0 * pltpu.roll(dl, nx - 1, 1), dl)
    to_high = jnp.where(even, -dr, 8.0 * pltpu.roll(dr, 1, 1) - dr)
    second = (lane // 2) % 2 == 1
    return jnp.where(second, to_low, to_high), jnp.where(second, to_high, to_low)


def along_x(tile, edges, m, lane):
    nx = tile.shape[-1]
    e = pltpu.roll(edges, (2 * nx - 2 - 2 * m) % nx if isinstance(m, int) else 2 * nx - 2 - 2 * m, 1)
    d = 8.0 * (pltpu.roll(tile, nx - 1, 1) - pltpu.roll(tile, 1, 1)) - (
        pltpu.roll(tile, nx - 2, 1) - pltpu.roll(tile, 2, 1)
    )
    return d + jnp.where((lane < 2) | (lane >= nx - 2), e, 0.0)


def lookup(row, tile):
    table = jnp.broadcast_to(row, tile.shape)
    return jnp.take_along_axis(table, tile, axis=1, mode="promise_in_bounds")


def table_rows(refs, nx):
    n = refs[0].shape[1]
    return [jnp.concatenate([r, jnp.zeros((1, nx - n), F32)], axis=1) for r in refs]


def fill_edges(n_gx, edge_ref, got_left_ref, got_right_ref, low_ref, high_ref):
    gx = lax.axis_index("gx")
    for c in range(3):
        at = slice(SUB * c, SUB * c + SUB)
        left = jnp.where(gx > 0, got_left_ref[at, :], 0.0)
        right = jnp.where(gx < n_gx - 1, got_right_ref[at, :], 0.0)
        first, second = edge_terms(left, right, low_ref[at, :], high_ref[at, :])
        edge_ref[c, 0] = first
        edge_ref[c, 1] = second


def fill_rows(n_gy, tall, field, yb_ref, ya_ref, nz, ny):
    gy = lax.axis_index("gy")
    for c in range(3):
        for k in range(nz):
            j = 2 * (c * nz + k)
            tall[c, k, PAD : PAD + ny, :] = field(c, k)
            tall[c, k, PAD - 2 : PAD, :] = jnp.where(gy > 0, yb_ref[j : j + 2, :], 0.0)
            tall[c, k, PAD + ny : PAD + ny + 2, :] = jnp.where(
                gy < n_gy - 1, ya_ref[j : j + 2, :], 0.0
            )


def depth_halos(n_gz, zb, za, zb_ref, za_ref):
    gz = lax.axis_index("gz")
    zb[...] = jnp.where(gz > 0, zb_ref[...], 0.0)
    za[...] = jnp.where(gz < n_gz - 1, za_ref[...], 0.0)


def over_layers(nz, layer):
    for k in (0, 1):
        layer(k)

    @pl.loop(2, nz - 2)
    def _(k):
        layer(k)

    for k in (nz - 2, nz - 1):
        layer(k)


def velocity_kernel(
    sizes, velocity_ref, stress_ref, material_ref, buoy_ref, factor_ref, mz_ref, slope_ref,
    got_left_ref, got_right_ref, low_ref, high_ref, yb_ref, ya_ref, zb_ref, za_ref,
    out_ref, vlow_ref, vhigh_ref, vya_ref, vyb_ref, vza_ref, vzb_ref,
    edge, tall, zb, za,
):
    n_gx, n_gy, n_gz = sizes
    _, nz, ny, nx = velocity_ref.shape
    tiles = ny // SUB
    lane = lanes_of((SUB, nx))
    fill_edges(n_gx, edge, got_left_ref, got_right_ref, low_ref, high_ref)
    of_y = (3, 1, 5)
    fill_rows(n_gy, tall, lambda c, k: stress_ref[of_y[c], k], yb_ref, ya_ref, nz, ny)
    depth_halos(n_gz, zb, za, zb_ref, za_ref)
    (buoy_row,) = table_rows([buoy_ref[...] * (step_size / 12.0)], nx)

    def layer(k):
        def depth(c, t):
            rows = slice(SUB * t, SUB * t + SUB)

            def at(s):
                if isinstance(k, int) and k + s < 0:
                    return zb[c, k + s + 2, rows, :]
                if isinstance(k, int) and k + s >= nz:
                    return za[c, k + s - nz, rows, :]
                return stress_ref[c, k + s, rows, :]

            return centred12(at)

        for t in range(tiles):
            rows = slice(SUB * t, SUB * t + SUB)
            m = k * tiles + t

            def gx_of(c, comp):
                return along_x(stress_ref[comp, k, rows, :], edge[c, t % 2], m, lane)

            def gy_of(c):
                return centred12(
                    lambda s: tall[c, k, PAD + SUB * t + s : PAD + SUB * t + s + SUB, :]
                )

            b = lookup(buoy_row, material_ref[k, rows, :])
            factor = factor_ref[k, rows, :]
            mz = mz_ref[k, rows, :]
            mx = slope_ref[0, rows, :] * factor
            my = slope_ref[1, rows, :] * factor
            gk = [depth(c, t) for c in range(6)]
            accel = (
                gx_of(0, 0) + gy_of(0) - mx * gk[0] - my * gk[3] + mz * gk[4],
                gx_of(1, 3) + gy_of(1) - mx * gk[3] - my * gk[1] + mz * gk[5],
                gx_of(2, 4) + gy_of(2) - mx * gk[4] - my * gk[5] + mz * gk[2],
            )
            for c in range(3):
                out_ref[c, k, rows, :] = velocity_ref[c, k, rows, :] + b * accel[c]

    over_layers(nz, layer)
    low, high = pack_sides(lambda c, k, t: out_ref[c, k, SUB * t : SUB * t + SUB, :], nz, ny, nx)
    for c in range(3):
        vlow_ref[SUB * c : SUB * c + SUB, :] = low[c]
        vhigh_ref[SUB * c : SUB * c + SUB, :] = high[c]
        for k in range(nz):
            j = 2 * (c * nz + k)
            vya_ref[j : j + 2, :] = out_ref[c, k, ny - 2 : ny, :]
            vyb_ref[j : j + 2, :] = out_ref[c, k, 0:2, :]
    vza_ref[...] = out_ref[:, nz - 2 : nz]
    vzb_ref[...] = out_ref[:, 0:2]


def stress_kernel(
    sizes, vel_ref, stress_ref, memory_ref, material_ref, lam_ref, mu_ref, relax_ref, weight_ref,
    factor_ref, mz_ref, slope_ref, got_left_ref, got_right_ref, low_ref, high_ref, yb_ref, ya_ref, zb_ref, za_ref,
    stress_out, memory_out, edge, tall, zb, za,
):
    n_gx, n_gy, n_gz = sizes
    _, nz, ny, nx = vel_ref.shape
    tiles = ny // SUB
    lane = lanes_of((SUB, nx))
    fill_edges(n_gx, edge, got_left_ref, got_right_ref, low_ref, high_ref)
    fill_rows(n_gy, tall, lambda c, k: vel_ref[c, k], yb_ref, ya_ref, nz, ny)
    depth_halos(n_gz, zb, za, zb_ref, za_ref)
    keep1 = jnp.exp(-step_size / relax_ref[...])
    lam_row, mu_row, keep_row, gain_row = table_rows(
        [lam_ref[...] / 12.0, mu_ref[...] / 12.0, keep1, (1.0 - keep1) * weight_ref[...]], nx
    )

    def layer(k):
        for t in range(tiles):
            rows = slice(SUB * t, SUB * t + SUB)
            m = k * tiles + t
            kind = material_ref[k, rows, :]
            factor = factor_ref[k, rows, :]
            mz = mz_ref[k, rows, :]
            mx = slope_ref[0, rows, :] * factor
            my = slope_ref[1, rows, :] * factor

            def depth(c):
                def at(s):
                    if isinstance(k, int) and k + s < 0:
                        return zb[c, k + s + 2, rows, :]
                    if isinstance(k, int) and k + s >= nz:
                        return za[c, k + s - nz, rows, :]
                    return vel_ref[c, k + s, rows, :]

                return centred12(at)

            dk = [depth(c) for c in range(3)]
            dx = [
                along_x(vel_ref[c, k, rows, :], edge[c, t % 2], m, lane) - mx * dk[c]
                for c in range(3)
            ]
            dy = [
                centred12(lambda s: tall[c, k, PAD + SUB * t + s : PAD + SUB * t + s + SUB, :])
                - my * dk[c]
                for c in range(3)
            ]
            dz = [mz * dk[c] for c in range(3)]
            lam = lookup(lam_row, kind)
            mu = lookup(mu_row, kind)
            keep = lookup(keep_row, kind)
            gain = lookup(gain_row, kind)
            volume = lam * (dx[0] + dy[1] + dz[2])
            mu2 = mu + mu
            rates = (
                volume + mu2 * dx[0],
                volume + mu2 * dy[1],
                volume + mu2 * dz[2],
                mu * (dy[0] + dx[1]),
                mu * (dz[0] + dx[2]),
                mu * (dz[1] + dy[2]),
            )
            for c in range(6):
                kept = keep * memory_ref[c, k, rows, :] + gain * rates[c]
                memory_out[c, k, rows, :] = kept
                stress_out[c, k, rows, :] = stress_ref[c, k, rows, :] + step_size * (
                    rates[c] - kept
                )

    over_layers(nz, layer)


def call(kernel, outs, in_specs, scratch=(), name=None):
    return pl.pallas_call(
        kernel,
        out_shape=[jax.ShapeDtypeStruct(s, F32) for s in outs],
        in_specs=in_specs,
        out_specs=[VM] * len(outs),
        scratch_shapes=list(scratch),
        compiler_params=params(),
        name=name,
    )


def local(
    n_gx, n_gy, n_gz, elevation, layer_base, stretch, material, buoyancy, lame_lambda, shear_modulus,
    relax_time, anelastic_weight, velocity, stress, memory,
):
    _, nz, ny, nx = velocity.shape
    rows = ny + SUB
    slab = call(
        functools.partial(terrain_piece_kernel, "gz"), [(rows, nx)], [VM] * 3, name="terrain_piece"
    )(elevation, layer_base[None], stretch[None])[0]
    faces = 2 * 3 * nz
    low, high, y_up, y_down = call(
        functools.partial(pack_kernel, faces),
        [(3 * SUB, nx), (3 * SUB, nx), (faces, nx), (faces, nx)],
        [VM],
        name="pack_stress",
    )(stress)
    if n_gz & (n_gz - 1):
        slab = lax.psum(slab, "gz")
    else:
        bit = 1
        while bit < n_gz:
            slab = slab + lax.ppermute(slab, "gz", [(i, i ^ bit) for i in range(n_gz)])
            bit *= 2
    height = slab[:ny]
    from_left, from_right = exchange(
        "gx", n_gx, jnp.concatenate([high, height]), jnp.concatenate([low, height])
    )
    zb, za = exchange("gz", n_gz, stress[:, nz - 2 :], stress[:, :2])
    xs = 3 * SUB
    left_slab, right_slab = from_left[xs:], from_right[xs:]
    t_after, t_before = call(
        functools.partial(y_terrain_kernel, (n_gx,)),
        [(SUB, nx), (SUB, nx)],
        [VM] * 3,
        name="y_terrain",
    )(slab, left_slab, right_slab)
    from_b, from_a = exchange(
        "gy", n_gy, jnp.concatenate([y_up, t_after]), jnp.concatenate([y_down, t_before])
    )
    factor, mz, slope = call(
        functools.partial(metric_kernel, (n_gx, n_gy)),
        [(nz, ny, nx), (nz, ny, nx), (2, ny, nx)],
        [SM] + [VM] * 5,
        [
            pltpu.VMEM((ny + 2 * PAD, nx), F32),
            pltpu.VMEM((ny + 2 * PAD, nx), F32),
            pltpu.VMEM((ny + PAD, nx), F32),
        ],
        name="metrics",
    )(slab[ny:], slab, left_slab, right_slab, from_b[faces:], from_a[faces:])
    sizes = (n_gx, n_gy, n_gz)

    def scratch(comps):
        return [
            pltpu.VMEM((3, 2, SUB, nx), F32),
            pltpu.VMEM((3, nz, ny + 2 * PAD, nx), F32),
            pltpu.VMEM((comps, 2, ny, nx), F32),
            pltpu.VMEM((comps, 2, ny, nx), F32),
        ]

    vel, vlow, vhigh, vya, vyb, vza, vzb = call(
        functools.partial(velocity_kernel, sizes),
        [velocity.shape, (xs, nx), (xs, nx), (faces, nx), (faces, nx), (3, 2, ny, nx), (3, 2, ny, nx)],
        [VM] * 15,
        scratch(6),
        name="velocity",
    )(
        velocity, stress, material, buoyancy[None], factor, mz, slope, from_left, from_right, low, high,
        from_b, from_a, zb, za,
    )
    v_left, v_right = exchange("gx", n_gx, vhigh, vlow)
    v_zb, v_za = exchange("gz", n_gz, vza, vzb)
    v_yb, v_ya = exchange("gy", n_gy, vya, vyb)
    stress_next, memory_next = call(
        functools.partial(stress_kernel, sizes),
        [stress.shape, stress.shape],
        [VM] * 19,
        scratch(3),
        name="stress",
    )(
        vel, stress, memory, material, lame_lambda[None], shear_modulus[None], relax_time[None],
        anelastic_weight[None], factor, mz, slope, v_left, v_right, vlow, vhigh, v_yb, v_ya, v_zb, v_za,
    )
    return vel, stress_next, memory_next


def solution(mesh):
    sizes = mesh.shape
    field = P(None, "gz", "gy", "gx")
    return jax.shard_map(
        functools.partial(local, sizes["gx"], sizes["gy"], sizes["gz"]),
        mesh=mesh,
        in_specs=(
            P("gy", ("gx", "gz")), P("gz"), P("gz"), P("gz", "gy", "gx"),
            P(), P(), P(), P(), P(), field, field, field,
        ),
        out_specs=(field, field, field),
        check_vma=False,
    )
```

```python
import functools
import jax
import jax.numpy as jnp
import numpy as np
from jax import lax
from jax.experimental import pallas as pl
from jax.experimental.pallas import tpu as pltpu
from jax.sharding import PartitionSpec as P

step_size = 0.3
SUB = 8
PAD = 8
F32 = jnp.float32
params = functools.partial(pltpu.CompilerParams, vmem_limit_bytes=48 * 1024 * 1024)
VM = pl.BlockSpec(memory_space=pltpu.VMEM)
SM = pl.BlockSpec(memory_space=pltpu.SMEM)
HB = pl.BlockSpec(memory_space=pltpu.HBM)
DMA = pltpu.SemaphoreType.DMA


def pair_swaps(sizes, axis):
    names = tuple(sizes)
    shape = tuple(sizes.values())
    index = names.index(axis)
    n = shape[index]
    others = [d for d in (2, 1, 0) if d != index and shape[d] % 2 == 0]
    rounds = []
    for first in (0, 1)[: max(0, min(2, n - 1))]:
        table = []
        for spot in np.ndindex(*shape):
            mate = spot[index] + 1 if spot[index] % 2 == first else spot[index] - 1
            target = list(spot)
            if 0 <= mate < n:
                target[index] = mate
            elif others:
                target[others[0]] ^= 1
            else:
                continue
            table.append((int(np.ravel_multi_index(spot, shape)), int(np.ravel_multi_index(tuple(target), shape))))
        rounds.append(table)
    return rounds


def exchange(sizes, axis, first, second):
    rounds = pair_swaps(sizes, axis)
    got = [lax.ppermute(v, tuple(sizes), r) for v, r in zip((first, second), rounds)]
    return (got[0], got[-1]) if got else (first, second)


def even(axis):
    return lax.axis_index(axis) % 2 == 0


def from_before(axis, got):
    value = jnp.where(even(axis), got[1], got[0])
    return jnp.where(lax.axis_index(axis) > 0, value, 0.0)


def from_after(axis, n, got):
    value = jnp.where(even(axis), got[0], got[1])
    return jnp.where(lax.axis_index(axis) < n - 1, value, 0.0)


def order(axis, to_after, to_before):
    e = even(axis)
    return jnp.where(e, to_after, to_before), jnp.where(e, to_before, to_after)


def lanes_of(shape):
    return lax.broadcasted_iota(jnp.int32, shape, len(shape) - 1)


def terrain_piece_kernel(elev_hbm, base_hbm, stretch_hbm, out_ref, elev_ref, base_ref, stretch_ref, sems):
    mine = lax.axis_index("gz")
    pairs = ((elev_hbm, elev_ref), (base_hbm, base_ref), (stretch_hbm, stretch_ref))
    copies = [pltpu.make_async_copy(a, b, sems.at[i]) for i, (a, b) in enumerate(pairs)]
    for copy in copies:
        copy.start()
    for copy in copies:
        copy.wait()
    ny, width = elev_ref.shape
    nx = out_ref.shape[1]
    nz = base_ref.shape[1]
    height = elev_ref[...].astype(F32) / 200.0
    wide = jnp.concatenate([height, jnp.zeros((ny, nx - width), F32)], axis=1)
    out_ref[:ny, :] = pltpu.roll(wide, mine * width, 1)
    row = lax.broadcasted_iota(jnp.int32, (SUB, nx), 0)
    fill = jnp.zeros((1, nx - nz), F32)
    base = jnp.concatenate([base_ref[...], fill], axis=1)
    stretch = jnp.concatenate([stretch_ref[...], fill], axis=1)
    both = jnp.where(row == 0, base, jnp.where(row == 1, stretch, 0.0))
    out_ref[ny:, :] = pltpu.roll(both, mine * nz, 1)


def pack_sides(field, nz, ny, nx, low_ref, high_ref, out1_ref, out2_ref):
    tiles = ny // SUB
    lane2 = lanes_of((SUB, nx)) // 2
    for c in range(3):
        lo = jnp.zeros((SUB, nx), F32)
        hi = jnp.zeros((SUB, nx), F32)
        for k in range(nz):
            for t in range(tiles):
                m = k * tiles + t
                turned = pltpu.roll(field(c, k, t), (2 * m + 2) % nx, 1)
                hi = jnp.where(lane2 == m, turned, hi)
                lo = jnp.where(lane2 == (m + 1) % (nx // 2), turned, lo)
        at = slice(SUB * c, SUB * c + SUB)
        low_ref[at, :] = lo
        high_ref[at, :] = hi
        out1_ref[at, :], out2_ref[at, :] = order("gx", hi, lo)


def pack_rows(field, nz, ny, y1_ref, y2_ref):
    for c in range(3):
        for k in range(nz):
            j = 2 * (c * nz + k)
            one, two = order("gy", field(c, k, slice(ny - 2, ny)), field(c, k, slice(0, 2)))
            y1_ref[j : j + 2, :] = one
            y2_ref[j : j + 2, :] = two


def pack_kernel(
    stress_hbm, stress_ref, low_ref, high_ref, out1_ref, out2_ref, y1_ref, y2_ref, z1_ref, z2_ref, sems
):
    comps, nz, ny, nx = stress_ref.shape
    copies = [
        pltpu.make_async_copy(stress_hbm.at[c], stress_ref.at[c], sems.at[c]) for c in range(comps)
    ]
    z_even = even("gz")
    z1_at = jnp.where(z_even, nz - 2, 0)
    z2_at = jnp.where(z_even, 0, nz - 2)
    z_copies = [
        pltpu.make_async_copy(stress_hbm.at[:, pl.ds(z1_at, 2)], z1_ref, sems.at[comps]),
        pltpu.make_async_copy(stress_hbm.at[:, pl.ds(z2_at, 2)], z2_ref, sems.at[comps + 1]),
    ]
    of_x = (0, 3, 4)
    of_y = (3, 1, 5)
    loading = (0, 3, 4, 1, 5, 2)
    for c in loading[:5]:
        copies[c].start()
    for copy in z_copies:
        copy.start()
    copies[2].start()
    for c in of_x:
        copies[c].wait()
    x_even = even("gx")
    pack_sides(
        lambda c, k, t: stress_ref[of_x[c], k, SUB * t : SUB * t + SUB, :],
        nz, ny, nx, low_ref, high_ref, out1_ref, out2_ref,
    )
    copies[1].wait()
    copies[5].wait()
    pack_rows(lambda c, k, rows: stress_ref[of_y[c], k, rows, :], nz, ny, y1_ref, y2_ref)
    copies[2].wait()
    for copy in z_copies:
        copy.wait()


def y_terrain_kernel(n_gx, slab_ref, got1_ref, got2_ref, one_ref, two_ref):
    nx = slab_ref.shape[1]
    ny = slab_ref.shape[0] - SUB
    lane = lanes_of((4, nx))
    sent = []
    for start in (ny - 4, 0):
        rows = slice(start, start + 4)
        got = (got1_ref[rows, :], got2_ref[rows, :])
        rim = jnp.where(lane < nx // 2, from_after("gx", n_gx, got), from_before("gx", got))
        sent.append((slab_ref[rows, :], rim))
    for i in range(2):
        one_ref[4 * i : 4 * i + 4, :], two_ref[4 * i : 4 * i + 4, :] = order(
            "gy", sent[0][i], sent[1][i]
        )


def binomial(at):
    return (at(-2) + at(2) + 4.0 * (at(-1) + at(1)) + 6.0 * at(0)) / 16.0


def centred12(at):
    return 8.0 * (at(1) - at(-1)) - (at(2) - at(-2))


def metric_kernel(
    sizes, layers_ref, slab_ref, x1_ref, x2_ref, y1_ref, y2_ref, velocity_hbm, factor_ref, mz_ref, slope_ref,
    velocity_ref, own, rim, sown, sem,
):
    n_gx, n_gy, _ = sizes
    load = pltpu.make_async_copy(velocity_hbm, velocity_ref, sem)
    load.start()
    gz = lax.axis_index("gz")
    nz, ny, nx = factor_ref.shape
    lane = lanes_of((ny, nx))
    own[PAD : PAD + ny, :] = slab_ref[:ny, :]
    got = (x1_ref[...], x2_ref[...])
    rim[PAD : PAD + ny, :] = jnp.where(
        lane < nx // 2, from_after("gx", n_gx, got), from_before("gx", got)
    )
    for ref, at in ((own, 0), (rim, 4)):
        got = (y1_ref[at : at + 4, :], y2_ref[at : at + 4, :])
        ref[PAD - 4 : PAD, :] = from_before("gy", got)
        ref[PAD + ny : PAD + ny + 4, :] = from_after("gy", n_gy, got)
    rows = ny + 4
    tall_own = binomial(lambda s: own[PAD - 2 + s : PAD - 2 + s + rows, :])
    tall_rim = binomial(lambda s: rim[PAD - 2 + s : PAD - 2 + s + rows, :])

    def shifted(a, b, s):
        ln = lanes_of(a.shape)
        cut = (ln < s) if s > 0 else (ln >= nx + s)
        if s > 0:
            mixed_a, mixed_b = jnp.where(cut, b, a), jnp.where(cut, a, b)
        elif s < 0:
            mixed_a, mixed_b = jnp.where(cut, b, a), jnp.where(cut, a, b)
        else:
            return a, b
        return pltpu.roll(mixed_a, (-s) % nx, 1), pltpu.roll(mixed_b, (-s) % nx, 1)

    def padded_rows(a):
        return jnp.concatenate([a, jnp.zeros((SUB - rows % SUB, nx), F32)], axis=0)

    tall_own, tall_rim = padded_rows(tall_own), padded_rows(tall_rim)
    pairs = {s: shifted(tall_own, tall_rim, s) for s in (-2, -1, 0, 1, 2)}
    surf_own = binomial(lambda s: pairs[s][0])
    surf_rim = binomial(lambda s: pairs[s][1])
    sown[...] = surf_own
    slope_ref[1] = centred12(lambda s: sown[2 + s : 2 + s + ny, :]) / 12.0
    pairs2 = {s: shifted(surf_own, surf_rim, s)[0] for s in (-2, -1, 1, 2)}
    along = centred12(lambda s: pairs2[s]) / 12.0
    surface = sown[2 : 2 + ny, :]
    sown[...] = along
    slope_ref[0] = sown[2 : 2 + ny, :]

    def above(k, total):
        s = layers_ref[1, k]
        return total + (s * layers_ref[0, k]) * jnp.exp(s * surface)

    total = lax.fori_loop(0, gz * nz, above, jnp.zeros((ny, nx), F32))
    for k in range(nz):
        s = layers_ref[1, gz * nz + k]
        thickness = layers_ref[0, gz * nz + k] * jnp.exp(s * surface)
        weighted = s * thickness
        mz = 1.0 / thickness
        lift = total + 0.5 * weighted
        total = total + weighted
        mz_ref[k] = mz
        factor_ref[k] = (lift - 1.0) * mz
    load.wait()


def edge_terms(got_left, got_right, low, high):
    dl = got_left - high
    dr = got_right - low
    nx = dl.shape[-1]
    lane = lanes_of(dl.shape)
    even = lane % 2 == 0
    dl = pltpu.roll(dl, 2, 1)
    dr = pltpu.roll(dr, nx - 2, 1)
    to_low = jnp.where(even, dl - 8.0 * pltpu.roll(dl, nx - 1, 1), dl)
    to_high = jnp.where(even, -dr, 8.0 * pltpu.roll(dr, 1, 1) - dr)
    second = (lane // 2) % 2 == 1
    return jnp.where(second, to_low, to_high), jnp.where(second, to_high, to_low)


def along_x(tile, edges, m, lane):
    nx = tile.shape[-1]
    e = pltpu.roll(edges, (2 * nx - 2 - 2 * m) % nx if isinstance(m, int) else 2 * nx - 2 - 2 * m, 1)
    d = 8.0 * (pltpu.roll(tile, nx - 1, 1) - pltpu.roll(tile, 1, 1)) - (
        pltpu.roll(tile, nx - 2, 1) - pltpu.roll(tile, 2, 1)
    )
    return d + jnp.where((lane < 2) | (lane >= nx - 2), e, 0.0)


def lookup(row, tile):
    table = jnp.broadcast_to(row, tile.shape)
    return jnp.take_along_axis(table, tile, axis=1, mode="promise_in_bounds")


def table_rows(refs, nx):
    n = refs[0].shape[1]
    return [jnp.concatenate([r, jnp.zeros((1, nx - n), F32)], axis=1) for r in refs]


def fill_edges(n_gx, edge_ref, x1_ref, x2_ref, low_ref, high_ref):
    for c in range(3):
        at = slice(SUB * c, SUB * c + SUB)
        got = (x1_ref[at, :], x2_ref[at, :])
        first, second = edge_terms(
            from_before("gx", got), from_after("gx", n_gx, got), low_ref[at, :], high_ref[at, :]
        )
        edge_ref[c, 0] = first
        edge_ref[c, 1] = second


def fill_rows(n_gy, tall, field, y1_ref, y2_ref, nz, ny):
    for c in range(3):
        for k in range(nz):
            j = 2 * (c * nz + k)
            got = (y1_ref[j : j + 2, :], y2_ref[j : j + 2, :])
            tall[c, k, PAD : PAD + ny, :] = field(c, k)
            tall[c, k, PAD - 2 : PAD, :] = from_before("gy", got)
            tall[c, k, PAD + ny : PAD + ny + 2, :] = from_after("gy", n_gy, got)


def depth_halos(n_gz, zb, za, z1_ref, z2_ref):
    got = (z1_ref[...], z2_ref[...])
    zb[...] = from_before("gz", got)
    za[...] = from_after("gz", n_gz, got)


def over_layers(nz, layer):
    for k in (0, 1):
        layer(k)

    @pl.loop(2, nz - 2)
    def _(k):
        layer(k)

    for k in (nz - 2, nz - 1):
        layer(k)


def velocity_kernel(
    sizes, velocity_ref, stress_ref, material_ref, buoy_ref, factor_ref, mz_ref, slope_ref,
    x1_ref, x2_ref, low_ref, high_ref, y1_ref, y2_ref, z1_ref, z2_ref,
    out_ref, vlow_ref, vhigh_ref, vx1_ref, vx2_ref, vy1_ref, vy2_ref, vz1_ref, vz2_ref,
    edge, tall, zb, za,
):
    n_gx, n_gy, n_gz = sizes
    _, nz, ny, nx = velocity_ref.shape
    tiles = ny // SUB
    lane = lanes_of((SUB, nx))
    fill_edges(n_gx, edge, x1_ref, x2_ref, low_ref, high_ref)
    of_y = (3, 1, 5)
    fill_rows(n_gy, tall, lambda c, k: stress_ref[of_y[c], k], y1_ref, y2_ref, nz, ny)
    depth_halos(n_gz, zb, za, z1_ref, z2_ref)
    (buoy_row,) = table_rows([buoy_ref[...] * (step_size / 12.0)], nx)

    def layer(k):
        def depth(c, t):
            rows = slice(SUB * t, SUB * t + SUB)

            def at(s):
                if isinstance(k, int) and k + s < 0:
                    return zb[c, k + s + 2, rows, :]
                if isinstance(k, int) and k + s >= nz:
                    return za[c, k + s - nz, rows, :]
                return stress_ref[c, k + s, rows, :]

            return centred12(at)

        for t in range(tiles):
            rows = slice(SUB * t, SUB * t + SUB)
            m = k * tiles + t

            def gx_of(c, comp):
                return along_x(stress_ref[comp, k, rows, :], edge[c, t % 2], m, lane)

            def gy_of(c):
                return centred12(
                    lambda s: tall[c, k, PAD + SUB * t + s : PAD + SUB * t + s + SUB, :]
                )

            b = lookup(buoy_row, material_ref[k, rows, :])
            factor = factor_ref[k, rows, :]
            mz = mz_ref[k, rows, :]
            mx = slope_ref[0, rows, :] * factor
            my = slope_ref[1, rows, :] * factor
            gk = [depth(c, t) for c in range(6)]
            accel = (
                gx_of(0, 0) + gy_of(0) - mx * gk[0] - my * gk[3] + mz * gk[4],
                gx_of(1, 3) + gy_of(1) - mx * gk[3] - my * gk[1] + mz * gk[5],
                gx_of(2, 4) + gy_of(2) - mx * gk[4] - my * gk[5] + mz * gk[2],
            )
            for c in range(3):
                out_ref[c, k, rows, :] = velocity_ref[c, k, rows, :] + b * accel[c]

    over_layers(nz, layer)
    pack_sides(
        lambda c, k, t: out_ref[c, k, SUB * t : SUB * t + SUB, :],
        nz, ny, nx, vlow_ref, vhigh_ref, vx1_ref, vx2_ref,
    )
    pack_rows(lambda c, k, rows: out_ref[c, k, rows, :], nz, ny, vy1_ref, vy2_ref)
    vz1_ref[...], vz2_ref[...] = order("gz", out_ref[:, nz - 2 : nz], out_ref[:, 0:2])


def stress_kernel(
    sizes, vel_ref, stress_ref, memory_ref, material_ref, lam_ref, mu_ref, relax_ref, weight_ref,
    factor_ref, mz_ref, slope_ref, x1_ref, x2_ref, low_ref, high_ref, y1_ref, y2_ref, z1_ref, z2_ref,
    vel_hbm, stress_hbm, memory_hbm, edge, tall, zb, za, stress_out, memory_out, sems,
):
    n_gx, n_gy, n_gz = sizes
    _, nz, ny, nx = vel_ref.shape
    vel_copy = pltpu.make_async_copy(vel_ref, vel_hbm, sems.at[0, 0])
    vel_copy.start()

    def out_copies(first, count, spot):
        layers = pl.ds(first, count)
        return [
            pltpu.make_async_copy(a.at[:, layers], b.at[:, layers], sems.at[i, spot])
            for i, (a, b) in enumerate(((stress_out, stress_hbm), (memory_out, memory_hbm)))
        ]

    tiles = ny // SUB
    lane = lanes_of((SUB, nx))
    fill_edges(n_gx, edge, x1_ref, x2_ref, low_ref, high_ref)
    fill_rows(n_gy, tall, lambda c, k: vel_ref[c, k], y1_ref, y2_ref, nz, ny)
    depth_halos(n_gz, zb, za, z1_ref, z2_ref)
    keep1 = jnp.exp(-step_size / relax_ref[...])
    lam_row, mu_row, keep_row, gain_row = table_rows(
        [lam_ref[...] / 12.0, mu_ref[...] / 12.0, keep1, (1.0 - keep1) * weight_ref[...]], nx
    )

    def layer(k):
        for t in range(tiles):
            rows = slice(SUB * t, SUB * t + SUB)
            m = k * tiles + t
            kind = material_ref[k, rows, :]
            factor = factor_ref[k, rows, :]
            mz = mz_ref[k, rows, :]
            mx = slope_ref[0, rows, :] * factor
            my = slope_ref[1, rows, :] * factor

            def depth(c):
                def at(s):
                    if isinstance(k, int) and k + s < 0:
                        return zb[c, k + s + 2, rows, :]
                    if isinstance(k, int) and k + s >= nz:
                        return za[c, k + s - nz, rows, :]
                    return vel_ref[c, k + s, rows, :]

                return centred12(at)

            dk = [depth(c) for c in range(3)]
            dx = [
                along_x(vel_ref[c, k, rows, :], edge[c, t % 2], m, lane) - mx * dk[c]
                for c in range(3)
            ]
            dy = [
                centred12(lambda s: tall[c, k, PAD + SUB * t + s : PAD + SUB * t + s + SUB, :])
                - my * dk[c]
                for c in range(3)
            ]
            dz = [mz * dk[c] for c in range(3)]
            lam = lookup(lam_row, kind)
            mu = lookup(mu_row, kind)
            keep = lookup(keep_row, kind)
            gain = lookup(gain_row, kind)
            volume = lam * (dx[0] + dy[1] + dz[2])
            mu2 = mu + mu
            rates = (
                volume + mu2 * dx[0],
                volume + mu2 * dy[1],
                volume + mu2 * dz[2],
                mu * (dy[0] + dx[1]),
                mu * (dz[0] + dx[2]),
                mu * (dz[1] + dy[2]),
            )
            for c in range(6):
                kept = keep * memory_ref[c, k, rows, :] + gain * rates[c]
                memory_out[c, k, rows, :] = kept
                stress_out[c, k, rows, :] = stress_ref[c, k, rows, :] + step_size * (
                    rates[c] - kept
                )

    inner = nz - 4
    step = next(d for d in (4, 3, 2, 1) if inner % d == 0)
    chunks = inner // step
    layer(0)
    layer(1)
    for copy in out_copies(0, 2, 1):
        copy.start()

    @pl.loop(0, chunks)
    def _(j):
        @pl.loop(0, step)
        def _(k):
            layer(2 + j * step + k)

        for copy in out_copies(2 + j * step, step, 2 + j):
            copy.start()

    layer(nz - 2)
    layer(nz - 1)
    for copy in out_copies(nz - 2, 2, 2 + chunks):
        copy.start()
    vel_copy.wait()
    for copy in out_copies(0, 2, 1) + out_copies(nz - 2, 2, 2 + chunks):
        copy.wait()

    @pl.loop(0, chunks)
    def _(j):
        for copy in out_copies(2 + j * step, step, 2 + j):
            copy.wait()


def call(kernel, outs, in_specs, scratch=(), name=None, out_specs=None):
    return pl.pallas_call(
        kernel,
        out_shape=[jax.ShapeDtypeStruct(s, F32) for s in outs],
        in_specs=in_specs,
        out_specs=out_specs or [VM] * len(outs),
        scratch_shapes=list(scratch),
        compiler_params=params(),
        name=name,
    )


def local(
    sizes, elevation, layer_base, stretch, material, buoyancy, lame_lambda, shear_modulus,
    relax_time, anelastic_weight, velocity, stress, memory,
):
    n_gx, n_gy, n_gz = counts = tuple(sizes[a] for a in ("gx", "gy", "gz"))
    _, nz, ny, nx = velocity.shape
    rows = ny + SUB
    slab = call(
        terrain_piece_kernel,
        [(rows, nx)],
        [HB] * 3,
        [
            pltpu.VMEM(elevation.shape, jnp.int32),
            pltpu.VMEM((1, nz), F32),
            pltpu.VMEM((1, nz), F32),
            DMA((3,)),
        ],
        name="terrain_piece",
    )(elevation, layer_base[None], stretch[None])[0]
    faces = 2 * 3 * nz
    xs = 3 * SUB
    z_face = (6, 2, ny, nx)
    stress_vm, low, high, x1, x2, y1, y2, z1, z2 = call(
        pack_kernel,
        [stress.shape] + [(xs, nx)] * 4 + [(faces, nx)] * 2 + [z_face] * 2,
        [HB],
        [DMA((8,))],
        name="pack_stress",
    )(stress)
    if n_gz & (n_gz - 1):
        slab = lax.psum(slab, "gz")
    else:
        bit = 1
        while bit < n_gz:
            slab = slab + lax.ppermute(slab, "gz", [(i, i ^ bit) for i in range(n_gz)])
            bit *= 2
    height = slab[:ny]
    z1, z2 = exchange(sizes, "gz", z1, z2)
    x1, x2 = exchange(sizes, "gx", jnp.concatenate([x1, height]), jnp.concatenate([x2, height]))
    t1, t2 = call(
        functools.partial(y_terrain_kernel, n_gx),
        [(SUB, nx), (SUB, nx)],
        [VM] * 3,
        name="y_terrain",
    )(slab, x1[xs:], x2[xs:])
    y1, y2 = exchange(sizes, "gy", jnp.concatenate([y1, t1]), jnp.concatenate([y2, t2]))
    factor, mz, slope, velocity_vm = call(
        functools.partial(metric_kernel, counts),
        [(nz, ny, nx), (nz, ny, nx), (2, ny, nx), velocity.shape],
        [SM] + [VM] * 5 + [HB],
        [
            pltpu.VMEM((ny + 2 * PAD, nx), F32),
            pltpu.VMEM((ny + 2 * PAD, nx), F32),
            pltpu.VMEM((ny + PAD, nx), F32),
            DMA,
        ],
        name="metrics",
    )(slab[ny:], slab, x1[xs:], x2[xs:], y1[faces:], y2[faces:], velocity)

    def scratch(comps):
        return [
            pltpu.VMEM((3, 2, SUB, nx), F32),
            pltpu.VMEM((3, nz, ny + 2 * PAD, nx), F32),
            pltpu.VMEM((comps, 2, ny, nx), F32),
            pltpu.VMEM((comps, 2, ny, nx), F32),
        ]

    vel, vlow, vhigh, vx1, vx2, vy1, vy2, vz1, vz2 = call(
        functools.partial(velocity_kernel, counts),
        [velocity.shape] + [(xs, nx)] * 4 + [(faces, nx)] * 2 + [(3, 2, ny, nx)] * 2,
        [VM] * 15,
        scratch(6),
        name="velocity",
    )(
        velocity_vm, stress_vm, material, buoyancy[None], factor, mz, slope, x1, x2, low, high,
        y1, y2, z1, z2,
    )
    vx1, vx2 = exchange(sizes, "gx", vx1, vx2)
    vy1, vy2 = exchange(sizes, "gy", vy1, vy2)
    vz1, vz2 = exchange(sizes, "gz", vz1, vz2)
    return call(
        functools.partial(stress_kernel, counts),
        [velocity.shape, stress.shape, stress.shape],
        [VM] * 19,
        scratch(3) + [pltpu.VMEM(stress.shape, F32), pltpu.VMEM(stress.shape, F32), DMA((2, nz))],
        name="stress",
        out_specs=[HB] * 3,
    )(
        vel, stress_vm, memory, material, lame_lambda[None], shear_modulus[None], relax_time[None],
        anelastic_weight[None], factor, mz, slope, vx1, vx2, vlow, vhigh, vy1, vy2, vz1, vz2,
    )


def solution(mesh):
    sizes = {a: mesh.shape[a] for a in ("gx", "gy", "gz")}
    field = P(None, "gz", "gy", "gx")
    return jax.shard_map(
        functools.partial(local, sizes),
        mesh=mesh,
        in_specs=(
            P("gy", ("gx", "gz")), P("gz"), P("gz"), P("gz", "gy", "gx"),
            P(), P(), P(), P(), P(), field, field, field,
        ),
        out_specs=(field, field, field),
        check_vma=False,
    )
```

```python
import functools
import jax
import jax.numpy as jnp
import numpy as np
from jax import lax
from jax.experimental import pallas as pl
from jax.experimental.pallas import tpu as pltpu
from jax.sharding import PartitionSpec as P

step_size = 0.3
SUB = 8
PAD = 8
F32 = jnp.float32
params = functools.partial(pltpu.CompilerParams, vmem_limit_bytes=20 * 1024 * 1024)
VM = pl.BlockSpec(memory_space=pltpu.VMEM)
SM = pl.BlockSpec(memory_space=pltpu.SMEM)
HB = pl.BlockSpec(memory_space=pltpu.HBM)
DMA = pltpu.SemaphoreType.DMA


def pair_swaps(sizes, axis):
    names = tuple(sizes)
    shape = tuple(sizes.values())
    index = names.index(axis)
    n = shape[index]
    others = [d for d in (2, 1, 0) if d != index and shape[d] % 2 == 0]
    rounds = []
    for first in (0, 1)[: max(0, min(2, n - 1))]:
        table = []
        for spot in np.ndindex(*shape):
            mate = spot[index] + 1 if spot[index] % 2 == first else spot[index] - 1
            target = list(spot)
            if 0 <= mate < n:
                target[index] = mate
            elif others:
                target[others[0]] ^= 1
            else:
                continue
            table.append((int(np.ravel_multi_index(spot, shape)), int(np.ravel_multi_index(tuple(target), shape))))
        rounds.append(table)
    return rounds


def exchange(sizes, axis, first, second):
    rounds = pair_swaps(sizes, axis)
    got = [lax.ppermute(v, tuple(sizes), r) for v, r in zip((first, second), rounds)]
    return (got[0], got[-1]) if got else (first, second)


def even(axis):
    return lax.axis_index(axis) % 2 == 0


def from_before(axis, got):
    value = jnp.where(even(axis), got[1], got[0])
    return jnp.where(lax.axis_index(axis) > 0, value, 0.0)


def from_after(axis, n, got):
    value = jnp.where(even(axis), got[0], got[1])
    return jnp.where(lax.axis_index(axis) < n - 1, value, 0.0)


def order(axis, to_after, to_before):
    e = even(axis)
    return jnp.where(e, to_after, to_before), jnp.where(e, to_before, to_after)


def lanes_of(shape):
    return lax.broadcasted_iota(jnp.int32, shape, len(shape) - 1)


def terrain_piece_kernel(elev_hbm, base_hbm, stretch_hbm, out_ref, elev_ref, base_ref, stretch_ref, sems):
    mine = lax.axis_index("gz")
    pairs = ((elev_hbm, elev_ref), (base_hbm, base_ref), (stretch_hbm, stretch_ref))
    copies = [pltpu.make_async_copy(a, b, sems.at[i]) for i, (a, b) in enumerate(pairs)]
    for copy in copies:
        copy.start()
    for copy in copies:
        copy.wait()
    ny, width = elev_ref.shape
    nx = out_ref.shape[1]
    nz = base_ref.shape[1]
    height = elev_ref[...].astype(F32) / 200.0
    wide = jnp.concatenate([height, jnp.zeros((ny, nx - width), F32)], axis=1)
    out_ref[:ny, :] = pltpu.roll(wide, mine * width, 1)
    row = lax.broadcasted_iota(jnp.int32, (SUB, nx), 0)
    fill = jnp.zeros((1, nx - nz), F32)
    base = jnp.concatenate([base_ref[...], fill], axis=1)
    stretch = jnp.concatenate([stretch_ref[...], fill], axis=1)
    both = jnp.where(row == 0, base, jnp.where(row == 1, stretch, 0.0))
    out_ref[ny:, :] = pltpu.roll(both, mine * nz, 1)


def pack_sides(field, nz, ny, nx, low_ref, high_ref, out1_ref, out2_ref):
    tiles = ny // SUB
    lane2 = lanes_of((SUB, nx)) // 2
    for c in range(3):
        lo = jnp.zeros((SUB, nx), F32)
        hi = jnp.zeros((SUB, nx), F32)
        for k in range(nz):
            for t in range(tiles):
                m = k * tiles + t
                turned = pltpu.roll(field(c, k, t), (2 * m + 2) % nx, 1)
                hi = jnp.where(lane2 == m, turned, hi)
                lo = jnp.where(lane2 == (m + 1) % (nx // 2), turned, lo)
        at = slice(SUB * c, SUB * c + SUB)
        low_ref[at, :] = lo
        high_ref[at, :] = hi
        out1_ref[at, :], out2_ref[at, :] = order("gx", hi, lo)


def pack_rows(field, nz, ny, y_refs):
    for c in range(3):
        for k in range(nz):
            j = 2 * (c * nz + k)
            both = order("gy", field(c, k, slice(ny - 2, ny)), field(c, k, slice(0, 2)))
            for ref, rows in zip(y_refs, both):
                ref[j : j + 2, :] = rows


def pack_kernel(
    stress_hbm, stress_ref, low_ref, high_ref, out1_ref, out2_ref, z1_ref, z2_ref, *rest
):
    *y_refs, sems = rest
    comps, nz, ny, nx = stress_ref.shape
    copies = [
        pltpu.make_async_copy(stress_hbm.at[c], stress_ref.at[c], sems.at[c]) for c in range(comps)
    ]
    z_even = even("gz")
    z1_at = jnp.where(z_even, nz - 2, 0)
    z2_at = jnp.where(z_even, 0, nz - 2)
    z_copies = [
        pltpu.make_async_copy(stress_hbm.at[:, pl.ds(z1_at, 2)], z1_ref, sems.at[comps]),
        pltpu.make_async_copy(stress_hbm.at[:, pl.ds(z2_at, 2)], z2_ref, sems.at[comps + 1]),
    ]
    of_x = (0, 3, 4)
    of_y = (3, 1, 5)
    loading = (0, 3, 4, 1, 5, 2)
    for c in loading[:5]:
        copies[c].start()
    for copy in z_copies:
        copy.start()
    copies[2].start()
    for c in of_x:
        copies[c].wait()
    pack_sides(
        lambda c, k, t: stress_ref[of_x[c], k, SUB * t : SUB * t + SUB, :],
        nz, ny, nx, low_ref, high_ref, out1_ref, out2_ref,
    )
    copies[1].wait()
    copies[5].wait()
    pack_rows(lambda c, k, rows: stress_ref[of_y[c], k, rows, :], nz, ny, y_refs)
    copies[2].wait()
    for copy in z_copies:
        copy.wait()


def y_send_kernel(rounds, slab_ref, *refs):
    ny = slab_ref.shape[0] - SUB
    faces = refs[0].shape[0]
    rows = order("gy", slab_ref[ny - 4 : ny, :], slab_ref[0:4, :])
    for i in range(rounds):
        refs[rounds + i][:faces, :] = refs[i][...]
        refs[rounds + i][faces : faces + 4, :] = rows[i]
        refs[rounds + i][faces + 4 :, :] = jnp.zeros_like(rows[i])


def x_send_kernel(n_gy, slab_ref, y1_ref, y2_ref, x1_ref, x2_ref, tall_ref, out1_ref, out2_ref):
    ny = slab_ref.shape[0] - SUB
    nx = slab_ref.shape[1]
    xs = x1_ref.shape[0]
    lane4 = lanes_of((SUB, nx)) // 4
    got = (y1_ref[0:4, :], y2_ref[0:4, :])
    tall_ref[: PAD - 4, :] = jnp.zeros((PAD - 4, nx), F32)
    tall_ref[PAD - 4 : PAD, :] = from_before("gy", got)
    tall_ref[PAD : PAD + ny, :] = slab_ref[:ny, :]
    tall_ref[PAD + ny : PAD + ny + 4, :] = from_after("gy", n_gy, got)
    tall_ref[PAD + ny + 4 :, :] = jnp.zeros((PAD - 4, nx), F32)
    lo = jnp.zeros((SUB, nx), F32)
    hi = jnp.zeros((SUB, nx), F32)
    for j in range((ny + 2 * PAD) // SUB):
        tile = tall_ref[SUB * j : SUB * j + SUB, :]
        lo = jnp.where(lane4 == j, pltpu.roll(tile, 4 * j, 1), lo)
        hi = jnp.where(lane4 == j, pltpu.roll(tile, (4 * j + 4) % nx, 1), hi)
    out1_ref[:xs, :] = x1_ref[...]
    out2_ref[:xs, :] = x2_ref[...]
    out1_ref[xs:, :], out2_ref[xs:, :] = order("gx", hi, lo)


def binomial(at):
    return (at(-2) + at(2) + 4.0 * (at(-1) + at(1)) + 6.0 * at(0)) / 16.0


def centred12(at):
    return 8.0 * (at(1) - at(-1)) - (at(2) - at(-2))


def metric_kernel(
    sizes, layers_ref, own, x1_ref, x2_ref, factor_ref, mz_ref, slope_ref, rim, sown,
):
    n_gx = sizes[0]
    gz = lax.axis_index("gz")
    nz, ny, nx = factor_ref.shape
    lane = lanes_of((SUB, nx))
    got = (x1_ref[...], x2_ref[...])
    left, right = from_before("gx", got), from_after("gx", n_gx, got)
    for j in range((ny + 2 * PAD) // SUB):
        rim[SUB * j : SUB * j + SUB, :] = jnp.where(
            lane < nx // 2,
            pltpu.roll(right, (nx - 4 * j) % nx, 1),
            pltpu.roll(left, nx - 4 - 4 * j, 1),
        )
    rows = ny + 4
    tall_own = binomial(lambda s: own[PAD - 2 + s : PAD - 2 + s + rows, :])
    tall_rim = binomial(lambda s: rim[PAD - 2 + s : PAD - 2 + s + rows, :])

    def shifted(a, b, s):
        ln = lanes_of(a.shape)
        cut = (ln < s) if s > 0 else (ln >= nx + s)
        if s > 0:
            mixed_a, mixed_b = jnp.where(cut, b, a), jnp.where(cut, a, b)
        elif s < 0:
            mixed_a, mixed_b = jnp.where(cut, b, a), jnp.where(cut, a, b)
        else:
            return a, b
        return pltpu.roll(mixed_a, (-s) % nx, 1), pltpu.roll(mixed_b, (-s) % nx, 1)

    def padded_rows(a):
        return jnp.concatenate([a, jnp.zeros((SUB - rows % SUB, nx), F32)], axis=0)

    tall_own, tall_rim = padded_rows(tall_own), padded_rows(tall_rim)
    pairs = {s: shifted(tall_own, tall_rim, s) for s in (-2, -1, 0, 1, 2)}
    surf_own = binomial(lambda s: pairs[s][0])
    surf_rim = binomial(lambda s: pairs[s][1])
    sown[...] = surf_own
    slope_ref[1] = centred12(lambda s: sown[2 + s : 2 + s + ny, :]) / 12.0
    pairs2 = {s: shifted(surf_own, surf_rim, s)[0] for s in (-2, -1, 1, 2)}
    along = centred12(lambda s: pairs2[s]) / 12.0
    surface = sown[2 : 2 + ny, :]
    sown[...] = along
    slope_ref[0] = sown[2 : 2 + ny, :]

    def above(slab, total):
        for k in range(nz):
            s = layers_ref[1, slab * nz + k]
            total = total + (s * layers_ref[0, slab * nz + k]) * jnp.exp(s * surface)
        return total

    total = lax.fori_loop(0, gz, above, jnp.zeros((ny, nx), F32))
    for k in range(nz):
        s = layers_ref[1, gz * nz + k]
        thickness = layers_ref[0, gz * nz + k] * jnp.exp(s * surface)
        weighted = s * thickness
        mz = 1.0 / thickness
        lift = total + 0.5 * weighted
        total = total + weighted
        mz_ref[k] = mz
        factor_ref[k] = (lift - 1.0) * mz

def edge_terms(got_left, got_right, low, high):
    dl = got_left - high
    dr = got_right - low
    nx = dl.shape[-1]
    lane = lanes_of(dl.shape)
    even = lane % 2 == 0
    dl = pltpu.roll(dl, 2, 1)
    dr = pltpu.roll(dr, nx - 2, 1)
    to_low = jnp.where(even, dl - 8.0 * pltpu.roll(dl, nx - 1, 1), dl)
    to_high = jnp.where(even, -dr, 8.0 * pltpu.roll(dr, 1, 1) - dr)
    second = (lane // 2) % 2 == 1
    return jnp.where(second, to_low, to_high), jnp.where(second, to_high, to_low)


def turned_left(edges, m):
    nx = edges.shape[-1]
    shift = (2 * nx - 2 - 2 * m) % nx if isinstance(m, int) else 2 * nx - 2 - 2 * m
    return pltpu.roll(edges, shift, 1)


def sides(lane):
    return (lane < 2) | (lane >= lane.shape[-1] - 2)


def periodic_x(tile):
    nx = tile.shape[-1]
    return 8.0 * (pltpu.roll(tile, nx - 1, 1) - pltpu.roll(tile, 1, 1)) - (
        pltpu.roll(tile, nx - 2, 1) - pltpu.roll(tile, 2, 1)
    )


def lookup(row, tile):
    table = jnp.broadcast_to(row, tile.shape)
    return jnp.take_along_axis(table, tile, axis=1, mode="promise_in_bounds")


def table_rows(refs, nx):
    n = refs[0].shape[1]
    return [jnp.concatenate([r, jnp.zeros((1, nx - n), F32)], axis=1) for r in refs]


def fill_edges(n_gx, edge_ref, x1_ref, x2_ref, low_ref, high_ref):
    for c in range(3):
        at = slice(SUB * c, SUB * c + SUB)
        got = (x1_ref[at, :], x2_ref[at, :])
        first, second = edge_terms(
            from_before("gx", got), from_after("gx", n_gx, got), low_ref[at, :], high_ref[at, :]
        )
        edge_ref[c, 0] = first
        edge_ref[c, 1] = second


def fill_rows(n_gy, tall, field, y1_ref, y2_ref, nz, ny, layers):
    for c in range(3):
        for spot, k in enumerate(layers):
            j = 2 * (c * nz + k)
            got = (y1_ref[j : j + 2, :], y2_ref[j : j + 2, :])
            tall[c, spot, PAD : PAD + ny, :] = field(c, k)
            tall[c, spot, PAD - 2 : PAD, :] = from_before("gy", got)
            tall[c, spot, PAD + ny : PAD + ny + 2, :] = from_after("gy", n_gy, got)


def depth_halos(n_gz, zb, za, z1_ref, z2_ref):
    got = (z1_ref[...], z2_ref[...])
    zb[...] = from_before("gz", got)
    za[...] = from_after("gz", n_gz, got)


def tile_rows(t):
    return slice(SUB * t, SUB * t + SUB)


def row_difference(tall, c, spot, t):
    return centred12(lambda s: tall[c, spot, PAD + SUB * t + s : PAD + SUB * t + s + SUB, :])


def inner_depth(ref, out_ref, comps, k, tiles):
    for t in range(tiles):
        for c in range(comps):
            out_ref[c, k - 2, tile_rows(t), :] = centred12(lambda s: ref[c, k + s, tile_rows(t), :])


def outer_depth(ref, zb, za, out_ref, comps, nz, tiles):
    for spot, k in enumerate((0, 1, nz - 2, nz - 1)):
        for t in range(tiles):
            for c in range(comps):

                def at(s):
                    if k + s < 0:
                        return zb[c, k + s + 2, tile_rows(t), :]
                    if k + s >= nz:
                        return za[c, k + s - nz, tile_rows(t), :]
                    return ref[c, k + s, tile_rows(t), :]

                out_ref[c, spot, tile_rows(t), :] = centred12(at)


def cell_kernel(*refs):
    given, cells_ref, held, sems = refs[:6], refs[6], refs[7:13], refs[13]
    copies = [
        pltpu.make_async_copy(a, b, sems.at[i]) for i, (a, b) in enumerate(zip(given, held))
    ]
    for copy in copies:
        copy.start()
    for copy in copies:
        copy.wait()
    material_ref, buoy_ref, lam_ref, mu_ref, relax_ref, weight_ref = held
    nz, ny, nx = material_ref.shape
    keep = jnp.exp(-step_size / relax_ref[...])
    tables = table_rows(
        [
            buoy_ref[...] * (step_size / 12.0), lam_ref[...] / 12.0, mu_ref[...] / 12.0, keep,
            (1.0 - keep) * weight_ref[...],
        ],
        nx,
    )

    @pl.loop(0, nz)
    def _(k):
        for t in range(ny // SUB):
            kind = material_ref[k, tile_rows(t), :]
            for i, table in enumerate(tables):
                cells_ref[i, k, tile_rows(t), :] = lookup(table, kind)


def depth_kernel(stress_ref, velocity_hbm, depth_ref, along_ref, velocity_ref, sem):
    load = pltpu.make_async_copy(velocity_hbm, velocity_ref, sem)
    load.start()
    _, nz, ny, _ = stress_ref.shape
    tiles = ny // SUB

    def along(k):
        for t in range(tiles):
            for c, comp in enumerate((0, 3, 4)):
                along_ref[c, k, tile_rows(t), :] = periodic_x(stress_ref[comp, k, tile_rows(t), :])

    for k in (0, 1, nz - 2, nz - 1):
        along(k)

    @pl.loop(2, nz - 2)
    def _(k):
        along(k)
        inner_depth(stress_ref, depth_ref, 6, k, tiles)

    load.wait()


def plane_kernel(sizes, stress_ref, along_ref, y1_ref, y2_ref, plane_ref, tall):
    _, nz, ny, nx = stress_ref.shape
    tiles = ny // SUB
    of_y = (3, 1, 5)
    fill_rows(sizes[1], tall, lambda c, k: stress_ref[of_y[c], k], y1_ref, y2_ref, nz, ny, range(nz))

    @pl.loop(0, nz)
    def _(k):
        for t in range(tiles):
            for c in range(3):
                plane_ref[c, k, tile_rows(t), :] = along_ref[
                    c, k, tile_rows(t), :
                ] + row_difference(tall, c, k, t)


def velocity_kernel(
    sizes, velocity_ref, stress_ref, cells_ref, inner_ref, plane_ref, factor_ref, mz_ref, slope_ref,
    x1_ref, x2_ref, z1_ref, z2_ref, low_ref, high_ref, out_ref, vlow_ref, vhigh_ref, vx1_ref, vx2_ref, vz1_ref, vz2_ref,
    *rest,
):
    *vy_refs, edge, zb, za, outer_ref = rest
    _, nz, ny, nx = velocity_ref.shape
    tiles = ny // SUB
    lane = lanes_of((SUB, nx))
    fill_edges(sizes[0], edge, x1_ref, x2_ref, low_ref, high_ref)
    depth_halos(sizes[2], zb, za, z1_ref, z2_ref)
    outer_depth(stress_ref, zb, za, outer_ref, 6, nz, tiles)

    def layer(k, depth_ref, spot):
        for t in range(tiles):
            rows = tile_rows(t)
            b = cells_ref[0, k, rows, :]
            factor = factor_ref[k, rows, :]
            mz = mz_ref[k, rows, :]
            mx = slope_ref[0, rows, :] * factor
            my = slope_ref[1, rows, :] * factor
            gk = [depth_ref[c, spot, rows, :] for c in range(6)]
            beside = [
                plane_ref[c, k, rows, :]
                + jnp.where(sides(lane), turned_left(edge[c, t % 2], k * tiles + t), 0.0)
                for c in range(3)
            ]
            accel = (
                beside[0] - mx * gk[0] - my * gk[3] + mz * gk[4],
                beside[1] - mx * gk[3] - my * gk[1] + mz * gk[5],
                beside[2] - mx * gk[4] - my * gk[5] + mz * gk[2],
            )
            for c in range(3):
                out_ref[c, k, rows, :] = velocity_ref[c, k, rows, :] + b * accel[c]

    for spot, k in enumerate((0, 1, nz - 2, nz - 1)):
        layer(k, outer_ref, spot)

    @pl.loop(2, nz - 2)
    def _(k):
        layer(k, inner_ref, k - 2)

    pack_sides(
        lambda c, k, t: out_ref[c, k, tile_rows(t), :], nz, ny, nx, vlow_ref, vhigh_ref, vx1_ref, vx2_ref
    )
    pack_rows(lambda c, k, rows: out_ref[c, k, rows, :], nz, ny, vy_refs)
    vz1_ref[...], vz2_ref[...] = order("gz", out_ref[:, nz - 2 : nz], out_ref[:, 0:2])


def velocity_inner_kernel(vel_ref, vel_hbm, depth_ref, along_ref, sem):
    store = pltpu.make_async_copy(vel_ref, vel_hbm, sem)
    store.start()
    _, nz, ny, nx = vel_ref.shape
    tiles = ny // SUB

    def along(k):
        for t in range(tiles):
            for c in range(3):
                along_ref[c, k, tile_rows(t), :] = periodic_x(vel_ref[c, k, tile_rows(t), :])

    for k in (0, 1, nz - 2, nz - 1):
        along(k)

    @pl.loop(2, nz - 2)
    def _(k):
        along(k)
        inner_depth(vel_ref, depth_ref, 3, k, tiles)

    store.wait()


def stress_kernel(
    sizes, vel_ref, stress_ref, memory_ref, cells_ref, inner_ref, along_ref, factor_ref, mz_ref, slope_ref,
    x1_ref, x2_ref, low_ref, high_ref, y1_ref, y2_ref, z1_ref, z2_ref,
    stress_hbm, memory_hbm, edge, tall, zb, za, outer, stress_out, memory_out, sems,
):
    n_gx, n_gy, n_gz = sizes
    _, nz, ny, nx = vel_ref.shape
    tiles = ny // SUB
    lane = lanes_of((SUB, nx))
    fill_edges(n_gx, edge, x1_ref, x2_ref, low_ref, high_ref)
    fill_rows(n_gy, tall, lambda c, k: vel_ref[c, k], y1_ref, y2_ref, nz, ny, range(nz))

    def layer(k, depth_ref, spot):
        for t in range(tiles):
            rows = tile_rows(t)
            factor = factor_ref[k, rows, :]
            mz = mz_ref[k, rows, :]
            mx = slope_ref[0, rows, :] * factor
            my = slope_ref[1, rows, :] * factor
            dk = [depth_ref[c, spot, rows, :] for c in range(3)]
            dx = [
                along_ref[c, k, rows, :]
                + jnp.where(sides(lane), turned_left(edge[c, t % 2], k * tiles + t), 0.0)
                - mx * dk[c]
                for c in range(3)
            ]
            dy = [row_difference(tall, c, k, t) - my * dk[c] for c in range(3)]
            dz = [mz * dk[c] for c in range(3)]
            lam, mu, keep, gain = (cells_ref[i, k, rows, :] for i in range(1, 5))
            volume = lam * (dx[0] + dy[1] + dz[2])
            mu2 = mu + mu
            rates = (
                volume + mu2 * dx[0],
                volume + mu2 * dy[1],
                volume + mu2 * dz[2],
                mu * (dy[0] + dx[1]),
                mu * (dz[0] + dx[2]),
                mu * (dz[1] + dy[2]),
            )
            for c in range(6):
                kept = keep * memory_ref[c, k, rows, :] + gain * rates[c]
                memory_out[c, k, rows, :] = kept
                stress_out[c, k, rows, :] = stress_ref[c, k, rows, :] + step_size * (
                    rates[c] - kept
                )

    def out_copies(first, count, spot):
        layers = pl.ds(first, count)
        return [
            pltpu.make_async_copy(a.at[:, layers], b.at[:, layers], sems.at[i, spot])
            for i, (a, b) in enumerate(((stress_out, stress_hbm), (memory_out, memory_hbm)))
        ]

    inner = nz - 4
    step = next(d for d in (4, 3, 2, 1) if inner % d == 0)
    chunks = inner // step

    @pl.loop(0, chunks)
    def _(j):
        @pl.loop(0, step)
        def _(i):
            k = 2 + j * step + i
            layer(k, inner_ref, k - 2)

        for copy in out_copies(2 + j * step, step, 2 + j):
            copy.start()

    depth_halos(n_gz, zb, za, z1_ref, z2_ref)
    outer_depth(vel_ref, zb, za, outer, 3, nz, tiles)
    last = []
    for spot, k in enumerate((0, 1, nz - 2, nz - 1)):
        layer(k, outer, spot)
        if spot % 2 == 1:
            last += out_copies(k - 1, 2, spot // 2)
            for copy in last[-2:]:
                copy.start()

    @pl.loop(0, chunks)
    def _(j):
        for copy in out_copies(2 + j * step, step, 2 + j):
            copy.wait()

    for copy in last:
        copy.wait()


def in_hbm(value):
    return pltpu.with_memory_space_constraint(value, pltpu.HBM)


def call(kernel, outs, in_specs, scratch=(), name=None, out_specs=None, aliases=None):
    return pl.pallas_call(
        kernel,
        out_shape=[jax.ShapeDtypeStruct(s, F32) for s in outs],
        in_specs=in_specs,
        out_specs=out_specs or [VM] * len(outs),
        scratch_shapes=list(scratch),
        compiler_params=params(),
        input_output_aliases=aliases or {},
        name=name,
    )


def local(
    sizes, elevation, layer_base, stretch, material, buoyancy, lame_lambda, shear_modulus,
    relax_time, anelastic_weight, velocity, stress, memory,
):
    n_gx, n_gy, n_gz = counts = tuple(sizes[a] for a in ("gx", "gy", "gz"))
    _, nz, ny, nx = velocity.shape
    rows = ny + SUB
    slab = call(
        terrain_piece_kernel,
        [(rows, nx)],
        [HB] * 3,
        [
            pltpu.VMEM(elevation.shape, jnp.int32),
            pltpu.VMEM((1, nz), F32),
            pltpu.VMEM((1, nz), F32),
            DMA((3,)),
        ],
        name="terrain_piece",
    )(in_hbm(elevation), in_hbm(layer_base[None]), in_hbm(stretch[None]))[0]
    tied = lax.optimization_barrier
    faces = 2 * 3 * nz
    xs = 3 * SUB
    y_rounds = min(2, n_gy - 1) if n_gy > 1 else 1
    z_face = (6, 2, ny, nx)
    slab, material = tied((slab, material))
    tables = (buoyancy, lame_lambda, shear_modulus, relax_time, anelastic_weight)
    cells = call(
        cell_kernel,
        [(5, nz, ny, nx)],
        [HB] * 6,
        [pltpu.VMEM(material.shape, jnp.int32)]
        + [pltpu.VMEM((1, table.shape[0]), F32) for table in tables]
        + [DMA((6,))],
        name="cells",
    )(in_hbm(material), *[in_hbm(table[None]) for table in tables])[0]
    if n_gz & (n_gz - 1):
        slab = lax.psum(slab, "gz")
        slab, stress = tied((slab, stress))
    else:
        bit = 1
        while bit < n_gz:
            slab = slab + lax.ppermute(slab, "gz", [(i, i ^ bit) for i in range(n_gz)])
            if bit == 1:
                slab, stress, cells = tied((slab, stress, cells))
            bit *= 2
    stress_vm, low, high, x1, x2, z1, z2, *ys = call(
        pack_kernel,
        [stress.shape] + [(xs, nx)] * 4 + [z_face] * 2 + [(faces, nx)] * y_rounds,
        [HB],
        [DMA((8,))],
        name="pack_stress",
    )(in_hbm(stress))
    ys = call(
        functools.partial(y_send_kernel, y_rounds),
        [(faces + SUB, nx)] * y_rounds,
        [VM] * (1 + y_rounds),
        name="y_send",
    )(slab, *ys)
    ys, velocity = tied((ys, velocity))
    y1, y2 = exchange(sizes, "gy", ys[0], ys[-1])
    inner_k, along, velocity_vm = call(
        depth_kernel,
        [(6, nz - 4, ny, nx), velocity.shape, velocity.shape],
        [VM, HB],
        [DMA],
        name="depth",
    )(stress_vm, in_hbm(velocity))
    x1, x2, inner_k = tied((x1, x2, inner_k))
    terrain, x1, x2 = call(
        functools.partial(x_send_kernel, n_gy),
        [(ny + 2 * PAD, nx)] + [(xs + SUB, nx)] * 2,
        [VM] * 5,
        name="x_send",
    )(slab, y1[faces:], y2[faces:], x1, x2)
    x1, x2, z1, z2 = tied((x1, x2, z1, z2))
    x1, x2 = exchange(sizes, "gx", x1, x2)
    z1, z2 = exchange(sizes, "gz", z1, z2)
    edge = pltpu.VMEM((3, 2, SUB, nx), F32)
    tall = pltpu.VMEM((3, nz, ny + 2 * PAD, nx), F32)

    def depth(comps):
        return [pltpu.VMEM((comps, 2, ny, nx), F32)] * 2

    plane = call(
        functools.partial(plane_kernel, counts), [velocity.shape], [VM] * 4, [tall], name="planes"
    )(stress_vm, along, y1, y2)[0]
    plane, x1, x2 = tied((plane, x1, x2))
    factor, mz, slope = call(
        functools.partial(metric_kernel, counts),
        [(nz, ny, nx), (nz, ny, nx), (2, ny, nx)],
        [SM] + [VM] * 3,
        [pltpu.VMEM((ny + 2 * PAD, nx), F32), pltpu.VMEM((ny + PAD, nx), F32)],
        name="metrics",
    )(slab[ny:], terrain, x1[xs:], x2[xs:])
    vel, vlow, vhigh, vx1, vx2, vz1, vz2, *vys = call(
        functools.partial(velocity_kernel, counts),
        [velocity.shape] + [(xs, nx)] * 4 + [(3, 2, ny, nx)] * 2 + [(faces, nx)] * y_rounds,
        [VM] * 14,
        [edge] + depth(6) + [pltpu.VMEM((6, 4, ny, nx), F32)],
        name="velocity",
    )(velocity_vm, stress_vm, cells, inner_k, plane, factor, mz, slope, x1, x2, z1, z2, low, high)
    vz1, vz2 = exchange(sizes, "gz", vz1, vz2)
    vy1, vy2 = exchange(sizes, "gy", vys[0], vys[-1])
    vx1, vx2 = exchange(sizes, "gx", vx1, vx2)
    vel_next, vel_k, vel_x = call(
        velocity_inner_kernel,
        [velocity.shape, (3, nz - 4, ny, nx), velocity.shape],
        [VM],
        [DMA],
        name="velocity_inner",
        out_specs=[HB, VM, VM],
    )(vel)
    stress_next, memory_next = call(
        functools.partial(stress_kernel, counts),
        [stress.shape, stress.shape],
        [VM] * 17,
        [edge, tall] + depth(3)
        + [pltpu.VMEM((3, 4, ny, nx), F32), pltpu.VMEM(stress.shape, F32), pltpu.VMEM(stress.shape, F32)]
        + [DMA((2, nz))],
        name="stress",
        out_specs=[HB] * 2,
    )(
        vel, stress_vm, memory, cells, vel_k, vel_x, factor, mz, slope, vx1, vx2, vlow, vhigh, vy1, vy2,
        vz1, vz2,
    )
    return vel_next, stress_next, memory_next


def solution(mesh):
    sizes = {a: mesh.shape[a] for a in ("gx", "gy", "gz")}
    field = P(None, "gz", "gy", "gx")
    return jax.shard_map(
        functools.partial(local, sizes),
        mesh=mesh,
        in_specs=(
            P("gy", ("gx", "gz")), P("gz"), P("gz"), P("gz", "gy", "gx"),
            P(), P(), P(), P(), P(), field, field, field,
        ),
        out_specs=(field, field, field),
        check_vma=False,
    )
```

```python
import functools
import jax
import jax.numpy as jnp
import numpy as np
from jax import lax
from jax.experimental import pallas as pl
from jax.experimental.pallas import tpu as pltpu
from jax.sharding import PartitionSpec as P

step_size = 0.3
SUB = 8
PAD = 8
F32 = jnp.float32
params = functools.partial(pltpu.CompilerParams, vmem_limit_bytes=20 * 1024 * 1024)
VM = pl.BlockSpec(memory_space=pltpu.VMEM)
SM = pl.BlockSpec(memory_space=pltpu.SMEM)
HB = pl.BlockSpec(memory_space=pltpu.HBM)
DMA = pltpu.SemaphoreType.DMA


def pair_swaps(sizes, axis):
    names = tuple(sizes)
    shape = tuple(sizes.values())
    index = names.index(axis)
    n = shape[index]
    others = [d for d in (2, 1, 0) if d != index and shape[d] % 2 == 0]
    rounds = []
    for first in (0, 1)[: max(0, min(2, n - 1))]:
        table = []
        for spot in np.ndindex(*shape):
            mate = spot[index] + 1 if spot[index] % 2 == first else spot[index] - 1
            target = list(spot)
            if 0 <= mate < n:
                target[index] = mate
            elif others:
                target[others[0]] ^= 1
            else:
                continue
            table.append((int(np.ravel_multi_index(spot, shape)), int(np.ravel_multi_index(tuple(target), shape))))
        rounds.append(table)
    return rounds


def exchange(sizes, axis, first, second):
    rounds = pair_swaps(sizes, axis)
    got = [lax.ppermute(v, tuple(sizes), r) for v, r in zip((first, second), rounds)]
    return (got[0], got[-1]) if got else (first, second)


def even(axis):
    return lax.axis_index(axis) % 2 == 0


def from_before(axis, got):
    value = jnp.where(even(axis), got[1], got[0])
    return jnp.where(lax.axis_index(axis) > 0, value, 0.0)


def from_after(axis, n, got):
    value = jnp.where(even(axis), got[0], got[1])
    return jnp.where(lax.axis_index(axis) < n - 1, value, 0.0)


def order(axis, to_after, to_before):
    e = even(axis)
    return jnp.where(e, to_after, to_before), jnp.where(e, to_before, to_after)


def lanes_of(shape):
    return lax.broadcasted_iota(jnp.int32, shape, len(shape) - 1)


def terrain_piece_kernel(elev_hbm, base_hbm, stretch_hbm, out_ref, elev_ref, base_ref, stretch_ref, sems):
    mine = lax.axis_index("gz")
    pairs = ((elev_hbm, elev_ref), (base_hbm, base_ref), (stretch_hbm, stretch_ref))
    copies = [pltpu.make_async_copy(a, b, sems.at[i]) for i, (a, b) in enumerate(pairs)]
    for copy in copies:
        copy.start()
    for copy in copies:
        copy.wait()
    ny, width = elev_ref.shape
    nx = out_ref.shape[1]
    nz = base_ref.shape[1]
    height = elev_ref[...].astype(F32) / 200.0
    wide = jnp.concatenate([height, jnp.zeros((ny, nx - width), F32)], axis=1)
    out_ref[:ny, :] = pltpu.roll(wide, mine * width, 1)
    row = lax.broadcasted_iota(jnp.int32, (SUB, nx), 0)
    fill = jnp.zeros((1, nx - nz), F32)
    base = jnp.concatenate([base_ref[...], fill], axis=1)
    stretch = jnp.concatenate([stretch_ref[...], fill], axis=1)
    both = jnp.where(row == 0, base, jnp.where(row == 1, stretch, 0.0))
    out_ref[ny:, :] = pltpu.roll(both, mine * nz, 1)


def pack_sides(field, nz, ny, nx, low_ref, high_ref, out1_ref, out2_ref):
    tiles = ny // SUB
    lane2 = lanes_of((SUB, nx)) // 2
    for c in range(3):
        lo = jnp.zeros((SUB, nx), F32)
        hi = jnp.zeros((SUB, nx), F32)
        for k in range(nz):
            for t in range(tiles):
                m = k * tiles + t
                turned = pltpu.roll(field(c, k, t), (2 * m + 2) % nx, 1)
                hi = jnp.where(lane2 == m, turned, hi)
                lo = jnp.where(lane2 == (m + 1) % (nx // 2), turned, lo)
        at = slice(SUB * c, SUB * c + SUB)
        low_ref[at, :] = lo
        high_ref[at, :] = hi
        out1_ref[at, :], out2_ref[at, :] = order("gx", hi, lo)


def pack_rows(field, nz, ny, y_refs):
    for c in range(3):
        for k in range(nz):
            j = 2 * (c * nz + k)
            both = order("gy", field(c, k, slice(ny - 2, ny)), field(c, k, slice(0, 2)))
            for ref, rows in zip(y_refs, both):
                ref[j : j + 2, :] = rows


def pack_kernel(
    stress_hbm, stress_ref, low_ref, high_ref, out1_ref, out2_ref, z1_ref, z2_ref, *rest
):
    *y_refs, sems = rest
    comps, nz, ny, nx = stress_ref.shape
    copies = [
        pltpu.make_async_copy(stress_hbm.at[c], stress_ref.at[c], sems.at[c]) for c in range(comps)
    ]
    z_even = even("gz")
    z1_at = jnp.where(z_even, nz - 2, 0)
    z2_at = jnp.where(z_even, 0, nz - 2)
    z_copies = [
        pltpu.make_async_copy(stress_hbm.at[:, pl.ds(z1_at, 2)], z1_ref, sems.at[comps]),
        pltpu.make_async_copy(stress_hbm.at[:, pl.ds(z2_at, 2)], z2_ref, sems.at[comps + 1]),
    ]
    of_x = (0, 3, 4)
    of_y = (3, 1, 5)
    loading = (0, 3, 4, 1, 5, 2)
    for c in loading[:5]:
        copies[c].start()
    for copy in z_copies:
        copy.start()
    copies[2].start()
    for c in of_x:
        copies[c].wait()
    pack_sides(
        lambda c, k, t: stress_ref[of_x[c], k, SUB * t : SUB * t + SUB, :],
        nz, ny, nx, low_ref, high_ref, out1_ref, out2_ref,
    )
    copies[1].wait()
    copies[5].wait()
    pack_rows(lambda c, k, rows: stress_ref[of_y[c], k, rows, :], nz, ny, y_refs)
    copies[2].wait()
    for copy in z_copies:
        copy.wait()


def y_send_kernel(rounds, slab_ref, *refs):
    ny = slab_ref.shape[0] - SUB
    faces = refs[0].shape[0]
    rows = order("gy", slab_ref[ny - 4 : ny, :], slab_ref[0:4, :])
    for i in range(rounds):
        refs[rounds + i][:faces, :] = refs[i][...]
        refs[rounds + i][faces : faces + 4, :] = rows[i]
        refs[rounds + i][faces + 4 :, :] = jnp.zeros_like(rows[i])


def x_send_kernel(n_gy, slab_ref, y1_ref, y2_ref, x1_ref, x2_ref, tall_ref, out1_ref, out2_ref):
    ny = slab_ref.shape[0] - SUB
    nx = slab_ref.shape[1]
    xs = x1_ref.shape[0]
    lane4 = lanes_of((SUB, nx)) // 4
    got = (y1_ref[0:4, :], y2_ref[0:4, :])
    tall_ref[: PAD - 4, :] = jnp.zeros((PAD - 4, nx), F32)
    tall_ref[PAD - 4 : PAD, :] = from_before("gy", got)
    tall_ref[PAD : PAD + ny, :] = slab_ref[:ny, :]
    tall_ref[PAD + ny : PAD + ny + 4, :] = from_after("gy", n_gy, got)
    tall_ref[PAD + ny + 4 :, :] = jnp.zeros((PAD - 4, nx), F32)
    lo = jnp.zeros((SUB, nx), F32)
    hi = jnp.zeros((SUB, nx), F32)
    for j in range((ny + 2 * PAD) // SUB):
        tile = tall_ref[SUB * j : SUB * j + SUB, :]
        lo = jnp.where(lane4 == j, pltpu.roll(tile, 4 * j, 1), lo)
        hi = jnp.where(lane4 == j, pltpu.roll(tile, (4 * j + 4) % nx, 1), hi)
    out1_ref[:xs, :] = x1_ref[...]
    out2_ref[:xs, :] = x2_ref[...]
    out1_ref[xs:, :], out2_ref[xs:, :] = order("gx", hi, lo)


def binomial(at):
    return (at(-2) + at(2) + 4.0 * (at(-1) + at(1)) + 6.0 * at(0)) / 16.0


def centred12(at):
    return 8.0 * (at(1) - at(-1)) - (at(2) - at(-2))


def metric_kernel(
    sizes, layers_ref, own, x1_ref, x2_ref, factor_ref, mz_ref, slope_ref, rim, sown,
):
    n_gx = sizes[0]
    gz = lax.axis_index("gz")
    nz, ny, nx = factor_ref.shape
    lane = lanes_of((SUB, nx))
    got = (x1_ref[...], x2_ref[...])
    left, right = from_before("gx", got), from_after("gx", n_gx, got)
    for j in range((ny + 2 * PAD) // SUB):
        rim[SUB * j : SUB * j + SUB, :] = jnp.where(
            lane < nx // 2,
            pltpu.roll(right, (nx - 4 * j) % nx, 1),
            pltpu.roll(left, nx - 4 - 4 * j, 1),
        )
    rows = ny + 4
    tall_own = binomial(lambda s: own[PAD - 2 + s : PAD - 2 + s + rows, :])
    tall_rim = binomial(lambda s: rim[PAD - 2 + s : PAD - 2 + s + rows, :])

    def shifted(a, b, s):
        ln = lanes_of(a.shape)
        cut = (ln < s) if s > 0 else (ln >= nx + s)
        if s > 0:
            mixed_a, mixed_b = jnp.where(cut, b, a), jnp.where(cut, a, b)
        elif s < 0:
            mixed_a, mixed_b = jnp.where(cut, b, a), jnp.where(cut, a, b)
        else:
            return a, b
        return pltpu.roll(mixed_a, (-s) % nx, 1), pltpu.roll(mixed_b, (-s) % nx, 1)

    def padded_rows(a):
        return jnp.concatenate([a, jnp.zeros((SUB - rows % SUB, nx), F32)], axis=0)

    tall_own, tall_rim = padded_rows(tall_own), padded_rows(tall_rim)
    pairs = {s: shifted(tall_own, tall_rim, s) for s in (-2, -1, 0, 1, 2)}
    surf_own = binomial(lambda s: pairs[s][0])
    surf_rim = binomial(lambda s: pairs[s][1])
    sown[...] = surf_own
    slope_ref[1] = centred12(lambda s: sown[2 + s : 2 + s + ny, :]) / 12.0
    pairs2 = {s: shifted(surf_own, surf_rim, s)[0] for s in (-2, -1, 1, 2)}
    along = centred12(lambda s: pairs2[s]) / 12.0
    surface = sown[2 : 2 + ny, :]
    sown[...] = along
    slope_ref[0] = sown[2 : 2 + ny, :]

    def above(slab, total):
        for k in range(nz):
            s = layers_ref[1, slab * nz + k]
            total = total + (s * layers_ref[0, slab * nz + k]) * jnp.exp(s * surface)
        return total

    total = lax.fori_loop(0, gz, above, jnp.zeros((ny, nx), F32))
    for k in range(nz):
        s = layers_ref[1, gz * nz + k]
        thickness = layers_ref[0, gz * nz + k] * jnp.exp(s * surface)
        weighted = s * thickness
        mz = 1.0 / thickness
        lift = total + 0.5 * weighted
        total = total + weighted
        mz_ref[k] = mz
        factor_ref[k] = (lift - 1.0) * mz

def edge_terms(got_left, got_right, low, high):
    dl = got_left - high
    dr = got_right - low
    nx = dl.shape[-1]
    lane = lanes_of(dl.shape)
    even = lane % 2 == 0
    dl = pltpu.roll(dl, 2, 1)
    dr = pltpu.roll(dr, nx - 2, 1)
    to_low = jnp.where(even, dl - 8.0 * pltpu.roll(dl, nx - 1, 1), dl)
    to_high = jnp.where(even, -dr, 8.0 * pltpu.roll(dr, 1, 1) - dr)
    second = (lane // 2) % 2 == 1
    return jnp.where(second, to_low, to_high), jnp.where(second, to_high, to_low)


def turned_left(edges, m):
    nx = edges.shape[-1]
    shift = (2 * nx - 2 - 2 * m) % nx if isinstance(m, int) else 2 * nx - 2 - 2 * m
    return pltpu.roll(edges, shift, 1)


def sides(lane):
    return (lane < 2) | (lane >= lane.shape[-1] - 2)


def periodic_x(tile):
    nx = tile.shape[-1]
    return 8.0 * (pltpu.roll(tile, nx - 1, 1) - pltpu.roll(tile, 1, 1)) - (
        pltpu.roll(tile, nx - 2, 1) - pltpu.roll(tile, 2, 1)
    )


def lookup(row, tile):
    table = jnp.broadcast_to(row, tile.shape)
    return jnp.take_along_axis(table, tile, axis=1, mode="promise_in_bounds")


def table_rows(refs, nx):
    n = refs[0].shape[1]
    return [jnp.concatenate([r, jnp.zeros((1, nx - n), F32)], axis=1) for r in refs]


def fill_edges(n_gx, edge_ref, x1_ref, x2_ref, low_ref, high_ref):
    for c in range(3):
        at = slice(SUB * c, SUB * c + SUB)
        got = (x1_ref[at, :], x2_ref[at, :])
        first, second = edge_terms(
            from_before("gx", got), from_after("gx", n_gx, got), low_ref[at, :], high_ref[at, :]
        )
        edge_ref[c, 0] = first
        edge_ref[c, 1] = second


def fill_rows(n_gy, tall, field, y1_ref, y2_ref, nz, ny, layers):
    for c in range(3):
        for spot, k in enumerate(layers):
            j = 2 * (c * nz + k)
            got = (y1_ref[j : j + 2, :], y2_ref[j : j + 2, :])
            tall[c, spot, PAD : PAD + ny, :] = field(c, k)
            tall[c, spot, PAD - 2 : PAD, :] = from_before("gy", got)
            tall[c, spot, PAD + ny : PAD + ny + 2, :] = from_after("gy", n_gy, got)


def depth_halos(n_gz, zb, za, z1_ref, z2_ref):
    got = (z1_ref[...], z2_ref[...])
    zb[...] = from_before("gz", got)
    za[...] = from_after("gz", n_gz, got)


def over(low, high, most, body):
    count = high - low
    group = next(d for d in range(most, 0, -1) if count % d == 0)

    @pl.loop(0, count // group)
    def _(j):
        for i in range(group):
            body(low + j * group + i)


def tile_rows(t):
    return slice(SUB * t, SUB * t + SUB)


def row_difference(tall, c, spot, t):
    return centred12(lambda s: tall[c, spot, PAD + SUB * t + s : PAD + SUB * t + s + SUB, :])


def inner_depth(ref, out_ref, comps, k, tiles):
    for t in range(tiles):
        for c in range(comps):
            out_ref[c, k - 2, tile_rows(t), :] = centred12(lambda s: ref[c, k + s, tile_rows(t), :])


def outer_depth(ref, zb, za, out_ref, comps, nz, tiles):
    for spot, k in enumerate((0, 1, nz - 2, nz - 1)):
        for t in range(tiles):
            for c in range(comps):

                def at(s):
                    if k + s < 0:
                        return zb[c, k + s + 2, tile_rows(t), :]
                    if k + s >= nz:
                        return za[c, k + s - nz, tile_rows(t), :]
                    return ref[c, k + s, tile_rows(t), :]

                out_ref[c, spot, tile_rows(t), :] = centred12(at)


def cell_kernel(*refs):
    given, cells_ref, held, sems = refs[:6], refs[6], refs[7:13], refs[13]
    copies = [
        pltpu.make_async_copy(a, b, sems.at[i]) for i, (a, b) in enumerate(zip(given, held))
    ]
    for copy in copies:
        copy.start()
    for copy in copies:
        copy.wait()
    material_ref, buoy_ref, lam_ref, mu_ref, relax_ref, weight_ref = held
    nz, ny, nx = material_ref.shape
    keep = jnp.exp(-step_size / relax_ref[...])
    tables = table_rows(
        [
            buoy_ref[...] * (step_size / 12.0), lam_ref[...] / 12.0, mu_ref[...] / 12.0, keep,
            (1.0 - keep) * weight_ref[...],
        ],
        nx,
    )

    def layer(k):
        for t in range(ny // SUB):
            kind = material_ref[k, tile_rows(t), :]
            for i, table in enumerate(tables):
                cells_ref[i, k, tile_rows(t), :] = lookup(table, kind)

    over(0, nz, 4, layer)


def depth_kernel(stress_ref, velocity_hbm, depth_ref, along_ref, velocity_ref, sem):
    load = pltpu.make_async_copy(velocity_hbm, velocity_ref, sem)
    load.start()
    _, nz, ny, _ = stress_ref.shape
    tiles = ny // SUB

    def along(k):
        for t in range(tiles):
            for c, comp in enumerate((0, 3, 4)):
                along_ref[c, k, tile_rows(t), :] = periodic_x(stress_ref[comp, k, tile_rows(t), :])

    over(0, nz, 4, along)
    over(2, nz - 2, 4, lambda k: inner_depth(stress_ref, depth_ref, 6, k, tiles))
    load.wait()


def plane_kernel(sizes, stress_ref, along_ref, y1_ref, y2_ref, plane_ref, tall):
    _, nz, ny, nx = stress_ref.shape
    tiles = ny // SUB
    of_y = (3, 1, 5)
    fill_rows(sizes[1], tall, lambda c, k: stress_ref[of_y[c], k], y1_ref, y2_ref, nz, ny, range(nz))

    def layer(k):
        for t in range(tiles):
            for c in range(3):
                plane_ref[c, k, tile_rows(t), :] = along_ref[
                    c, k, tile_rows(t), :
                ] + row_difference(tall, c, k, t)

    over(0, nz, 4, layer)


def velocity_kernel(
    sizes, velocity_ref, stress_ref, cells_ref, inner_ref, plane_ref, factor_ref, mz_ref, slope_ref,
    x1_ref, x2_ref, z1_ref, z2_ref, low_ref, high_ref, out_ref, vlow_ref, vhigh_ref, vx1_ref, vx2_ref, vz1_ref, vz2_ref,
    *rest,
):
    *vy_refs, edge, zb, za, outer_ref = rest
    _, nz, ny, nx = velocity_ref.shape
    tiles = ny // SUB
    lane = lanes_of((SUB, nx))
    fill_edges(sizes[0], edge, x1_ref, x2_ref, low_ref, high_ref)
    depth_halos(sizes[2], zb, za, z1_ref, z2_ref)
    outer_depth(stress_ref, zb, za, outer_ref, 6, nz, tiles)

    def layer(k, depth_ref, spot):
        for t in range(tiles):
            rows = tile_rows(t)
            b = cells_ref[0, k, rows, :]
            factor = factor_ref[k, rows, :]
            mz = mz_ref[k, rows, :]
            mx = slope_ref[0, rows, :] * factor
            my = slope_ref[1, rows, :] * factor
            gk = [depth_ref[c, spot, rows, :] for c in range(6)]
            beside = [
                plane_ref[c, k, rows, :]
                + jnp.where(sides(lane), turned_left(edge[c, t % 2], k * tiles + t), 0.0)
                for c in range(3)
            ]
            accel = (
                beside[0] - mx * gk[0] - my * gk[3] + mz * gk[4],
                beside[1] - mx * gk[3] - my * gk[1] + mz * gk[5],
                beside[2] - mx * gk[4] - my * gk[5] + mz * gk[2],
            )
            for c in range(3):
                out_ref[c, k, rows, :] = velocity_ref[c, k, rows, :] + b * accel[c]

    for spot, k in enumerate((0, 1, nz - 2, nz - 1)):
        layer(k, outer_ref, spot)

    over(2, nz - 2, 4, lambda k: layer(k, inner_ref, k - 2))
    pack_sides(
        lambda c, k, t: out_ref[c, k, tile_rows(t), :], nz, ny, nx, vlow_ref, vhigh_ref, vx1_ref, vx2_ref
    )
    pack_rows(lambda c, k, rows: out_ref[c, k, rows, :], nz, ny, vy_refs)
    vz1_ref[...], vz2_ref[...] = order("gz", out_ref[:, nz - 2 : nz], out_ref[:, 0:2])


def velocity_inner_kernel(vel_ref, vel_hbm, depth_ref, along_ref, sem):
    store = pltpu.make_async_copy(vel_ref, vel_hbm, sem)
    store.start()
    _, nz, ny, nx = vel_ref.shape
    tiles = ny // SUB

    def along(k):
        for t in range(tiles):
            for c in range(3):
                along_ref[c, k, tile_rows(t), :] = periodic_x(vel_ref[c, k, tile_rows(t), :])

    over(0, nz, 4, along)
    over(2, nz - 2, 4, lambda k: inner_depth(vel_ref, depth_ref, 3, k, tiles))
    store.wait()


def stress_kernel(
    sizes, vel_ref, stress_ref, memory_ref, cells_ref, inner_ref, along_ref, factor_ref, mz_ref, slope_ref,
    x1_ref, x2_ref, low_ref, high_ref, y1_ref, y2_ref, z1_ref, z2_ref,
    stress_hbm, memory_hbm, edge, tall, zb, za, outer, stress_out, memory_out, sems,
):
    n_gx, n_gy, n_gz = sizes
    _, nz, ny, nx = vel_ref.shape
    tiles = ny // SUB
    lane = lanes_of((SUB, nx))
    fill_edges(n_gx, edge, x1_ref, x2_ref, low_ref, high_ref)
    fill_rows(n_gy, tall, lambda c, k: vel_ref[c, k], y1_ref, y2_ref, nz, ny, range(nz))

    def layer(k, depth_ref, spot):
        for t in range(tiles):
            rows = tile_rows(t)
            factor = factor_ref[k, rows, :]
            mz = mz_ref[k, rows, :]
            mx = slope_ref[0, rows, :] * factor
            my = slope_ref[1, rows, :] * factor
            dk = [depth_ref[c, spot, rows, :] for c in range(3)]
            dx = [
                along_ref[c, k, rows, :]
                + jnp.where(sides(lane), turned_left(edge[c, t % 2], k * tiles + t), 0.0)
                - mx * dk[c]
                for c in range(3)
            ]
            dy = [row_difference(tall, c, k, t) - my * dk[c] for c in range(3)]
            dz = [mz * dk[c] for c in range(3)]
            lam, mu, keep, gain = (cells_ref[i, k, rows, :] for i in range(1, 5))
            volume = lam * (dx[0] + dy[1] + dz[2])
            mu2 = mu + mu
            rates = (
                volume + mu2 * dx[0],
                volume + mu2 * dy[1],
                volume + mu2 * dz[2],
                mu * (dy[0] + dx[1]),
                mu * (dz[0] + dx[2]),
                mu * (dz[1] + dy[2]),
            )
            for c in range(6):
                kept = keep * memory_ref[c, k, rows, :] + gain * rates[c]
                memory_out[c, k, rows, :] = kept
                stress_out[c, k, rows, :] = stress_ref[c, k, rows, :] + step_size * (
                    rates[c] - kept
                )

    def out_copies(first, count, spot):
        layers = pl.ds(first, count)
        return [
            pltpu.make_async_copy(a.at[:, layers], b.at[:, layers], sems.at[i, spot])
            for i, (a, b) in enumerate(((stress_out, stress_hbm), (memory_out, memory_hbm)))
        ]

    inner = nz - 4
    step = next(d for d in (4, 3, 2, 1) if inner % d == 0)
    chunks = inner // step

    @pl.loop(0, chunks)
    def _(j):
        for i in range(step):
            k = 2 + j * step + i
            layer(k, inner_ref, k - 2)

        for copy in out_copies(2 + j * step, step, 2 + j):
            copy.start()

    depth_halos(n_gz, zb, za, z1_ref, z2_ref)
    outer_depth(vel_ref, zb, za, outer, 3, nz, tiles)
    last = []
    for spot, k in enumerate((0, 1, nz - 2, nz - 1)):
        layer(k, outer, spot)
        if spot % 2 == 1:
            last += out_copies(k - 1, 2, spot // 2)
            for copy in last[-2:]:
                copy.start()

    @pl.loop(0, chunks)
    def _(j):
        for copy in out_copies(2 + j * step, step, 2 + j):
            copy.wait()

    for copy in last:
        copy.wait()


def in_hbm(value):
    return pltpu.with_memory_space_constraint(value, pltpu.HBM)


def call(kernel, outs, in_specs, scratch=(), name=None, out_specs=None, cost=0.0):
    return pl.pallas_call(
        kernel,
        out_shape=[jax.ShapeDtypeStruct(s, F32) for s in outs],
        in_specs=in_specs,
        out_specs=out_specs or [VM] * len(outs),
        scratch_shapes=list(scratch),
        compiler_params=params(),
        cost_estimate=pl.CostEstimate(flops=int(cost * 1e9), transcendentals=0, bytes_accessed=int(cost * 3.5e6)),
        name=name,
    )


def local(
    sizes, elevation, layer_base, stretch, material, buoyancy, lame_lambda, shear_modulus,
    relax_time, anelastic_weight, velocity, stress, memory,
):
    n_gx, n_gy, n_gz = counts = tuple(sizes[a] for a in ("gx", "gy", "gz"))
    _, nz, ny, nx = velocity.shape
    rows = ny + SUB
    slab = call(
        terrain_piece_kernel,
        [(rows, nx)],
        [HB] * 3,
        [
            pltpu.VMEM(elevation.shape, jnp.int32),
            pltpu.VMEM((1, nz), F32),
            pltpu.VMEM((1, nz), F32),
            DMA((3,)),
        ],
        name="terrain_piece", cost=0.8,
    )(in_hbm(elevation), in_hbm(layer_base[None]), in_hbm(stretch[None]))[0]
    tied = lax.optimization_barrier
    faces = 2 * 3 * nz
    xs = 3 * SUB
    y_rounds = min(2, n_gy - 1) if n_gy > 1 else 1
    z_face = (6, 2, ny, nx)
    slab, stress = tied((slab, stress))
    stress_vm, low, high, x1, x2, z1, z2, *ys = call(
        pack_kernel,
        [stress.shape] + [(xs, nx)] * 4 + [z_face] * 2 + [(faces, nx)] * y_rounds,
        [HB],
        [DMA((8,))],
        name="pack_stress", cost=1.5,
    )(in_hbm(stress))
    if n_gz & (n_gz - 1):
        slab = lax.psum(slab, "gz")
    else:
        bit = 1
        while bit < n_gz:
            slab = slab + lax.ppermute(slab, "gz", [(i, i ^ bit) for i in range(n_gz)])
            if bit == 1:
                slab, z1, z2 = tied((slab, z1, z2))
            bit *= 2
    z1, z2 = exchange(sizes, "gz", z1, z2)
    ys = call(
        functools.partial(y_send_kernel, y_rounds),
        [(faces + SUB, nx)] * y_rounds,
        [VM] * (1 + y_rounds),
        name="y_send", cost=0.02,
    )(slab, *ys)
    ys, stress_vm = tied((ys, stress_vm))
    y1, y2 = exchange(sizes, "gy", ys[0], ys[-1])
    inner_k, along, velocity_vm = call(
        depth_kernel,
        [(6, nz - 4, ny, nx), velocity.shape, velocity.shape],
        [VM, HB],
        [DMA],
        name="depth", cost=1.0,
    )(stress_vm, in_hbm(velocity))
    x1, x2, inner_k = tied((x1, x2, inner_k))
    terrain, x1, x2 = call(
        functools.partial(x_send_kernel, n_gy),
        [(ny + 2 * PAD, nx)] + [(xs + SUB, nx)] * 2,
        [VM] * 5,
        name="x_send", cost=0.1,
    )(slab, y1[faces:], y2[faces:], x1, x2)
    x1, x2, material = tied((x1, x2, material))
    x1, x2 = exchange(sizes, "gx", x1, x2)
    edge = pltpu.VMEM((3, 2, SUB, nx), F32)
    tall = pltpu.VMEM((3, nz, ny + 2 * PAD, nx), F32)

    def depth(comps):
        return [pltpu.VMEM((comps, 2, ny, nx), F32)] * 2

    tables = (buoyancy, lame_lambda, shear_modulus, relax_time, anelastic_weight)
    cells = call(
        cell_kernel,
        [(5, nz, ny, nx)],
        [HB] * 6,
        [pltpu.VMEM(material.shape, jnp.int32)]
        + [pltpu.VMEM((1, table.shape[0]), F32) for table in tables]
        + [DMA((6,))],
        name="cells", cost=1.2,
    )(in_hbm(material), *[in_hbm(table[None]) for table in tables])[0]
    plane = call(
        functools.partial(plane_kernel, counts), [velocity.shape], [VM] * 4, [tall], name="planes", cost=0.4
    )(stress_vm, along, y1, y2)[0]
    plane, cells, x1, x2 = tied((plane, cells, x1, x2))
    factor, mz, slope = call(
        functools.partial(metric_kernel, counts),
        [(nz, ny, nx), (nz, ny, nx), (2, ny, nx)],
        [SM] + [VM] * 3,
        [pltpu.VMEM((ny + 2 * PAD, nx), F32), pltpu.VMEM((ny + PAD, nx), F32)],
        name="metrics", cost=1.1,
    )(slab[ny:], terrain, x1[xs:], x2[xs:])
    vel, vlow, vhigh, vx1, vx2, vz1, vz2, *vys = call(
        functools.partial(velocity_kernel, counts),
        [velocity.shape] + [(xs, nx)] * 4 + [(3, 2, ny, nx)] * 2 + [(faces, nx)] * y_rounds,
        [VM] * 14,
        [edge] + depth(6) + [pltpu.VMEM((6, 4, ny, nx), F32)],
        name="velocity", cost=1.5,
    )(velocity_vm, stress_vm, cells, inner_k, plane, factor, mz, slope, x1, x2, z1, z2, low, high)
    vz1, vz2 = exchange(sizes, "gz", vz1, vz2)
    vy1, vy2 = exchange(sizes, "gy", vys[0], vys[-1])
    vx1, vx2 = exchange(sizes, "gx", vx1, vx2)
    vel_next, vel_k, vel_x = call(
        velocity_inner_kernel,
        [velocity.shape, (3, nz - 4, ny, nx), velocity.shape],
        [VM],
        [DMA],
        name="velocity_inner", cost=1.0,
        out_specs=[HB, VM, VM],
    )(vel)
    stress_next, memory_next = call(
        functools.partial(stress_kernel, counts),
        [stress.shape, stress.shape],
        [VM] * 17,
        [edge, tall] + depth(3)
        + [pltpu.VMEM((3, 4, ny, nx), F32), pltpu.VMEM(stress.shape, F32), pltpu.VMEM(stress.shape, F32)]
        + [DMA((2, nz))],
        name="stress", cost=2.8,
        out_specs=[HB] * 2,
    )(
        vel, stress_vm, memory, cells, vel_k, vel_x, factor, mz, slope, vx1, vx2, vlow, vhigh, vy1, vy2,
        vz1, vz2,
    )
    return vel_next, stress_next, memory_next


def solution(mesh):
    sizes = {a: mesh.shape[a] for a in ("gx", "gy", "gz")}
    field = P(None, "gz", "gy", "gx")
    return jax.shard_map(
        functools.partial(local, sizes),
        mesh=mesh,
        in_specs=(
            P("gy", ("gx", "gz")), P("gz"), P("gz"), P("gz", "gy", "gx"),
            P(), P(), P(), P(), P(), field, field, field,
        ),
        out_specs=(field, field, field),
        check_vma=False,
    )
```

```python
import functools
import jax
import jax.numpy as jnp
import numpy as np
from jax import lax
from jax.experimental import pallas as pl
from jax.experimental.pallas import tpu as pltpu
from jax.sharding import PartitionSpec as P

step_size = 0.3
SUB = 8
PAD = 8
F32 = jnp.float32
params = functools.partial(pltpu.CompilerParams, vmem_limit_bytes=20 * 1024 * 1024)
VM = pl.BlockSpec(memory_space=pltpu.VMEM)
SM = pl.BlockSpec(memory_space=pltpu.SMEM)
HB = pl.BlockSpec(memory_space=pltpu.HBM)
DMA = pltpu.SemaphoreType.DMA


def pair_swaps(sizes, axis):
    names = tuple(sizes)
    shape = tuple(sizes.values())
    index = names.index(axis)
    n = shape[index]
    others = [d for d in (2, 1, 0) if d != index and shape[d] % 2 == 0]
    rounds = []
    for first in (0, 1)[: max(0, min(2, n - 1))]:
        table = []
        for spot in np.ndindex(*shape):
            mate = spot[index] + 1 if spot[index] % 2 == first else spot[index] - 1
            target = list(spot)
            if 0 <= mate < n or axis == "gz":
                target[index] = mate % n
            elif others:
                target[others[0]] ^= 1
            else:
                continue
            table.append((int(np.ravel_multi_index(spot, shape)), int(np.ravel_multi_index(tuple(target), shape))))
        rounds.append(table)
    return rounds


def exchange(sizes, axis, first, second):
    rounds = pair_swaps(sizes, axis)
    got = [lax.ppermute(v, tuple(sizes), r) for v, r in zip((first, second), rounds)]
    return (got[0], got[-1]) if got else (first, second)


def even(axis):
    return lax.axis_index(axis) % 2 == 0


def from_before(axis, got):
    value = jnp.where(even(axis), got[1], got[0])
    return jnp.where(lax.axis_index(axis) > 0, value, 0.0)


def from_after(axis, n, got):
    value = jnp.where(even(axis), got[0], got[1])
    return jnp.where(lax.axis_index(axis) < n - 1, value, 0.0)


def order(axis, to_after, to_before):
    e = even(axis)
    return jnp.where(e, to_after, to_before), jnp.where(e, to_before, to_after)


def lanes_of(shape):
    return lax.broadcasted_iota(jnp.int32, shape, len(shape) - 1)


def terrain_piece_kernel(elev_hbm, base_hbm, stretch_hbm, out_ref, elev_ref, base_ref, stretch_ref, sems):
    mine = lax.axis_index("gz")
    pairs = ((elev_hbm, elev_ref), (base_hbm, base_ref), (stretch_hbm, stretch_ref))
    copies = [pltpu.make_async_copy(a, b, sems.at[i]) for i, (a, b) in enumerate(pairs)]
    for copy in copies:
        copy.start()
    for copy in copies:
        copy.wait()
    ny, width = elev_ref.shape
    nx = out_ref.shape[1]
    nz = base_ref.shape[1]
    height = elev_ref[...].astype(F32) / 200.0
    wide = jnp.concatenate([height, jnp.zeros((ny, nx - width), F32)], axis=1)
    out_ref[:ny, :] = pltpu.roll(wide, mine * width, 1)
    row = lax.broadcasted_iota(jnp.int32, (SUB, nx), 0)
    fill = jnp.zeros((1, nx - nz), F32)
    base = jnp.concatenate([base_ref[...], fill], axis=1)
    stretch = jnp.concatenate([stretch_ref[...], fill], axis=1)
    both = jnp.where(row == 0, base, jnp.where(row == 1, stretch, 0.0))
    out_ref[ny:, :] = pltpu.roll(both, mine * nz, 1)


def pack_sides(field, nz, ny, nx, low_ref, high_ref, out1_ref, out2_ref):
    tiles = ny // SUB
    lane2 = lanes_of((SUB, nx)) // 2
    for c in range(3):
        lo = jnp.zeros((SUB, nx), F32)
        hi = jnp.zeros((SUB, nx), F32)
        for k in range(nz):
            for t in range(tiles):
                m = k * tiles + t
                turned = pltpu.roll(field(c, k, t), (2 * m + 2) % nx, 1)
                hi = jnp.where(lane2 == m, turned, hi)
                lo = jnp.where(lane2 == (m + 1) % (nx // 2), turned, lo)
        at = slice(SUB * c, SUB * c + SUB)
        low_ref[at, :] = lo
        high_ref[at, :] = hi
        out1_ref[at, :], out2_ref[at, :] = order("gx", hi, lo)


def pack_rows(field, nz, ny, y_refs):
    for c in range(3):
        for k in range(nz):
            j = 2 * (c * nz + k)
            both = order("gy", field(c, k, slice(ny - 2, ny)), field(c, k, slice(0, 2)))
            for ref, rows in zip(y_refs, both):
                ref[j : j + 2, :] = rows


def pack_kernel(stress_ref, low_ref, high_ref, out1_ref, out2_ref, z1_ref, z2_ref, *y_refs):
    _, nz, ny, nx = stress_ref.shape
    of_x = (0, 3, 4)
    of_y = (3, 1, 5)
    z1_ref[...], z2_ref[...] = order("gz", stress_ref[:, nz - 2 : nz], stress_ref[:, 0:2])
    pack_sides(
        lambda c, k, t: stress_ref[of_x[c], k, SUB * t : SUB * t + SUB, :],
        nz, ny, nx, low_ref, high_ref, out1_ref, out2_ref,
    )
    pack_rows(lambda c, k, rows: stress_ref[of_y[c], k, rows, :], nz, ny, y_refs)


def y_send_kernel(slab_ref, *out_refs):
    ny = slab_ref.shape[0] - SUB
    both = order("gy", slab_ref[ny - 4 : ny, :], slab_ref[0:4, :])
    for ref, rows in zip(out_refs, both):
        ref[0:4, :] = rows
        ref[4:, :] = jnp.zeros_like(rows)


def x_send_kernel(n_gy, slab_ref, y1_ref, y2_ref, x1_ref, x2_ref, tall_ref, out1_ref, out2_ref):
    ny = slab_ref.shape[0] - SUB
    nx = slab_ref.shape[1]
    xs = x1_ref.shape[0]
    lane4 = lanes_of((SUB, nx)) // 4
    got = (y1_ref[0:4, :], y2_ref[0:4, :])
    tall_ref[: PAD - 4, :] = jnp.zeros((PAD - 4, nx), F32)
    tall_ref[PAD - 4 : PAD, :] = from_before("gy", got)
    tall_ref[PAD : PAD + ny, :] = slab_ref[:ny, :]
    tall_ref[PAD + ny : PAD + ny + 4, :] = from_after("gy", n_gy, got)
    tall_ref[PAD + ny + 4 :, :] = jnp.zeros((PAD - 4, nx), F32)
    lo = jnp.zeros((SUB, nx), F32)
    hi = jnp.zeros((SUB, nx), F32)
    for j in range((ny + 2 * PAD) // SUB):
        tile = tall_ref[SUB * j : SUB * j + SUB, :]
        lo = jnp.where(lane4 == j, pltpu.roll(tile, 4 * j, 1), lo)
        hi = jnp.where(lane4 == j, pltpu.roll(tile, (4 * j + 4) % nx, 1), hi)
    out1_ref[:xs, :] = x1_ref[...]
    out2_ref[:xs, :] = x2_ref[...]
    out1_ref[xs:, :], out2_ref[xs:, :] = order("gx", hi, lo)


def binomial(at):
    return (at(-2) + at(2) + 4.0 * (at(-1) + at(1)) + 6.0 * at(0)) / 16.0


def centred12(at):
    return 8.0 * (at(1) - at(-1)) - (at(2) - at(-2))


def metric_kernel(
    sizes, layers_ref, own, x1_ref, x2_ref, factor_ref, mz_ref, slope_ref, rim, sown,
):
    n_gx = sizes[0]
    gz = lax.axis_index("gz")
    nz, ny, nx = factor_ref.shape
    lane = lanes_of((SUB, nx))
    got = (x1_ref[...], x2_ref[...])
    left, right = from_before("gx", got), from_after("gx", n_gx, got)
    for j in range((ny + 2 * PAD) // SUB):
        rim[SUB * j : SUB * j + SUB, :] = jnp.where(
            lane < nx // 2,
            pltpu.roll(right, (nx - 4 * j) % nx, 1),
            pltpu.roll(left, nx - 4 - 4 * j, 1),
        )
    rows = ny + 4
    tall_own = binomial(lambda s: own[PAD - 2 + s : PAD - 2 + s + rows, :])
    tall_rim = binomial(lambda s: rim[PAD - 2 + s : PAD - 2 + s + rows, :])

    def shifted(a, b, s):
        ln = lanes_of(a.shape)
        cut = (ln < s) if s > 0 else (ln >= nx + s)
        if s > 0:
            mixed_a, mixed_b = jnp.where(cut, b, a), jnp.where(cut, a, b)
        elif s < 0:
            mixed_a, mixed_b = jnp.where(cut, b, a), jnp.where(cut, a, b)
        else:
            return a, b
        return pltpu.roll(mixed_a, (-s) % nx, 1), pltpu.roll(mixed_b, (-s) % nx, 1)

    def padded_rows(a):
        return jnp.concatenate([a, jnp.zeros((SUB - rows % SUB, nx), F32)], axis=0)

    tall_own, tall_rim = padded_rows(tall_own), padded_rows(tall_rim)
    pairs = {s: shifted(tall_own, tall_rim, s) for s in (-2, -1, 0, 1, 2)}
    surf_own = binomial(lambda s: pairs[s][0])
    surf_rim = binomial(lambda s: pairs[s][1])
    sown[...] = surf_own
    slope_ref[1] = centred12(lambda s: sown[2 + s : 2 + s + ny, :]) / 12.0
    pairs2 = {s: shifted(surf_own, surf_rim, s)[0] for s in (-2, -1, 1, 2)}
    along = centred12(lambda s: pairs2[s]) / 12.0
    surface = sown[2 : 2 + ny, :]
    sown[...] = along
    slope_ref[0] = sown[2 : 2 + ny, :]

    def above(slab, total):
        for k in range(nz):
            at = pl.ds(slab * nz + k, 1)
            s = layers_ref[1, at, :]
            total = total + (s * layers_ref[0, at, :]) * jnp.exp(s * surface)
        return total

    total = lax.fori_loop(0, gz, above, jnp.zeros((ny, nx), F32))
    for k in range(nz):
        at = pl.ds(gz * nz + k, 1)
        s = layers_ref[1, at, :]
        thickness = layers_ref[0, at, :] * jnp.exp(s * surface)
        weighted = s * thickness
        mz = 1.0 / thickness
        lift = total + 0.5 * weighted
        total = total + weighted
        mz_ref[k] = mz
        factor_ref[k] = (lift - 1.0) * mz

def edge_terms(got_left, got_right, low, high):
    dl = got_left - high
    dr = got_right - low
    nx = dl.shape[-1]
    lane = lanes_of(dl.shape)
    even = lane % 2 == 0
    dl = pltpu.roll(dl, 2, 1)
    dr = pltpu.roll(dr, nx - 2, 1)
    to_low = jnp.where(even, dl - 8.0 * pltpu.roll(dl, nx - 1, 1), dl)
    to_high = jnp.where(even, -dr, 8.0 * pltpu.roll(dr, 1, 1) - dr)
    second = (lane // 2) % 2 == 1
    return jnp.where(second, to_low, to_high), jnp.where(second, to_high, to_low)


def turned_left(edges, m):
    nx = edges.shape[-1]
    shift = (2 * nx - 2 - 2 * m) % nx if isinstance(m, int) else 2 * nx - 2 - 2 * m
    return pltpu.roll(edges, shift, 1)


def sides(lane):
    return (lane < 2) | (lane >= lane.shape[-1] - 2)


def periodic_x(tile):
    nx = tile.shape[-1]
    return 8.0 * (pltpu.roll(tile, nx - 1, 1) - pltpu.roll(tile, 1, 1)) - (
        pltpu.roll(tile, nx - 2, 1) - pltpu.roll(tile, 2, 1)
    )


def lookup(row, tile):
    table = jnp.broadcast_to(row, tile.shape)
    return jnp.take_along_axis(table, tile, axis=1, mode="promise_in_bounds")


def table_rows(refs, nx):
    n = refs[0].shape[1]
    return [jnp.concatenate([r, jnp.zeros((1, nx - n), F32)], axis=1) for r in refs]


def fill_edges(n_gx, edge_ref, x1_ref, x2_ref, low_ref, high_ref):
    for c in range(3):
        at = slice(SUB * c, SUB * c + SUB)
        got = (x1_ref[at, :], x2_ref[at, :])
        first, second = edge_terms(
            from_before("gx", got), from_after("gx", n_gx, got), low_ref[at, :], high_ref[at, :]
        )
        edge_ref[c, 0] = first
        edge_ref[c, 1] = second


def fill_rows(n_gy, tall, field, y1_ref, y2_ref, nz, ny, layers):
    for c in range(3):
        for spot, k in enumerate(layers):
            j = 2 * (c * nz + k)
            got = (y1_ref[j : j + 2, :], y2_ref[j : j + 2, :])
            tall[c, spot, PAD : PAD + ny, :] = field(c, k)
            tall[c, spot, PAD - 2 : PAD, :] = from_before("gy", got)
            tall[c, spot, PAD + ny : PAD + ny + 2, :] = from_after("gy", n_gy, got)


def depth_halos(n_gz, zb, za, z1_ref, z2_ref):
    got = (z1_ref[...], z2_ref[...])
    zb[...] = from_before("gz", got)
    za[...] = from_after("gz", n_gz, got)


def over(low, high, most, body):
    count = high - low
    group = next(d for d in range(most, 0, -1) if count % d == 0)

    @pl.loop(0, count // group)
    def _(j):
        for i in range(group):
            body(low + j * group + i)


def tile_rows(t):
    return slice(SUB * t, SUB * t + SUB)


def row_difference(tall, c, spot, t):
    return centred12(lambda s: tall[c, spot, PAD + SUB * t + s : PAD + SUB * t + s + SUB, :])


def inner_depth(ref, out_ref, comps, k, tiles):
    for t in range(tiles):
        for c in range(comps):
            out_ref[c, k - 2, tile_rows(t), :] = centred12(lambda s: ref[c, k + s, tile_rows(t), :])


def outer_depth(ref, zb, za, out_ref, comps, nz, tiles):
    for spot, k in enumerate((0, 1, nz - 2, nz - 1)):
        for t in range(tiles):
            for c in range(comps):

                def at(s):
                    if k + s < 0:
                        return zb[c, k + s + 2, tile_rows(t), :]
                    if k + s >= nz:
                        return za[c, k + s - nz, tile_rows(t), :]
                    return ref[c, k + s, tile_rows(t), :]

                out_ref[c, spot, tile_rows(t), :] = centred12(at)


def cell_kernel(
    layers_ref, material_ref, buoy_ref, lam_ref, mu_ref, relax_ref, weight_ref, cells_ref, spread_ref
):
    lane = lanes_of((SUB, layers_ref.shape[1]))
    sub = lax.broadcasted_iota(jnp.int32, lane.shape, 0)
    for i in range(2):
        row = jnp.broadcast_to(layers_ref[i : i + 1, :], lane.shape)
        for g in range(spread_ref.shape[1] // SUB):
            one = jnp.sum(jnp.where(lane == SUB * g + sub, row, 0.0), axis=1, keepdims=True)
            spread_ref[i, tile_rows(g), :] = jnp.broadcast_to(one, lane.shape)
    nz, ny, nx = material_ref.shape
    keep = jnp.exp(-step_size / relax_ref[...])
    tables = table_rows(
        [
            buoy_ref[...] * (step_size / 12.0), lam_ref[...] / 12.0, mu_ref[...] / 12.0, keep,
            (1.0 - keep) * weight_ref[...],
        ],
        nx,
    )

    def layer(k):
        for t in range(ny // SUB):
            kind = material_ref[k, tile_rows(t), :]
            for i, table in enumerate(tables):
                cells_ref[i, k, tile_rows(t), :] = lookup(table, kind)

    over(0, nz, 4, layer)


def depth_kernel(stress_ref, depth_ref, along_ref):
    _, nz, ny, _ = stress_ref.shape
    tiles = ny // SUB

    def along(k):
        for t in range(tiles):
            for c, comp in enumerate((0, 3, 4)):
                along_ref[c, k, tile_rows(t), :] = periodic_x(stress_ref[comp, k, tile_rows(t), :])

    over(0, nz, 4, along)
    over(2, nz - 2, 4, lambda k: inner_depth(stress_ref, depth_ref, 6, k, tiles))


def plane_kernel(sizes, stress_ref, along_ref, y1_ref, y2_ref, plane_ref, tall):
    _, nz, ny, nx = stress_ref.shape
    tiles = ny // SUB
    of_y = (3, 1, 5)
    fill_rows(sizes[1], tall, lambda c, k: stress_ref[of_y[c], k], y1_ref, y2_ref, nz, ny, range(nz))

    def layer(k):
        for t in range(tiles):
            for c in range(3):
                plane_ref[c, k, tile_rows(t), :] = along_ref[
                    c, k, tile_rows(t), :
                ] + row_difference(tall, c, k, t)

    over(0, nz, 4, layer)


def velocity_kernel(
    sizes, velocity_ref, stress_ref, cells_ref, inner_ref, plane_ref, factor_ref, mz_ref, slope_ref,
    x1_ref, x2_ref, z1_ref, z2_ref, low_ref, high_ref, out_ref, vlow_ref, vhigh_ref, vx1_ref, vx2_ref, vz1_ref, vz2_ref,
    *rest,
):
    *vy_refs, edge, zb, za, outer_ref = rest
    _, nz, ny, nx = velocity_ref.shape
    tiles = ny // SUB
    lane = lanes_of((SUB, nx))
    fill_edges(sizes[0], edge, x1_ref, x2_ref, low_ref, high_ref)
    depth_halos(sizes[2], zb, za, z1_ref, z2_ref)
    outer_depth(stress_ref, zb, za, outer_ref, 6, nz, tiles)

    def layer(k, depth_ref, spot):
        for t in range(tiles):
            rows = tile_rows(t)
            b = cells_ref[0, k, rows, :]
            factor = factor_ref[k, rows, :]
            mz = mz_ref[k, rows, :]
            mx = slope_ref[0, rows, :] * factor
            my = slope_ref[1, rows, :] * factor
            gk = [depth_ref[c, spot, rows, :] for c in range(6)]
            beside = [
                plane_ref[c, k, rows, :]
                + jnp.where(sides(lane), turned_left(edge[c, t % 2], k * tiles + t), 0.0)
                for c in range(3)
            ]
            accel = (
                beside[0] - mx * gk[0] - my * gk[3] + mz * gk[4],
                beside[1] - mx * gk[3] - my * gk[1] + mz * gk[5],
                beside[2] - mx * gk[4] - my * gk[5] + mz * gk[2],
            )
            for c in range(3):
                out_ref[c, k, rows, :] = velocity_ref[c, k, rows, :] + b * accel[c]

    for spot, k in enumerate((0, 1, nz - 2, nz - 1)):
        layer(k, outer_ref, spot)

    over(2, nz - 2, 4, lambda k: layer(k, inner_ref, k - 2))
    pack_sides(
        lambda c, k, t: out_ref[c, k, tile_rows(t), :], nz, ny, nx, vlow_ref, vhigh_ref, vx1_ref, vx2_ref
    )
    pack_rows(lambda c, k, rows: out_ref[c, k, rows, :], nz, ny, vy_refs)
    vz1_ref[...], vz2_ref[...] = order("gz", out_ref[:, nz - 2 : nz], out_ref[:, 0:2])


def velocity_inner_kernel(vel_ref, vel_hbm, depth_ref, along_ref, sem):
    store = pltpu.make_async_copy(vel_ref, vel_hbm, sem)
    store.start()
    _, nz, ny, nx = vel_ref.shape
    tiles = ny // SUB

    def along(k):
        for t in range(tiles):
            for c in range(3):
                along_ref[c, k, tile_rows(t), :] = periodic_x(vel_ref[c, k, tile_rows(t), :])

    over(0, nz, 4, along)
    over(2, nz - 2, 4, lambda k: inner_depth(vel_ref, depth_ref, 3, k, tiles))
    store.wait()


def stress_kernel(
    sizes, vel_ref, stress_ref, memory_ref, cells_ref, inner_ref, along_ref, factor_ref, mz_ref, slope_ref,
    x1_ref, x2_ref, low_ref, high_ref, y1_ref, y2_ref, z1_ref, z2_ref,
    stress_hbm, memory_hbm, edge, tall, zb, za, outer, stress_out, memory_out, sems,
):
    n_gx, n_gy, n_gz = sizes
    _, nz, ny, nx = vel_ref.shape
    tiles = ny // SUB
    lane = lanes_of((SUB, nx))
    fill_edges(n_gx, edge, x1_ref, x2_ref, low_ref, high_ref)
    fill_rows(n_gy, tall, lambda c, k: vel_ref[c, k], y1_ref, y2_ref, nz, ny, range(nz))

    def layer(k, depth_ref, spot):
        for t in range(tiles):
            rows = tile_rows(t)
            factor = factor_ref[k, rows, :]
            mz = mz_ref[k, rows, :]
            mx = slope_ref[0, rows, :] * factor
            my = slope_ref[1, rows, :] * factor
            dk = [depth_ref[c, spot, rows, :] for c in range(3)]
            dx = [
                along_ref[c, k, rows, :]
                + jnp.where(sides(lane), turned_left(edge[c, t % 2], k * tiles + t), 0.0)
                - mx * dk[c]
                for c in range(3)
            ]
            dy = [row_difference(tall, c, k, t) - my * dk[c] for c in range(3)]
            dz = [mz * dk[c] for c in range(3)]
            lam, mu, keep, gain = (cells_ref[i, k, rows, :] for i in range(1, 5))
            volume = lam * (dx[0] + dy[1] + dz[2])
            mu2 = mu + mu
            rates = (
                volume + mu2 * dx[0],
                volume + mu2 * dy[1],
                volume + mu2 * dz[2],
                mu * (dy[0] + dx[1]),
                mu * (dz[0] + dx[2]),
                mu * (dz[1] + dy[2]),
            )
            for c in range(6):
                kept = keep * memory_ref[c, k, rows, :] + gain * rates[c]
                memory_out[c, k, rows, :] = kept
                stress_out[c, k, rows, :] = stress_ref[c, k, rows, :] + step_size * (
                    rates[c] - kept
                )

    def out_copies(first, count, spot):
        layers = pl.ds(first, count)
        return [
            pltpu.make_async_copy(a.at[:, layers], b.at[:, layers], sems.at[i, spot])
            for i, (a, b) in enumerate(((stress_out, stress_hbm), (memory_out, memory_hbm)))
        ]

    inner = nz - 4
    step = next(d for d in (4, 3, 2, 1) if inner % d == 0)
    chunks = inner // step

    @pl.loop(0, chunks)
    def _(j):
        for i in range(step):
            k = 2 + j * step + i
            layer(k, inner_ref, k - 2)

        for copy in out_copies(2 + j * step, step, 2 + j):
            copy.start()

    depth_halos(n_gz, zb, za, z1_ref, z2_ref)
    outer_depth(vel_ref, zb, za, outer, 3, nz, tiles)
    last = []
    for spot, k in enumerate((0, 1, nz - 2, nz - 1)):
        layer(k, outer, spot)
        if spot % 2 == 1:
            last += out_copies(k - 1, 2, spot // 2)
            for copy in last[-2:]:
                copy.start()

    @pl.loop(0, chunks)
    def _(j):
        for copy in out_copies(2 + j * step, step, 2 + j):
            copy.wait()

    for copy in last:
        copy.wait()


def in_hbm(value):
    return pltpu.with_memory_space_constraint(value, pltpu.HBM)


def call(kernel, outs, in_specs, scratch=(), name=None, out_specs=None, cost=0.0):
    return pl.pallas_call(
        kernel,
        out_shape=[jax.ShapeDtypeStruct(s, F32) for s in outs],
        in_specs=in_specs,
        out_specs=out_specs or [VM] * len(outs),
        scratch_shapes=list(scratch),
        compiler_params=params(),
        cost_estimate=pl.CostEstimate(flops=int(cost * 6e8), transcendentals=0, bytes_accessed=int(cost * 3.5e6)),
        name=name,
    )


def local(
    sizes, elevation, layer_base, stretch, material, buoyancy, lame_lambda, shear_modulus,
    relax_time, anelastic_weight, velocity, stress, memory,
):
    n_gx, n_gy, n_gz = counts = tuple(sizes[a] for a in ("gx", "gy", "gz"))
    _, nz, ny, nx = velocity.shape
    rows = ny + SUB
    slab = call(
        terrain_piece_kernel,
        [(rows, nx)],
        [HB] * 3,
        [
            pltpu.VMEM(elevation.shape, jnp.int32),
            pltpu.VMEM((1, nz), F32),
            pltpu.VMEM((1, nz), F32),
            DMA((3,)),
        ],
        name="terrain_piece", cost=0.8,
    )(in_hbm(elevation), in_hbm(layer_base[None]), in_hbm(stretch[None]))[0]
    tied = lax.optimization_barrier
    faces = 2 * 3 * nz
    xs = 3 * SUB
    y_rounds = min(2, n_gy - 1) if n_gy > 1 else 1
    z_face = (6, 2, ny, nx)
    slab, stress = tied((slab, stress))
    stress_vm = stress
    low, high, x1, x2, z1, z2, *ys = call(
        pack_kernel,
        [(xs, nx)] * 4 + [z_face] * 2 + [(faces, nx)] * y_rounds,
        [VM],
        name="pack_stress", cost=0.5,
    )(stress)
    if n_gz & (n_gz - 1):
        slab = lax.psum(slab, "gz")
    else:
        bit = 1
        while bit < n_gz:
            slab = slab + lax.ppermute(slab, "gz", [(i, i ^ bit) for i in range(n_gz)])
            if bit == 1:
                slab, z1, z2 = tied((slab, z1, z2))
            bit *= 2
    z1, z2 = exchange(sizes, "gz", z1, z2)
    ts = call(y_send_kernel, [(SUB, nx)] * y_rounds, [VM], name="y_send", cost=0.02)(slab)
    ts, ys = tied((ts, ys))
    t1, t2 = exchange(sizes, "gy", ts[0], ts[-1])
    y1, y2 = exchange(sizes, "gy", ys[0], ys[-1])
    terrain, x1, x2 = call(
        functools.partial(x_send_kernel, n_gy),
        [(ny + 2 * PAD, nx)] + [(xs + SUB, nx)] * 2,
        [VM] * 5,
        name="x_send", cost=0.1,
    )(slab, t1, t2, x1, x2)
    x1, x2, material, stress_vm = tied((x1, x2, material, stress_vm))
    x1, x2 = exchange(sizes, "gx", x1, x2)
    edge = pltpu.VMEM((3, 2, SUB, nx), F32)
    tall = pltpu.VMEM((3, nz, ny + 2 * PAD, nx), F32)

    def depth(comps):
        return [pltpu.VMEM((comps, 2, ny, nx), F32)] * 2

    tables = (buoyancy, lame_lambda, shear_modulus, relax_time, anelastic_weight)
    all_layers = -(-n_gz * nz // SUB) * SUB
    cells, spread = call(
        cell_kernel, [(5, nz, ny, nx), (2, all_layers, nx)], [VM] * 7, name="cells", cost=0.8
    )(slab[ny:], material, *[table[None] for table in tables])
    inner_k, along = call(
        depth_kernel, [(6, nz - 4, ny, nx), velocity.shape], [VM], name="depth", cost=0.9
    )(stress_vm)
    plane = call(
        functools.partial(plane_kernel, counts), [velocity.shape], [VM] * 4, [tall], name="planes", cost=0.4
    )(stress_vm, along, y1, y2)[0]
    plane, cells, x1, x2 = tied((plane, cells, x1, x2))
    factor, mz, slope = call(
        functools.partial(metric_kernel, counts),
        [(nz, ny, nx), (nz, ny, nx), (2, ny, nx)],
        [VM] * 4,
        [pltpu.VMEM((ny + 2 * PAD, nx), F32), pltpu.VMEM((ny + PAD, nx), F32)],
        name="metrics", cost=1.1,
    )(spread, terrain, x1[xs:], x2[xs:])
    vel, vlow, vhigh, vx1, vx2, vz1, vz2, *vys = call(
        functools.partial(velocity_kernel, counts),
        [velocity.shape] + [(xs, nx)] * 4 + [(3, 2, ny, nx)] * 2 + [(faces, nx)] * y_rounds,
        [VM] * 14,
        [edge] + depth(6) + [pltpu.VMEM((6, 4, ny, nx), F32)],
        name="velocity", cost=1.5,
    )(velocity, stress_vm, cells, inner_k, plane, factor, mz, slope, x1, x2, z1, z2, low, high)
    vz1, vz2 = exchange(sizes, "gz", vz1, vz2)
    vy1, vy2 = exchange(sizes, "gy", vys[0], vys[-1])
    vx1, vx2 = exchange(sizes, "gx", vx1, vx2)
    vel_next, vel_k, vel_x = call(
        velocity_inner_kernel,
        [velocity.shape, (3, nz - 4, ny, nx), velocity.shape],
        [VM],
        [DMA],
        name="velocity_inner", cost=0.1,
        out_specs=[HB, VM, VM],
    )(vel)
    stress_next, memory_next = call(
        functools.partial(stress_kernel, counts),
        [stress.shape, stress.shape],
        [VM] * 17,
        [edge, tall] + depth(3)
        + [pltpu.VMEM((3, 4, ny, nx), F32), pltpu.VMEM(stress.shape, F32), pltpu.VMEM(stress.shape, F32)]
        + [DMA((2, nz))],
        name="stress", cost=2.8,
        out_specs=[HB] * 2,
    )(
        vel, stress_vm, memory, cells, vel_k, vel_x, factor, mz, slope, vx1, vx2, vlow, vhigh, vy1, vy2,
        vz1, vz2,
    )
    return vel_next, stress_next, memory_next


def solution(mesh):
    sizes = {a: mesh.shape[a] for a in ("gx", "gy", "gz")}
    field = P(None, "gz", "gy", "gx")
    return jax.shard_map(
        functools.partial(local, sizes),
        mesh=mesh,
        in_specs=(
            P("gy", ("gx", "gz")), P("gz"), P("gz"), P("gz", "gy", "gx"),
            P(), P(), P(), P(), P(), field, field, field,
        ),
        out_specs=(field, field, field),
        check_vma=False,
    )
```

```python
import functools
import jax
import jax.numpy as jnp
import numpy as np
from jax import lax
from jax.experimental import pallas as pl
from jax.experimental.pallas import tpu as pltpu
from jax.sharding import PartitionSpec as P

step_size = 0.3
SUB = 8
PAD = 8
F32 = jnp.float32
params = functools.partial(pltpu.CompilerParams, vmem_limit_bytes=20 * 1024 * 1024)
VM = pl.BlockSpec(memory_space=pltpu.VMEM)
SM = pl.BlockSpec(memory_space=pltpu.SMEM)
HB = pl.BlockSpec(memory_space=pltpu.HBM)
DMA = pltpu.SemaphoreType.DMA


def pair_swaps(sizes, axis):
    names = tuple(sizes)
    shape = tuple(sizes.values())
    index = names.index(axis)
    n = shape[index]
    others = [d for d in (2, 1, 0) if d != index and shape[d] % 2 == 0]
    rounds = []
    for first in (0, 1)[: max(0, min(2, n - 1))]:
        table = []
        for spot in np.ndindex(*shape):
            mate = spot[index] + 1 if spot[index] % 2 == first else spot[index] - 1
            target = list(spot)
            if 0 <= mate < n or axis == "gz":
                target[index] = mate % n
            elif others:
                target[others[0]] ^= 1
            else:
                continue
            table.append((int(np.ravel_multi_index(spot, shape)), int(np.ravel_multi_index(tuple(target), shape))))
        rounds.append(table)
    return rounds


def exchange(sizes, axis, first, second):
    rounds = pair_swaps(sizes, axis)
    got = [lax.ppermute(v, tuple(sizes), r) for v, r in zip((first, second), rounds)]
    return (got[0], got[-1]) if got else (first, second)


def even(axis):
    return lax.axis_index(axis) % 2 == 0


def from_before(axis, got):
    value = jnp.where(even(axis), got[1], got[0])
    return jnp.where(lax.axis_index(axis) > 0, value, 0.0)


def from_after(axis, n, got):
    value = jnp.where(even(axis), got[0], got[1])
    return jnp.where(lax.axis_index(axis) < n - 1, value, 0.0)


def order(axis, to_after, to_before):
    e = even(axis)
    return jnp.where(e, to_after, to_before), jnp.where(e, to_before, to_after)


def lanes_of(shape):
    return lax.broadcasted_iota(jnp.int32, shape, len(shape) - 1)


def terrain_piece_kernel(elev_hbm, base_hbm, stretch_hbm, out_ref, elev_ref, base_ref, stretch_ref, sems):
    mine = lax.axis_index("gz")
    pairs = ((elev_hbm, elev_ref), (base_hbm, base_ref), (stretch_hbm, stretch_ref))
    copies = [pltpu.make_async_copy(a, b, sems.at[i]) for i, (a, b) in enumerate(pairs)]
    for copy in copies:
        copy.start()
    for copy in copies:
        copy.wait()
    ny, width = elev_ref.shape
    nx = out_ref.shape[1]
    nz = base_ref.shape[1]
    height = elev_ref[...].astype(F32) / 200.0
    wide = jnp.concatenate([height, jnp.zeros((ny, nx - width), F32)], axis=1)
    out_ref[:ny, :] = pltpu.roll(wide, mine * width, 1)
    row = lax.broadcasted_iota(jnp.int32, (SUB, nx), 0)
    fill = jnp.zeros((1, nx - nz), F32)
    base = jnp.concatenate([base_ref[...], fill], axis=1)
    stretch = jnp.concatenate([stretch_ref[...], fill], axis=1)
    both = jnp.where(row == 0, base, jnp.where(row == 1, stretch, 0.0))
    out_ref[ny:, :] = pltpu.roll(both, mine * nz, 1)


def pack_sides(field, nz, ny, nx, low_ref, high_ref, out1_ref, out2_ref):
    tiles = ny // SUB
    lane2 = lanes_of((SUB, nx)) // 2
    for c in range(3):
        lo = jnp.zeros((SUB, nx), F32)
        hi = jnp.zeros((SUB, nx), F32)
        for k in range(nz):
            for t in range(tiles):
                m = k * tiles + t
                turned = pltpu.roll(field(c, k, t), (2 * m + 2) % nx, 1)
                hi = jnp.where(lane2 == m, turned, hi)
                lo = jnp.where(lane2 == (m + 1) % (nx // 2), turned, lo)
        at = slice(SUB * c, SUB * c + SUB)
        low_ref[at, :] = lo
        high_ref[at, :] = hi
        out1_ref[at, :], out2_ref[at, :] = order("gx", hi, lo)


def pack_rows(field, nz, ny, y_refs):
    for c in range(3):
        for k in range(nz):
            j = 2 * (c * nz + k)
            both = order("gy", field(c, k, slice(ny - 2, ny)), field(c, k, slice(0, 2)))
            for ref, rows in zip(y_refs, both):
                ref[j : j + 2, :] = rows


def pack_kernel(stress_ref, low_ref, high_ref, out1_ref, out2_ref, z1_ref, z2_ref, *y_refs):
    _, nz, ny, nx = stress_ref.shape
    of_x = (0, 3, 4)
    of_y = (3, 1, 5)
    z1_ref[...], z2_ref[...] = order("gz", stress_ref[:, nz - 2 : nz], stress_ref[:, 0:2])
    pack_sides(
        lambda c, k, t: stress_ref[of_x[c], k, SUB * t : SUB * t + SUB, :],
        nz, ny, nx, low_ref, high_ref, out1_ref, out2_ref,
    )
    pack_rows(lambda c, k, rows: stress_ref[of_y[c], k, rows, :], nz, ny, y_refs)


def y_send_kernel(slab_ref, *out_refs):
    ny = slab_ref.shape[0] - SUB
    both = order("gy", slab_ref[ny - 4 : ny, :], slab_ref[0:4, :])
    for ref, rows in zip(out_refs, both):
        ref[0:4, :] = rows
        ref[4:, :] = jnp.zeros_like(rows)


def x_send_kernel(n_gy, slab_ref, y1_ref, y2_ref, x1_ref, x2_ref, tall_ref, out1_ref, out2_ref):
    ny = slab_ref.shape[0] - SUB
    nx = slab_ref.shape[1]
    xs = x1_ref.shape[0]
    lane4 = lanes_of((SUB, nx)) // 4
    got = (y1_ref[0:4, :], y2_ref[0:4, :])
    tall_ref[: PAD - 4, :] = jnp.zeros((PAD - 4, nx), F32)
    tall_ref[PAD - 4 : PAD, :] = from_before("gy", got)
    tall_ref[PAD : PAD + ny, :] = slab_ref[:ny, :]
    tall_ref[PAD + ny : PAD + ny + 4, :] = from_after("gy", n_gy, got)
    tall_ref[PAD + ny + 4 :, :] = jnp.zeros((PAD - 4, nx), F32)
    lo = jnp.zeros((SUB, nx), F32)
    hi = jnp.zeros((SUB, nx), F32)
    for j in range((ny + 2 * PAD) // SUB):
        tile = tall_ref[SUB * j : SUB * j + SUB, :]
        lo = jnp.where(lane4 == j, pltpu.roll(tile, 4 * j, 1), lo)
        hi = jnp.where(lane4 == j, pltpu.roll(tile, (4 * j + 4) % nx, 1), hi)
    out1_ref[:xs, :] = x1_ref[...]
    out2_ref[:xs, :] = x2_ref[...]
    out1_ref[xs:, :], out2_ref[xs:, :] = order("gx", hi, lo)


def binomial(at):
    return (at(-2) + at(2) + 4.0 * (at(-1) + at(1)) + 6.0 * at(0)) / 16.0


def centred12(at):
    return 8.0 * (at(1) - at(-1)) - (at(2) - at(-2))


def metric_kernel(
    sizes, layers_ref, own, x1_ref, x2_ref, factor_ref, mz_ref, slope_ref, rim, sown,
):
    n_gx = sizes[0]
    gz = lax.axis_index("gz")
    nz, ny, nx = factor_ref.shape
    lane = lanes_of((SUB, nx))
    got = (x1_ref[...], x2_ref[...])
    left, right = from_before("gx", got), from_after("gx", n_gx, got)
    for j in range((ny + 2 * PAD) // SUB):
        rim[SUB * j : SUB * j + SUB, :] = jnp.where(
            lane < nx // 2,
            pltpu.roll(right, (nx - 4 * j) % nx, 1),
            pltpu.roll(left, nx - 4 - 4 * j, 1),
        )
    rows = ny + 4
    tall_own = binomial(lambda s: own[PAD - 2 + s : PAD - 2 + s + rows, :])
    tall_rim = binomial(lambda s: rim[PAD - 2 + s : PAD - 2 + s + rows, :])

    def shifted(a, b, s):
        ln = lanes_of(a.shape)
        cut = (ln < s) if s > 0 else (ln >= nx + s)
        if s > 0:
            mixed_a, mixed_b = jnp.where(cut, b, a), jnp.where(cut, a, b)
        elif s < 0:
            mixed_a, mixed_b = jnp.where(cut, b, a), jnp.where(cut, a, b)
        else:
            return a, b
        return pltpu.roll(mixed_a, (-s) % nx, 1), pltpu.roll(mixed_b, (-s) % nx, 1)

    def padded_rows(a):
        return jnp.concatenate([a, jnp.zeros((SUB - rows % SUB, nx), F32)], axis=0)

    tall_own, tall_rim = padded_rows(tall_own), padded_rows(tall_rim)
    pairs = {s: shifted(tall_own, tall_rim, s) for s in (-2, -1, 0, 1, 2)}
    surf_own = binomial(lambda s: pairs[s][0])
    surf_rim = binomial(lambda s: pairs[s][1])
    sown[...] = surf_own
    slope_ref[1] = centred12(lambda s: sown[2 + s : 2 + s + ny, :]) / 12.0
    pairs2 = {s: shifted(surf_own, surf_rim, s)[0] for s in (-2, -1, 1, 2)}
    along = centred12(lambda s: pairs2[s]) / 12.0
    surface = sown[2 : 2 + ny, :]
    sown[...] = along
    slope_ref[0] = sown[2 : 2 + ny, :]

    def above(slab, total):
        for k in range(nz):
            at = pl.ds(slab * nz + k, 1)
            s = layers_ref[1, at, :]
            total = total + (s * layers_ref[0, at, :]) * jnp.exp(s * surface)
        return total

    total = lax.fori_loop(0, gz, above, jnp.zeros((ny, nx), F32))
    for k in range(nz):
        at = pl.ds(gz * nz + k, 1)
        s = layers_ref[1, at, :]
        thickness = layers_ref[0, at, :] * jnp.exp(s * surface)
        weighted = s * thickness
        mz = 1.0 / thickness
        lift = total + 0.5 * weighted
        total = total + weighted
        mz_ref[k] = mz
        factor_ref[k] = (lift - 1.0) * mz

def edge_terms(got_left, got_right, low, high):
    dl = got_left - high
    dr = got_right - low
    nx = dl.shape[-1]
    lane = lanes_of(dl.shape)
    even = lane % 2 == 0
    dl = pltpu.roll(dl, 2, 1)
    dr = pltpu.roll(dr, nx - 2, 1)
    to_low = jnp.where(even, dl - 8.0 * pltpu.roll(dl, nx - 1, 1), dl)
    to_high = jnp.where(even, -dr, 8.0 * pltpu.roll(dr, 1, 1) - dr)
    second = (lane // 2) % 2 == 1
    return jnp.where(second, to_low, to_high), jnp.where(second, to_high, to_low)


def turned_left(edges, m):
    nx = edges.shape[-1]
    shift = (2 * nx - 2 - 2 * m) % nx if isinstance(m, int) else 2 * nx - 2 - 2 * m
    return pltpu.roll(edges, shift, 1)


def sides(lane):
    return (lane < 2) | (lane >= lane.shape[-1] - 2)


def x_weights(nx):
    ahead = (
        lax.broadcasted_iota(jnp.int32, (nx, nx), 0) - lax.broadcasted_iota(jnp.int32, (nx, nx), 1)
    )
    weights = jnp.zeros((nx, nx), F32)
    for offset, weight in ((1, 8.0), (-1, -8.0), (2, -1.0), (-2, 1.0)):
        weights = jnp.where((ahead == offset) | (ahead == offset + nx) | (ahead == offset - nx), weight, weights)
    weights = weights.astype(jnp.bfloat16)
    return jnp.concatenate([weights] * 3, axis=0)


def periodic_x(value, weights):
    high = value.astype(jnp.bfloat16)
    rest = value - high.astype(F32)
    middle = rest.astype(jnp.bfloat16)
    low = (rest - middle.astype(F32)).astype(jnp.bfloat16)
    return jnp.dot(
        jnp.concatenate([high, middle, low], axis=1), weights, preferred_element_type=F32
    )


def along_all(ref, comps, out_ref, group=16):
    _, nz, ny, nx = out_ref.shape
    group = next(d for d in range(group, 0, -1) if nz % d == 0)
    weights = x_weights(nx)

    @pl.loop(0, nz // group)
    def _(j):
        layers = pl.ds(j * group, group)
        rows = [ref[c, layers].reshape(group * ny, nx) for c in comps]
        result = periodic_x(jnp.concatenate(rows, axis=0), weights)
        for i in range(len(comps)):
            part = result[i * group * ny : (i + 1) * group * ny]
            out_ref[i, layers] = part.reshape(group, ny, nx)


def lookup(row, tile):
    table = jnp.broadcast_to(row, tile.shape)
    return jnp.take_along_axis(table, tile, axis=1, mode="promise_in_bounds")


def table_rows(refs, nx):
    n = refs[0].shape[1]
    return [jnp.concatenate([r, jnp.zeros((1, nx - n), F32)], axis=1) for r in refs]


def fill_edges(n_gx, edge_ref, x1_ref, x2_ref, low_ref, high_ref):
    for c in range(3):
        at = slice(SUB * c, SUB * c + SUB)
        got = (x1_ref[at, :], x2_ref[at, :])
        first, second = edge_terms(
            from_before("gx", got), from_after("gx", n_gx, got), low_ref[at, :], high_ref[at, :]
        )
        edge_ref[c, 0] = first
        edge_ref[c, 1] = second


def fill_rows(n_gy, tall, field, y1_ref, y2_ref, nz, ny, layers):
    for c in range(3):
        for spot, k in enumerate(layers):
            j = 2 * (c * nz + k)
            got = (y1_ref[j : j + 2, :], y2_ref[j : j + 2, :])
            tall[c, spot, PAD : PAD + ny, :] = field(c, k)
            tall[c, spot, PAD - 2 : PAD, :] = from_before("gy", got)
            tall[c, spot, PAD + ny : PAD + ny + 2, :] = from_after("gy", n_gy, got)


def depth_halos(n_gz, zb, za, z1_ref, z2_ref):
    got = (z1_ref[...], z2_ref[...])
    zb[...] = from_before("gz", got)
    za[...] = from_after("gz", n_gz, got)


def over(low, high, most, body):
    count = high - low
    group = next(d for d in range(most, 0, -1) if count % d == 0)

    @pl.loop(0, count // group)
    def _(j):
        for i in range(group):
            body(low + j * group + i)


def tile_rows(t):
    return slice(SUB * t, SUB * t + SUB)


def row_difference(tall, c, spot, t):
    return centred12(lambda s: tall[c, spot, PAD + SUB * t + s : PAD + SUB * t + s + SUB, :])


def inner_depth(ref, out_ref, comps, k, tiles):
    for t in range(tiles):
        for c in range(comps):
            out_ref[c, k - 2, tile_rows(t), :] = centred12(lambda s: ref[c, k + s, tile_rows(t), :])


def outer_depth(ref, zb, za, out_ref, comps, nz, tiles):
    for spot, k in enumerate((0, 1, nz - 2, nz - 1)):
        for t in range(tiles):
            for c in range(comps):

                def at(s):
                    if k + s < 0:
                        return zb[c, k + s + 2, tile_rows(t), :]
                    if k + s >= nz:
                        return za[c, k + s - nz, tile_rows(t), :]
                    return ref[c, k + s, tile_rows(t), :]

                out_ref[c, spot, tile_rows(t), :] = centred12(at)


def cell_kernel(
    layers_ref, material_ref, buoy_ref, lam_ref, mu_ref, relax_ref, weight_ref, cells_ref, spread_ref
):
    lane = lanes_of((SUB, layers_ref.shape[1]))
    sub = lax.broadcasted_iota(jnp.int32, lane.shape, 0)
    for i in range(2):
        row = jnp.broadcast_to(layers_ref[i : i + 1, :], lane.shape)
        for g in range(spread_ref.shape[1] // SUB):
            one = jnp.sum(jnp.where(lane == SUB * g + sub, row, 0.0), axis=1, keepdims=True)
            spread_ref[i, tile_rows(g), :] = jnp.broadcast_to(one, lane.shape)
    nz, ny, nx = material_ref.shape
    keep = jnp.exp(-step_size / relax_ref[...])
    tables = table_rows(
        [
            buoy_ref[...] * (step_size / 12.0), lam_ref[...] / 12.0, mu_ref[...] / 12.0, keep,
            (1.0 - keep) * weight_ref[...],
        ],
        nx,
    )

    def layer(k):
        for t in range(ny // SUB):
            kind = material_ref[k, tile_rows(t), :]
            for i, table in enumerate(tables):
                cells_ref[i, k, tile_rows(t), :] = lookup(table, kind)

    over(0, nz, 4, layer)


def depth_kernel(stress_ref, velocity_hbm, depth_ref, along_ref, velocity_ref, sem):
    load = pltpu.make_async_copy(velocity_hbm, velocity_ref, sem)
    load.start()
    _, nz, ny, _ = stress_ref.shape
    along_all(stress_ref, (0, 3, 4), along_ref)
    over(2, nz - 2, 4, lambda k: inner_depth(stress_ref, depth_ref, 6, k, ny // SUB))
    load.wait()


def plane_kernel(
    sizes, stress_ref, along_ref, y1_ref, y2_ref, z1_ref, z2_ref, plane_ref, outer_ref, tall, zb, za
):
    depth_halos(sizes[2], zb, za, z1_ref, z2_ref)
    outer_depth(stress_ref, zb, za, outer_ref, 6, stress_ref.shape[1], stress_ref.shape[2] // SUB)
    _, nz, ny, nx = stress_ref.shape
    tiles = ny // SUB
    of_y = (3, 1, 5)
    fill_rows(sizes[1], tall, lambda c, k: stress_ref[of_y[c], k], y1_ref, y2_ref, nz, ny, range(nz))

    def layer(k):
        for t in range(tiles):
            for c in range(3):
                plane_ref[c, k, tile_rows(t), :] = along_ref[
                    c, k, tile_rows(t), :
                ] + row_difference(tall, c, k, t)

    over(0, nz, 4, layer)


def velocity_kernel(
    sizes, velocity_ref, cells_ref, inner_ref, outer_ref, plane_ref, factor_ref, mz_ref, slope_ref,
    x1_ref, x2_ref, low_ref, high_ref, out_ref, vlow_ref, vhigh_ref, vx1_ref, vx2_ref, vz1_ref, vz2_ref,
    *rest,
):
    *vy_refs, edge = rest
    _, nz, ny, nx = velocity_ref.shape
    tiles = ny // SUB
    lane = lanes_of((SUB, nx))
    fill_edges(sizes[0], edge, x1_ref, x2_ref, low_ref, high_ref)

    def layer(k, depth_ref, spot):
        for t in range(tiles):
            rows = tile_rows(t)
            b = cells_ref[0, k, rows, :]
            factor = factor_ref[k, rows, :]
            mz = mz_ref[k, rows, :]
            mx = slope_ref[0, rows, :] * factor
            my = slope_ref[1, rows, :] * factor
            gk = [depth_ref[c, spot, rows, :] for c in range(6)]
            beside = [
                plane_ref[c, k, rows, :]
                + jnp.where(sides(lane), turned_left(edge[c, t % 2], k * tiles + t), 0.0)
                for c in range(3)
            ]
            accel = (
                beside[0] - mx * gk[0] - my * gk[3] + mz * gk[4],
                beside[1] - mx * gk[3] - my * gk[1] + mz * gk[5],
                beside[2] - mx * gk[4] - my * gk[5] + mz * gk[2],
            )
            for c in range(3):
                out_ref[c, k, rows, :] = velocity_ref[c, k, rows, :] + b * accel[c]

    for spot, k in enumerate((0, 1, nz - 2, nz - 1)):
        layer(k, outer_ref, spot)

    over(2, nz - 2, 4, lambda k: layer(k, inner_ref, k - 2))
    pack_sides(
        lambda c, k, t: out_ref[c, k, tile_rows(t), :], nz, ny, nx, vlow_ref, vhigh_ref, vx1_ref, vx2_ref
    )
    pack_rows(lambda c, k, rows: out_ref[c, k, rows, :], nz, ny, vy_refs)
    vz1_ref[...], vz2_ref[...] = order("gz", out_ref[:, nz - 2 : nz], out_ref[:, 0:2])


def velocity_inner_kernel(vel_ref, vel_hbm, depth_ref, along_ref, sem):
    store = pltpu.make_async_copy(vel_ref, vel_hbm, sem)
    store.start()
    _, nz, ny, nx = vel_ref.shape
    tiles = ny // SUB

    along_all(vel_ref, (0, 1, 2), along_ref)
    over(2, nz - 2, 4, lambda k: inner_depth(vel_ref, depth_ref, 3, k, tiles))
    store.wait()


def stress_kernel(
    sizes, vel_ref, stress_ref, memory_ref, cells_ref, inner_ref, along_ref, factor_ref, mz_ref, slope_ref,
    x1_ref, x2_ref, low_ref, high_ref, y1_ref, y2_ref, z1_ref, z2_ref,
    stress_hbm, memory_hbm, edge, tall, zb, za, outer, stress_out, memory_out, sems,
):
    n_gx, n_gy, n_gz = sizes
    _, nz, ny, nx = vel_ref.shape
    tiles = ny // SUB
    lane = lanes_of((SUB, nx))
    fill_edges(n_gx, edge, x1_ref, x2_ref, low_ref, high_ref)
    fill_rows(n_gy, tall, lambda c, k: vel_ref[c, k], y1_ref, y2_ref, nz, ny, range(nz))

    def layer(k, depth_ref, spot):
        for t in range(tiles):
            rows = tile_rows(t)
            factor = factor_ref[k, rows, :]
            mz = mz_ref[k, rows, :]
            mx = slope_ref[0, rows, :] * factor
            my = slope_ref[1, rows, :] * factor
            dk = [depth_ref[c, spot, rows, :] for c in range(3)]
            dx = [
                along_ref[c, k, rows, :]
                + jnp.where(sides(lane), turned_left(edge[c, t % 2], k * tiles + t), 0.0)
                - mx * dk[c]
                for c in range(3)
            ]
            dy = [row_difference(tall, c, k, t) - my * dk[c] for c in range(3)]
            dz = [mz * dk[c] for c in range(3)]
            lam, mu, keep, gain = (cells_ref[i, k, rows, :] for i in range(1, 5))
            volume = lam * (dx[0] + dy[1] + dz[2])
            mu2 = mu + mu
            rates = (
                volume + mu2 * dx[0],
                volume + mu2 * dy[1],
                volume + mu2 * dz[2],
                mu * (dy[0] + dx[1]),
                mu * (dz[0] + dx[2]),
                mu * (dz[1] + dy[2]),
            )
            for c in range(6):
                kept = keep * memory_ref[c, k, rows, :] + gain * rates[c]
                memory_out[c, k, rows, :] = kept
                stress_out[c, k, rows, :] = stress_ref[c, k, rows, :] + step_size * (
                    rates[c] - kept
                )

    def out_copies(first, count, spot):
        layers = pl.ds(first, count)
        return [
            pltpu.make_async_copy(a.at[:, layers], b.at[:, layers], sems.at[i, spot])
            for i, (a, b) in enumerate(((stress_out, stress_hbm), (memory_out, memory_hbm)))
        ]

    inner = nz - 4
    step = next(d for d in (4, 3, 2, 1) if inner % d == 0)
    chunks = inner // step

    @pl.loop(0, chunks)
    def _(j):
        for i in range(step):
            k = 2 + j * step + i
            layer(k, inner_ref, k - 2)

        for copy in out_copies(2 + j * step, step, 2 + j):
            copy.start()

    depth_halos(n_gz, zb, za, z1_ref, z2_ref)
    outer_depth(vel_ref, zb, za, outer, 3, nz, tiles)
    last = []
    for spot, k in enumerate((0, 1, nz - 2, nz - 1)):
        layer(k, outer, spot)
        if spot % 2 == 1:
            last += out_copies(k - 1, 2, spot // 2)
            for copy in last[-2:]:
                copy.start()

    @pl.loop(0, chunks)
    def _(j):
        for copy in out_copies(2 + j * step, step, 2 + j):
            copy.wait()

    for copy in last:
        copy.wait()


def in_hbm(value):
    return pltpu.with_memory_space_constraint(value, pltpu.HBM)


def call(kernel, outs, in_specs, scratch=(), name=None, out_specs=None, cost=0.0):
    return pl.pallas_call(
        kernel,
        out_shape=[jax.ShapeDtypeStruct(s, F32) for s in outs],
        in_specs=in_specs,
        out_specs=out_specs or [VM] * len(outs),
        scratch_shapes=list(scratch),
        compiler_params=params(),
        cost_estimate=pl.CostEstimate(flops=int(cost * 6e8), transcendentals=0, bytes_accessed=int(cost * 3.5e6)),
        name=name,
    )


def local(
    sizes, elevation, layer_base, stretch, material, buoyancy, lame_lambda, shear_modulus,
    relax_time, anelastic_weight, velocity, stress, memory,
):
    n_gx, n_gy, n_gz = counts = tuple(sizes[a] for a in ("gx", "gy", "gz"))
    _, nz, ny, nx = velocity.shape
    rows = ny + SUB
    slab = call(
        terrain_piece_kernel,
        [(rows, nx)],
        [HB] * 3,
        [
            pltpu.VMEM(elevation.shape, jnp.int32),
            pltpu.VMEM((1, nz), F32),
            pltpu.VMEM((1, nz), F32),
            DMA((3,)),
        ],
        name="terrain_piece", cost=0.8,
    )(in_hbm(elevation), in_hbm(layer_base[None]), in_hbm(stretch[None]))[0]
    tied = lax.optimization_barrier
    faces = 2 * 3 * nz
    xs = 3 * SUB
    y_rounds = min(2, n_gy - 1) if n_gy > 1 else 1
    z_face = (6, 2, ny, nx)
    slab, stress = tied((slab, stress))
    stress_vm = stress
    low, high, x1, x2, z1, z2, *ys = call(
        pack_kernel,
        [(xs, nx)] * 4 + [z_face] * 2 + [(faces, nx)] * y_rounds,
        [VM],
        name="pack_stress", cost=0.5,
    )(stress)
    if n_gz & (n_gz - 1):
        slab = lax.psum(slab, "gz")
    else:
        bit = 1
        rounds = pair_swaps(sizes, "gz")
        while bit < n_gz:
            if n_gz == 4:
                slab = slab + lax.ppermute(slab, tuple(sizes), rounds[bit - 1])
            else:
                slab = slab + lax.ppermute(slab, "gz", [(i, i ^ bit) for i in range(n_gz)])
            if bit == 1:
                slab, z1, z2 = tied((slab, z1, z2))
            bit *= 2
    z1, z2 = exchange(sizes, "gz", z1, z2)
    ts = call(y_send_kernel, [(SUB, nx)] * y_rounds, [VM], name="y_send", cost=0.02)(slab)
    ts, ys = tied((ts, ys))
    t1, t2 = exchange(sizes, "gy", ts[0], ts[-1])
    y1, y2 = exchange(sizes, "gy", ys[0], ys[-1])
    terrain, x1, x2 = call(
        functools.partial(x_send_kernel, n_gy),
        [(ny + 2 * PAD, nx)] + [(xs + SUB, nx)] * 2,
        [VM] * 5,
        name="x_send", cost=0.1,
    )(slab, t1, t2, x1, x2)
    x1, x2, material, stress_vm = tied((x1, x2, material, stress_vm))
    x1, x2 = exchange(sizes, "gx", x1, x2)
    edge = pltpu.VMEM((3, 2, SUB, nx), F32)
    tall = pltpu.VMEM((3, nz, ny + 2 * PAD, nx), F32)

    def depth(comps):
        return [pltpu.VMEM((comps, 2, ny, nx), F32)] * 2

    tables = (buoyancy, lame_lambda, shear_modulus, relax_time, anelastic_weight)
    all_layers = -(-n_gz * nz // SUB) * SUB
    cells, spread = call(
        cell_kernel, [(5, nz, ny, nx), (2, all_layers, nx)], [VM] * 7, name="cells", cost=0.8
    )(slab[ny:], material, *[table[None] for table in tables])
    inner_k, along, velocity_vm = call(
        depth_kernel,
        [(6, nz - 4, ny, nx), velocity.shape, velocity.shape],
        [VM, HB],
        [DMA],
        name="depth", cost=2.2,
    )(stress_vm, in_hbm(velocity))
    plane, outer_k = call(
        functools.partial(plane_kernel, counts),
        [velocity.shape, (6, 4, ny, nx)],
        [VM] * 6,
        [tall] + depth(6),
        name="planes", cost=0.6,
    )(stress_vm, along, y1, y2, z1, z2)
    plane, cells, x1, x2 = tied((plane, cells, x1, x2))
    factor, mz, slope = call(
        functools.partial(metric_kernel, counts),
        [(nz, ny, nx), (nz, ny, nx), (2, ny, nx)],
        [VM] * 4,
        [pltpu.VMEM((ny + 2 * PAD, nx), F32), pltpu.VMEM((ny + PAD, nx), F32)],
        name="metrics", cost=1.1,
    )(spread, terrain, x1[xs:], x2[xs:])
    vel, vlow, vhigh, vx1, vx2, vz1, vz2, *vys = call(
        functools.partial(velocity_kernel, counts),
        [velocity.shape] + [(xs, nx)] * 4 + [(3, 2, ny, nx)] * 2 + [(faces, nx)] * y_rounds,
        [VM] * 12,
        [edge],
        name="velocity", cost=1.5,
    )(velocity_vm, cells, inner_k, outer_k, plane, factor, mz, slope, x1, x2, low, high)
    vz1, vz2 = exchange(sizes, "gz", vz1, vz2)
    vy1, vy2 = exchange(sizes, "gy", vys[0], vys[-1])
    vx1, vx2 = exchange(sizes, "gx", vx1, vx2)
    vel_next, vel_k, vel_x = call(
        velocity_inner_kernel,
        [velocity.shape, (3, nz - 4, ny, nx), velocity.shape],
        [VM],
        [DMA],
        name="velocity_inner", cost=0.1,
        out_specs=[HB, VM, VM],
    )(vel)
    stress_next, memory_next = call(
        functools.partial(stress_kernel, counts),
        [stress.shape, stress.shape],
        [VM] * 17,
        [edge, tall] + depth(3)
        + [pltpu.VMEM((3, 4, ny, nx), F32), pltpu.VMEM(stress.shape, F32), pltpu.VMEM(stress.shape, F32)]
        + [DMA((2, nz))],
        name="stress", cost=2.8,
        out_specs=[HB] * 2,
    )(
        vel, stress_vm, memory, cells, vel_k, vel_x, factor, mz, slope, vx1, vx2, vlow, vhigh, vy1, vy2,
        vz1, vz2,
    )
    return vel_next, stress_next, memory_next


def solution(mesh):
    sizes = {a: mesh.shape[a] for a in ("gx", "gy", "gz")}
    field = P(None, "gz", "gy", "gx")
    return jax.shard_map(
        functools.partial(local, sizes),
        mesh=mesh,
        in_specs=(
            P("gy", ("gx", "gz")), P("gz"), P("gz"), P("gz", "gy", "gx"),
            P(), P(), P(), P(), P(), field, field, field,
        ),
        out_specs=(field, field, field),
        check_vma=False,
    )
```

```python
import functools
import jax
import jax.numpy as jnp
import numpy as np
from jax import lax
from jax.experimental import pallas as pl
from jax.experimental.pallas import tpu as pltpu
from jax.sharding import PartitionSpec as P

step_size = 0.3
SUB = 8
PAD = 8
F32 = jnp.float32
params = functools.partial(pltpu.CompilerParams, vmem_limit_bytes=20 * 1024 * 1024)
VM = pl.BlockSpec(memory_space=pltpu.VMEM)
SM = pl.BlockSpec(memory_space=pltpu.SMEM)
HB = pl.BlockSpec(memory_space=pltpu.HBM)
DMA = pltpu.SemaphoreType.DMA


def pair_swaps(sizes, axis):
    names = tuple(sizes)
    shape = tuple(sizes.values())
    index = names.index(axis)
    n = shape[index]
    others = [d for d in (2, 1, 0) if d != index and shape[d] % 2 == 0]
    rounds = []
    for first in (0, 1)[: max(0, min(2, n - 1))]:
        table = []
        for spot in np.ndindex(*shape):
            mate = spot[index] + 1 if spot[index] % 2 == first else spot[index] - 1
            target = list(spot)
            if 0 <= mate < n or axis == "gz":
                target[index] = mate % n
            elif others:
                target[others[0]] ^= 1
            else:
                continue
            table.append((int(np.ravel_multi_index(spot, shape)), int(np.ravel_multi_index(tuple(target), shape))))
        rounds.append(table)
    return rounds


def exchange(sizes, axis, first, second, second_first=False):
    rounds = list(zip((first, second), pair_swaps(sizes, axis)))
    if second_first:
        rounds = rounds[::-1]
    got = [lax.ppermute(v, tuple(sizes), r) for v, r in rounds]
    if second_first:
        got = got[::-1]
    return (got[0], got[-1]) if got else (first, second)


def even(axis):
    return lax.axis_index(axis) % 2 == 0


def from_before(axis, got):
    value = jnp.where(even(axis), got[1], got[0])
    return jnp.where(lax.axis_index(axis) > 0, value, 0.0)


def from_after(axis, n, got):
    value = jnp.where(even(axis), got[0], got[1])
    return jnp.where(lax.axis_index(axis) < n - 1, value, 0.0)


def order(axis, to_after, to_before):
    e = even(axis)
    return jnp.where(e, to_after, to_before), jnp.where(e, to_before, to_after)


def lanes_of(shape):
    return lax.broadcasted_iota(jnp.int32, shape, len(shape) - 1)


def terrain_piece_kernel(elev_hbm, base_hbm, stretch_hbm, out_ref, elev_ref, base_ref, stretch_ref, sems):
    mine = lax.axis_index("gz")
    pairs = ((elev_hbm, elev_ref), (base_hbm, base_ref), (stretch_hbm, stretch_ref))
    copies = [pltpu.make_async_copy(a, b, sems.at[i]) for i, (a, b) in enumerate(pairs)]
    for copy in copies:
        copy.start()
    for copy in copies:
        copy.wait()
    ny, width = elev_ref.shape
    nx = out_ref.shape[1]
    nz = base_ref.shape[1]
    height = elev_ref[...].astype(F32) / 200.0
    wide = jnp.concatenate([height, jnp.zeros((ny, nx - width), F32)], axis=1)
    out_ref[:ny, :] = pltpu.roll(wide, mine * width, 1)
    row = lax.broadcasted_iota(jnp.int32, (SUB, nx), 0)
    fill = jnp.zeros((1, nx - nz), F32)
    base = jnp.concatenate([base_ref[...], fill], axis=1)
    stretch = jnp.concatenate([stretch_ref[...], fill], axis=1)
    both = jnp.where(row == 0, base, jnp.where(row == 1, stretch, 0.0))
    out_ref[ny:, :] = pltpu.roll(both, mine * nz, 1)


def pack_sides(field, nz, ny, nx, low_ref, high_ref, out1_ref, out2_ref):
    tiles = ny // SUB
    lane2 = lanes_of((SUB, nx)) // 2
    for c in range(3):
        lo = jnp.zeros((SUB, nx), F32)
        hi = jnp.zeros((SUB, nx), F32)
        for k in range(nz):
            for t in range(tiles):
                m = k * tiles + t
                turned = pltpu.roll(field(c, k, t), (2 * m + 2) % nx, 1)
                hi = jnp.where(lane2 == m, turned, hi)
                lo = jnp.where(lane2 == (m + 1) % (nx // 2), turned, lo)
        at = slice(SUB * c, SUB * c + SUB)
        low_ref[at, :] = lo
        high_ref[at, :] = hi
        out1_ref[at, :], out2_ref[at, :] = order("gx", hi, lo)


def pack_rows(field, nz, ny, y_refs):
    for c in range(3):
        for k in range(nz):
            j = 2 * (c * nz + k)
            both = order("gy", field(c, k, slice(ny - 2, ny)), field(c, k, slice(0, 2)))
            for ref, rows in zip(y_refs, both):
                ref[j : j + 2, :] = rows


def pack_kernel(stress_ref, low_ref, high_ref, out1_ref, out2_ref, z1_ref, z2_ref, *y_refs):
    _, nz, ny, nx = stress_ref.shape
    of_x = (0, 3, 4)
    of_y = (3, 1, 5)
    z1_ref[...], z2_ref[...] = order("gz", stress_ref[:, nz - 2 : nz], stress_ref[:, 0:2])
    pack_sides(
        lambda c, k, t: stress_ref[of_x[c], k, SUB * t : SUB * t + SUB, :],
        nz, ny, nx, low_ref, high_ref, out1_ref, out2_ref,
    )
    pack_rows(lambda c, k, rows: stress_ref[of_y[c], k, rows, :], nz, ny, y_refs)


def y_send_kernel(slab_ref, *out_refs):
    ny = slab_ref.shape[0] - SUB
    both = order("gy", slab_ref[ny - 4 : ny, :], slab_ref[0:4, :])
    for ref, rows in zip(out_refs, both):
        ref[0:4, :] = rows
        ref[4:, :] = jnp.zeros_like(rows)


def x_send_kernel(n_gy, slab_ref, y1_ref, y2_ref, x1_ref, x2_ref, tall_ref, out1_ref, out2_ref):
    ny = slab_ref.shape[0] - SUB
    nx = slab_ref.shape[1]
    xs = x1_ref.shape[0]
    lane4 = lanes_of((SUB, nx)) // 4
    got = (y1_ref[0:4, :], y2_ref[0:4, :])
    tall_ref[: PAD - 4, :] = jnp.zeros((PAD - 4, nx), F32)
    tall_ref[PAD - 4 : PAD, :] = from_before("gy", got)
    tall_ref[PAD : PAD + ny, :] = slab_ref[:ny, :]
    tall_ref[PAD + ny : PAD + ny + 4, :] = from_after("gy", n_gy, got)
    tall_ref[PAD + ny + 4 :, :] = jnp.zeros((PAD - 4, nx), F32)
    lo = jnp.zeros((SUB, nx), F32)
    hi = jnp.zeros((SUB, nx), F32)
    for j in range((ny + 2 * PAD) // SUB):
        tile = tall_ref[SUB * j : SUB * j + SUB, :]
        lo = jnp.where(lane4 == j, pltpu.roll(tile, 4 * j, 1), lo)
        hi = jnp.where(lane4 == j, pltpu.roll(tile, (4 * j + 4) % nx, 1), hi)
    out1_ref[:xs, :] = x1_ref[...]
    out2_ref[:xs, :] = x2_ref[...]
    out1_ref[xs:, :], out2_ref[xs:, :] = order("gx", hi, lo)


def binomial(at):
    return (at(-2) + at(2) + 4.0 * (at(-1) + at(1)) + 6.0 * at(0)) / 16.0


def centred12(at):
    return 8.0 * (at(1) - at(-1)) - (at(2) - at(-2))


def metric_kernel(
    sizes, layers_ref, own, x1_ref, x2_ref, factor_ref, mz_ref, slope_ref, rim, sown,
):
    n_gx = sizes[0]
    gz = lax.axis_index("gz")
    nz, ny, nx = factor_ref.shape
    lane = lanes_of((SUB, nx))
    got = (x1_ref[...], x2_ref[...])
    left, right = from_before("gx", got), from_after("gx", n_gx, got)
    for j in range((ny + 2 * PAD) // SUB):
        rim[SUB * j : SUB * j + SUB, :] = jnp.where(
            lane < nx // 2,
            pltpu.roll(right, (nx - 4 * j) % nx, 1),
            pltpu.roll(left, nx - 4 - 4 * j, 1),
        )
    rows = ny + 4
    tall_own = binomial(lambda s: own[PAD - 2 + s : PAD - 2 + s + rows, :])
    tall_rim = binomial(lambda s: rim[PAD - 2 + s : PAD - 2 + s + rows, :])

    def shifted(a, b, s):
        ln = lanes_of(a.shape)
        cut = (ln < s) if s > 0 else (ln >= nx + s)
        if s > 0:
            mixed_a, mixed_b = jnp.where(cut, b, a), jnp.where(cut, a, b)
        elif s < 0:
            mixed_a, mixed_b = jnp.where(cut, b, a), jnp.where(cut, a, b)
        else:
            return a, b
        return pltpu.roll(mixed_a, (-s) % nx, 1), pltpu.roll(mixed_b, (-s) % nx, 1)

    def padded_rows(a):
        return jnp.concatenate([a, jnp.zeros((SUB - rows % SUB, nx), F32)], axis=0)

    tall_own, tall_rim = padded_rows(tall_own), padded_rows(tall_rim)
    pairs = {s: shifted(tall_own, tall_rim, s) for s in (-2, -1, 0, 1, 2)}
    surf_own = binomial(lambda s: pairs[s][0])
    surf_rim = binomial(lambda s: pairs[s][1])
    sown[...] = surf_own
    slope_ref[1] = centred12(lambda s: sown[2 + s : 2 + s + ny, :]) / 12.0
    pairs2 = {s: shifted(surf_own, surf_rim, s)[0] for s in (-2, -1, 1, 2)}
    along = centred12(lambda s: pairs2[s]) / 12.0
    surface = sown[2 : 2 + ny, :]
    sown[...] = along
    slope_ref[0] = sown[2 : 2 + ny, :]

    def above(slab, total):
        for k in range(nz):
            at = pl.ds(slab * nz + k, 1)
            s = layers_ref[1, at, :]
            total = total + (s * layers_ref[0, at, :]) * jnp.exp(s * surface)
        return total

    total = lax.fori_loop(0, gz, above, jnp.zeros((ny, nx), F32))
    for k in range(nz):
        at = pl.ds(gz * nz + k, 1)
        s = layers_ref[1, at, :]
        thickness = layers_ref[0, at, :] * jnp.exp(s * surface)
        weighted = s * thickness
        mz = 1.0 / thickness
        lift = total + 0.5 * weighted
        total = total + weighted
        mz_ref[k] = mz
        factor_ref[k] = (lift - 1.0) * mz

def edge_terms(got_left, got_right, low, high):
    dl = got_left - high
    dr = got_right - low
    nx = dl.shape[-1]
    lane = lanes_of(dl.shape)
    even = lane % 2 == 0
    dl = pltpu.roll(dl, 2, 1)
    dr = pltpu.roll(dr, nx - 2, 1)
    to_low = jnp.where(even, dl - 8.0 * pltpu.roll(dl, nx - 1, 1), dl)
    to_high = jnp.where(even, -dr, 8.0 * pltpu.roll(dr, 1, 1) - dr)
    second = (lane // 2) % 2 == 1
    return jnp.where(second, to_low, to_high), jnp.where(second, to_high, to_low)


def turned_left(edges, m):
    nx = edges.shape[-1]
    shift = (2 * nx - 2 - 2 * m) % nx if isinstance(m, int) else 2 * nx - 2 - 2 * m
    return pltpu.roll(edges, shift, 1)


def sides(lane):
    return (lane < 2) | (lane >= lane.shape[-1] - 2)


def x_weights(nx):
    ahead = (
        lax.broadcasted_iota(jnp.int32, (nx, nx), 0) - lax.broadcasted_iota(jnp.int32, (nx, nx), 1)
    )
    weights = jnp.zeros((nx, nx), F32)
    for offset, weight in ((1, 8.0), (-1, -8.0), (2, -1.0), (-2, 1.0)):
        weights = jnp.where((ahead == offset) | (ahead == offset + nx) | (ahead == offset - nx), weight, weights)
    weights = weights.astype(jnp.bfloat16)
    return jnp.concatenate([weights] * 3, axis=0)


def periodic_x(value, weights):
    high = value.astype(jnp.bfloat16)
    rest = value - high.astype(F32)
    middle = rest.astype(jnp.bfloat16)
    low = (rest - middle.astype(F32)).astype(jnp.bfloat16)
    return jnp.dot(
        jnp.concatenate([high, middle, low], axis=1), weights, preferred_element_type=F32
    )


def along_all(ref, comps, out_ref, group=16):
    _, nz, ny, nx = out_ref.shape
    group = next(d for d in range(group, 0, -1) if nz % d == 0)
    weights = x_weights(nx)

    @pl.loop(0, nz // group)
    def _(j):
        layers = pl.ds(j * group, group)
        rows = [ref[c, layers].reshape(group * ny, nx) for c in comps]
        result = periodic_x(jnp.concatenate(rows, axis=0), weights)
        for i in range(len(comps)):
            part = result[i * group * ny : (i + 1) * group * ny]
            out_ref[i, layers] = part.reshape(group, ny, nx)


def lookup(row, tile):
    table = jnp.broadcast_to(row, tile.shape)
    return jnp.take_along_axis(table, tile, axis=1, mode="promise_in_bounds")


def table_rows(refs, nx):
    n = refs[0].shape[1]
    return [jnp.concatenate([r, jnp.zeros((1, nx - n), F32)], axis=1) for r in refs]


def fill_edges(n_gx, edge_ref, x1_ref, x2_ref, low_ref, high_ref):
    for c in range(3):
        at = slice(SUB * c, SUB * c + SUB)
        got = (x1_ref[at, :], x2_ref[at, :])
        first, second = edge_terms(
            from_before("gx", got), from_after("gx", n_gx, got), low_ref[at, :], high_ref[at, :]
        )
        edge_ref[c, 0] = first
        edge_ref[c, 1] = second


def fill_rows(n_gy, tall, field, y1_ref, y2_ref, nz, ny, layers):
    for c in range(3):
        for spot, k in enumerate(layers):
            j = 2 * (c * nz + k)
            got = (y1_ref[j : j + 2, :], y2_ref[j : j + 2, :])
            tall[c, spot, PAD : PAD + ny, :] = field(c, k)
            tall[c, spot, PAD - 2 : PAD, :] = from_before("gy", got)
            tall[c, spot, PAD + ny : PAD + ny + 2, :] = from_after("gy", n_gy, got)


def depth_halos(n_gz, zb, za, z1_ref, z2_ref):
    got = (z1_ref[...], z2_ref[...])
    zb[...] = from_before("gz", got)
    za[...] = from_after("gz", n_gz, got)


def over(low, high, most, body):
    count = high - low
    group = next(d for d in range(most, 0, -1) if count % d == 0)

    @pl.loop(0, count // group)
    def _(j):
        for i in range(group):
            body(low + j * group + i)


def tile_rows(t):
    return slice(SUB * t, SUB * t + SUB)


def row_difference(tall, c, spot, t):
    return centred12(lambda s: tall[c, spot, PAD + SUB * t + s : PAD + SUB * t + s + SUB, :])


def inner_depth(ref, out_ref, comps, k, tiles):
    for t in range(tiles):
        for c in range(comps):
            out_ref[c, k - 2, tile_rows(t), :] = centred12(lambda s: ref[c, k + s, tile_rows(t), :])


def outer_depth(ref, zb, za, out_ref, comps, nz, tiles):
    for spot, k in enumerate((0, 1, nz - 2, nz - 1)):
        for t in range(tiles):
            for c in range(comps):

                def at(s):
                    if k + s < 0:
                        return zb[c, k + s + 2, tile_rows(t), :]
                    if k + s >= nz:
                        return za[c, k + s - nz, tile_rows(t), :]
                    return ref[c, k + s, tile_rows(t), :]

                out_ref[c, spot, tile_rows(t), :] = centred12(at)


def cell_kernel(
    layers_ref, material_ref, buoy_ref, lam_ref, mu_ref, relax_ref, weight_ref, cells_ref, spread_ref
):
    lane = lanes_of((SUB, layers_ref.shape[1]))
    sub = lax.broadcasted_iota(jnp.int32, lane.shape, 0)
    for i in range(2):
        row = jnp.broadcast_to(layers_ref[i : i + 1, :], lane.shape)
        for g in range(spread_ref.shape[1] // SUB):
            one = jnp.sum(jnp.where(lane == SUB * g + sub, row, 0.0), axis=1, keepdims=True)
            spread_ref[i, tile_rows(g), :] = jnp.broadcast_to(one, lane.shape)
    nz, ny, nx = material_ref.shape
    keep = jnp.exp(-step_size / relax_ref[...])
    tables = table_rows(
        [
            buoy_ref[...] * (step_size / 12.0), lam_ref[...] / 12.0, mu_ref[...] / 12.0, keep,
            (1.0 - keep) * weight_ref[...],
        ],
        nx,
    )

    def layer(k):
        for t in range(ny // SUB):
            kind = material_ref[k, tile_rows(t), :]
            for i, table in enumerate(tables):
                cells_ref[i, k, tile_rows(t), :] = lookup(table, kind)

    over(0, nz, 4, layer)


def depth_kernel(stress_ref, velocity_hbm, depth_ref, along_ref, velocity_ref, sem):
    load = pltpu.make_async_copy(velocity_hbm, velocity_ref, sem)
    load.start()
    _, nz, ny, _ = stress_ref.shape
    along_all(stress_ref, (0, 3, 4), along_ref)
    over(2, nz - 2, 4, lambda k: inner_depth(stress_ref, depth_ref, 6, k, ny // SUB))
    load.wait()


def plane_kernel(
    sizes, stress_ref, along_ref, y1_ref, y2_ref, z1_ref, z2_ref, plane_ref, outer_ref, tall, zb, za
):
    depth_halos(sizes[2], zb, za, z1_ref, z2_ref)
    outer_depth(stress_ref, zb, za, outer_ref, 6, stress_ref.shape[1], stress_ref.shape[2] // SUB)
    _, nz, ny, nx = stress_ref.shape
    tiles = ny // SUB
    of_y = (3, 1, 5)
    fill_rows(sizes[1], tall, lambda c, k: stress_ref[of_y[c], k], y1_ref, y2_ref, nz, ny, range(nz))

    def layer(k):
        for t in range(tiles):
            for c in range(3):
                plane_ref[c, k, tile_rows(t), :] = along_ref[
                    c, k, tile_rows(t), :
                ] + row_difference(tall, c, k, t)

    over(0, nz, 4, layer)


def velocity_kernel(
    sizes, velocity_ref, cells_ref, inner_ref, outer_ref, plane_ref, factor_ref, mz_ref, slope_ref,
    x1_ref, x2_ref, low_ref, high_ref, out_ref, vlow_ref, vhigh_ref, vx1_ref, vx2_ref, vz1_ref, vz2_ref,
    *rest,
):
    *vy_refs, edge = rest
    _, nz, ny, nx = velocity_ref.shape
    tiles = ny // SUB
    lane = lanes_of((SUB, nx))
    fill_edges(sizes[0], edge, x1_ref, x2_ref, low_ref, high_ref)

    def layer(k, depth_ref, spot):
        for t in range(tiles):
            rows = tile_rows(t)
            b = cells_ref[0, k, rows, :]
            factor = factor_ref[k, rows, :]
            mz = mz_ref[k, rows, :]
            mx = slope_ref[0, rows, :] * factor
            my = slope_ref[1, rows, :] * factor
            gk = [depth_ref[c, spot, rows, :] for c in range(6)]
            beside = [
                plane_ref[c, k, rows, :]
                + jnp.where(sides(lane), turned_left(edge[c, t % 2], k * tiles + t), 0.0)
                for c in range(3)
            ]
            accel = (
                beside[0] - mx * gk[0] - my * gk[3] + mz * gk[4],
                beside[1] - mx * gk[3] - my * gk[1] + mz * gk[5],
                beside[2] - mx * gk[4] - my * gk[5] + mz * gk[2],
            )
            for c in range(3):
                out_ref[c, k, rows, :] = velocity_ref[c, k, rows, :] + b * accel[c]

    for spot, k in enumerate((0, 1, nz - 2, nz - 1)):
        layer(k, outer_ref, spot)

    over(2, nz - 2, 4, lambda k: layer(k, inner_ref, k - 2))
    pack_sides(
        lambda c, k, t: out_ref[c, k, tile_rows(t), :], nz, ny, nx, vlow_ref, vhigh_ref, vx1_ref, vx2_ref
    )
    pack_rows(lambda c, k, rows: out_ref[c, k, rows, :], nz, ny, vy_refs)
    vz1_ref[...], vz2_ref[...] = order("gz", out_ref[:, nz - 2 : nz], out_ref[:, 0:2])


def velocity_inner_kernel(vel_ref, vel_hbm, depth_ref, along_ref, sem):
    store = pltpu.make_async_copy(vel_ref, vel_hbm, sem)
    store.start()
    _, nz, ny, nx = vel_ref.shape
    tiles = ny // SUB

    along_all(vel_ref, (0, 1, 2), along_ref)
    over(2, nz - 2, 4, lambda k: inner_depth(vel_ref, depth_ref, 3, k, tiles))
    store.wait()


def stress_kernel(
    sizes, vel_ref, stress_ref, memory_ref, cells_ref, inner_ref, along_ref, factor_ref, mz_ref, slope_ref,
    x1_ref, x2_ref, low_ref, high_ref, y1_ref, y2_ref, z1_ref, z2_ref,
    stress_hbm, memory_hbm, edge, tall, zb, za, outer, stress_out, memory_out, sems,
):
    n_gx, n_gy, n_gz = sizes
    _, nz, ny, nx = vel_ref.shape
    tiles = ny // SUB
    lane = lanes_of((SUB, nx))
    fill_edges(n_gx, edge, x1_ref, x2_ref, low_ref, high_ref)
    fill_rows(n_gy, tall, lambda c, k: vel_ref[c, k], y1_ref, y2_ref, nz, ny, range(nz))

    def layer(k, depth_ref, spot):
        for t in range(tiles):
            rows = tile_rows(t)
            factor = factor_ref[k, rows, :]
            mz = mz_ref[k, rows, :]
            mx = slope_ref[0, rows, :] * factor
            my = slope_ref[1, rows, :] * factor
            dk = [depth_ref[c, spot, rows, :] for c in range(3)]
            dx = [
                along_ref[c, k, rows, :]
                + jnp.where(sides(lane), turned_left(edge[c, t % 2], k * tiles + t), 0.0)
                - mx * dk[c]
                for c in range(3)
            ]
            dy = [row_difference(tall, c, k, t) - my * dk[c] for c in range(3)]
            dz = [mz * dk[c] for c in range(3)]
            lam, mu, keep, gain = (cells_ref[i, k, rows, :] for i in range(1, 5))
            volume = lam * (dx[0] + dy[1] + dz[2])
            mu2 = mu + mu
            rates = (
                volume + mu2 * dx[0],
                volume + mu2 * dy[1],
                volume + mu2 * dz[2],
                mu * (dy[0] + dx[1]),
                mu * (dz[0] + dx[2]),
                mu * (dz[1] + dy[2]),
            )
            for c in range(6):
                kept = keep * memory_ref[c, k, rows, :] + gain * rates[c]
                memory_out[c, k, rows, :] = kept
                stress_out[c, k, rows, :] = stress_ref[c, k, rows, :] + step_size * (
                    rates[c] - kept
                )

    def out_copies(first, count, spot):
        layers = pl.ds(first, count)
        return [
            pltpu.make_async_copy(a.at[:, layers], b.at[:, layers], sems.at[i, spot])
            for i, (a, b) in enumerate(((stress_out, stress_hbm), (memory_out, memory_hbm)))
        ]

    inner = nz - 4
    step = next(d for d in (4, 3, 2, 1) if inner % d == 0)
    chunks = inner // step

    @pl.loop(0, chunks)
    def _(j):
        for i in range(step):
            k = 2 + j * step + i
            layer(k, inner_ref, k - 2)

        for copy in out_copies(2 + j * step, step, 2 + j):
            copy.start()

    depth_halos(n_gz, zb, za, z1_ref, z2_ref)
    outer_depth(vel_ref, zb, za, outer, 3, nz, tiles)
    last = []
    for spot, k in enumerate((0, 1, nz - 2, nz - 1)):
        layer(k, outer, spot)
        if spot % 2 == 1:
            last += out_copies(k - 1, 2, spot // 2)
            for copy in last[-2:]:
                copy.start()

    @pl.loop(0, chunks)
    def _(j):
        for copy in out_copies(2 + j * step, step, 2 + j):
            copy.wait()

    for copy in last:
        copy.wait()


def in_hbm(value):
    return pltpu.with_memory_space_constraint(value, pltpu.HBM)


def call(kernel, outs, in_specs, scratch=(), name=None, out_specs=None, cost=0.0):
    return pl.pallas_call(
        kernel,
        out_shape=[jax.ShapeDtypeStruct(s, F32) for s in outs],
        in_specs=in_specs,
        out_specs=out_specs or [VM] * len(outs),
        scratch_shapes=list(scratch),
        compiler_params=params(),
        cost_estimate=pl.CostEstimate(flops=int(cost * 6e8), transcendentals=0, bytes_accessed=int(cost * 3.5e6)),
        name=name,
    )


def local(
    sizes, elevation, layer_base, stretch, material, buoyancy, lame_lambda, shear_modulus,
    relax_time, anelastic_weight, velocity, stress, memory,
):
    n_gx, n_gy, n_gz = counts = tuple(sizes[a] for a in ("gx", "gy", "gz"))
    _, nz, ny, nx = velocity.shape
    rows = ny + SUB
    slab = call(
        terrain_piece_kernel,
        [(rows, nx)],
        [HB] * 3,
        [
            pltpu.VMEM(elevation.shape, jnp.int32),
            pltpu.VMEM((1, nz), F32),
            pltpu.VMEM((1, nz), F32),
            DMA((3,)),
        ],
        name="terrain_piece", cost=0.8,
    )(in_hbm(elevation), in_hbm(layer_base[None]), in_hbm(stretch[None]))[0]
    tied = lax.optimization_barrier
    faces = 2 * 3 * nz
    xs = 3 * SUB
    y_rounds = min(2, n_gy - 1) if n_gy > 1 else 1
    z_face = (6, 2, ny, nx)
    slab, stress = tied((slab, stress))
    stress_vm = stress
    low, high, x1, x2, z1, z2, *ys = call(
        pack_kernel,
        [(xs, nx)] * 4 + [z_face] * 2 + [(faces, nx)] * y_rounds,
        [VM],
        name="pack_stress", cost=0.5,
    )(stress)
    if n_gz & (n_gz - 1):
        slab = lax.psum(slab, "gz")
    else:
        bit = 1
        rounds = pair_swaps(sizes, "gz")
        while bit < n_gz:
            if n_gz == 4:
                slab = slab + lax.ppermute(slab, tuple(sizes), rounds[bit - 1])
            else:
                slab = slab + lax.ppermute(slab, "gz", [(i, i ^ bit) for i in range(n_gz)])
            if bit == 1:
                slab, z1, z2 = tied((slab, z1, z2))
            bit *= 2
    z1, z2 = exchange(sizes, "gz", z1, z2)
    ts = call(y_send_kernel, [(SUB, nx)] * y_rounds, [VM], name="y_send", cost=0.02)(slab)
    ts, ys, stress_vm = tied((ts, ys, stress_vm))
    t1, t2 = exchange(sizes, "gy", ts[0], ts[-1])
    y1, y2 = exchange(sizes, "gy", ys[0], ys[-1])
    inner_k, along, velocity_vm = call(
        depth_kernel,
        [(6, nz - 4, ny, nx), velocity.shape, velocity.shape],
        [VM, HB],
        [DMA],
        name="depth", cost=2.2,
    )(stress_vm, in_hbm(velocity))
    x1, x2, inner_k = tied((x1, x2, inner_k))
    terrain, x1, x2 = call(
        functools.partial(x_send_kernel, n_gy),
        [(ny + 2 * PAD, nx)] + [(xs + SUB, nx)] * 2,
        [VM] * 5,
        name="x_send", cost=0.1,
    )(slab, t1, t2, x1, x2)
    x1, x2, material = tied((x1, x2, material))
    x1, x2 = exchange(sizes, "gx", x1, x2, True)
    edge = pltpu.VMEM((3, 2, SUB, nx), F32)
    tall = pltpu.VMEM((3, nz, ny + 2 * PAD, nx), F32)

    def depth(comps):
        return [pltpu.VMEM((comps, 2, ny, nx), F32)] * 2

    tables = (buoyancy, lame_lambda, shear_modulus, relax_time, anelastic_weight)
    all_layers = -(-n_gz * nz // SUB) * SUB
    cells, spread = call(
        cell_kernel, [(5, nz, ny, nx), (2, all_layers, nx)], [VM] * 7, name="cells", cost=0.8
    )(slab[ny:], material, *[table[None] for table in tables])
    plane, outer_k = call(
        functools.partial(plane_kernel, counts),
        [velocity.shape, (6, 4, ny, nx)],
        [VM] * 6,
        [tall] + depth(6),
        name="planes", cost=0.6,
    )(stress_vm, along, y1, y2, z1, z2)
    plane, cells, x1, x2 = tied((plane, cells, x1, x2))
    factor, mz, slope = call(
        functools.partial(metric_kernel, counts),
        [(nz, ny, nx), (nz, ny, nx), (2, ny, nx)],
        [VM] * 4,
        [pltpu.VMEM((ny + 2 * PAD, nx), F32), pltpu.VMEM((ny + PAD, nx), F32)],
        name="metrics", cost=1.1,
    )(spread, terrain, x1[xs:], x2[xs:])
    vel, vlow, vhigh, vx1, vx2, vz1, vz2, *vys = call(
        functools.partial(velocity_kernel, counts),
        [velocity.shape] + [(xs, nx)] * 4 + [(3, 2, ny, nx)] * 2 + [(faces, nx)] * y_rounds,
        [VM] * 12,
        [edge],
        name="velocity", cost=1.5,
    )(velocity_vm, cells, inner_k, outer_k, plane, factor, mz, slope, x1, x2, low, high)
    vz1, vz2 = exchange(sizes, "gz", vz1, vz2)
    vy1, vy2 = exchange(sizes, "gy", vys[0], vys[-1])
    vx1, vx2 = exchange(sizes, "gx", vx1, vx2)
    vel_next, vel_k, vel_x = call(
        velocity_inner_kernel,
        [velocity.shape, (3, nz - 4, ny, nx), velocity.shape],
        [VM],
        [DMA],
        name="velocity_inner", cost=0.1,
        out_specs=[HB, VM, VM],
    )(vel)
    stress_next, memory_next = call(
        functools.partial(stress_kernel, counts),
        [stress.shape, stress.shape],
        [VM] * 17,
        [edge, tall] + depth(3)
        + [pltpu.VMEM((3, 4, ny, nx), F32), pltpu.VMEM(stress.shape, F32), pltpu.VMEM(stress.shape, F32)]
        + [DMA((2, nz))],
        name="stress", cost=2.8,
        out_specs=[HB] * 2,
    )(
        vel, stress_vm, memory, cells, vel_k, vel_x, factor, mz, slope, vx1, vx2, vlow, vhigh, vy1, vy2,
        vz1, vz2,
    )
    return vel_next, stress_next, memory_next


def solution(mesh):
    sizes = {a: mesh.shape[a] for a in ("gx", "gy", "gz")}
    field = P(None, "gz", "gy", "gx")
    return jax.shard_map(
        functools.partial(local, sizes),
        mesh=mesh,
        in_specs=(
            P("gy", ("gx", "gz")), P("gz"), P("gz"), P("gz", "gy", "gx"),
            P(), P(), P(), P(), P(), field, field, field,
        ),
        out_specs=(field, field, field),
        check_vma=False,
    )
```

```python
import functools
import jax
import jax.numpy as jnp
import numpy as np
from jax import lax
from jax.experimental import pallas as pl
from jax.experimental.pallas import tpu as pltpu
from jax.sharding import PartitionSpec as P

step_size = 0.3
SUB = 8
PAD = 8
F32 = jnp.float32
params = functools.partial(pltpu.CompilerParams, vmem_limit_bytes=20 * 1024 * 1024)
VM = pl.BlockSpec(memory_space=pltpu.VMEM)
SM = pl.BlockSpec(memory_space=pltpu.SMEM)
HB = pl.BlockSpec(memory_space=pltpu.HBM)
DMA = pltpu.SemaphoreType.DMA


def pair_swaps(sizes, axis):
    names = tuple(sizes)
    shape = tuple(sizes.values())
    index = names.index(axis)
    n = shape[index]
    others = [d for d in (2, 1, 0) if d != index and shape[d] % 2 == 0]
    rounds = []
    for first in (0, 1)[: max(0, min(2, n - 1))]:
        table = []
        for spot in np.ndindex(*shape):
            mate = spot[index] + 1 if spot[index] % 2 == first else spot[index] - 1
            target = list(spot)
            if 0 <= mate < n or axis == "gz":
                target[index] = mate % n
            elif others:
                target[others[0]] ^= 1
            else:
                continue
            table.append((int(np.ravel_multi_index(spot, shape)), int(np.ravel_multi_index(tuple(target), shape))))
        rounds.append(table)
    return rounds


def exchange(sizes, axis, first, second, second_first=False):
    rounds = list(zip((first, second), pair_swaps(sizes, axis)))
    if second_first:
        rounds = rounds[::-1]
    got = [lax.ppermute(v, tuple(sizes), r) for v, r in rounds]
    if second_first:
        got = got[::-1]
    return (got[0], got[-1]) if got else (first, second)


def even(axis):
    return lax.axis_index(axis) % 2 == 0


def from_before(axis, got):
    value = jnp.where(even(axis), got[1], got[0])
    return jnp.where(lax.axis_index(axis) > 0, value, 0.0)


def from_after(axis, n, got):
    value = jnp.where(even(axis), got[0], got[1])
    return jnp.where(lax.axis_index(axis) < n - 1, value, 0.0)


def order(axis, to_after, to_before):
    e = even(axis)
    return jnp.where(e, to_after, to_before), jnp.where(e, to_before, to_after)


def lanes_of(shape):
    return lax.broadcasted_iota(jnp.int32, shape, len(shape) - 1)


def terrain_piece_kernel(elev_hbm, base_hbm, stretch_hbm, out_ref, elev_ref, base_ref, stretch_ref, sems):
    mine = lax.axis_index("gz")
    pairs = ((elev_hbm, elev_ref), (base_hbm, base_ref), (stretch_hbm, stretch_ref))
    copies = [pltpu.make_async_copy(a, b, sems.at[i]) for i, (a, b) in enumerate(pairs)]
    for copy in copies:
        copy.start()
    for copy in copies:
        copy.wait()
    ny, width = elev_ref.shape
    nx = out_ref.shape[1]
    nz = base_ref.shape[1]
    height = elev_ref[...].astype(F32) / 200.0
    wide = jnp.concatenate([height, jnp.zeros((ny, nx - width), F32)], axis=1)
    out_ref[:ny, :] = pltpu.roll(wide, mine * width, 1)
    row = lax.broadcasted_iota(jnp.int32, (SUB, nx), 0)
    fill = jnp.zeros((1, nx - nz), F32)
    base = jnp.concatenate([base_ref[...], fill], axis=1)
    stretch = jnp.concatenate([stretch_ref[...], fill], axis=1)
    both = jnp.where(row == 0, base, jnp.where(row == 1, stretch, 0.0))
    out_ref[ny:, :] = pltpu.roll(both, mine * nz, 1)


def merge_kernel(first_ref, elev_ref, out_ref):
    ny, width = elev_ref.shape
    nx = out_ref.shape[1]
    height = elev_ref[...].astype(F32) / 200.0
    wide = jnp.concatenate([height, jnp.zeros((ny, nx - width), F32)], axis=1)
    mate = lax.axis_index("gz") + jnp.where(even("gz"), 1, -1)
    out_ref[:ny, :] = first_ref[:ny, :] + pltpu.roll(wide, mate * width, 1)
    out_ref[ny:, :] = first_ref[ny:, :]


def pack_sides(field, nz, ny, nx, low_ref, high_ref, out1_ref, out2_ref):
    tiles = ny // SUB
    lane2 = lanes_of((SUB, nx)) // 2
    for c in range(3):
        lo = jnp.zeros((SUB, nx), F32)
        hi = jnp.zeros((SUB, nx), F32)
        for k in range(nz):
            for t in range(tiles):
                m = k * tiles + t
                turned = pltpu.roll(field(c, k, t), (2 * m + 2) % nx, 1)
                hi = jnp.where(lane2 == m, turned, hi)
                lo = jnp.where(lane2 == (m + 1) % (nx // 2), turned, lo)
        at = slice(SUB * c, SUB * c + SUB)
        low_ref[at, :] = lo
        high_ref[at, :] = hi
        out1_ref[at, :], out2_ref[at, :] = order("gx", hi, lo)


def pack_rows(field, nz, ny, y_refs):
    for c in range(3):
        for k in range(nz):
            j = 2 * (c * nz + k)
            both = order("gy", field(c, k, slice(ny - 2, ny)), field(c, k, slice(0, 2)))
            for ref, rows in zip(y_refs, both):
                ref[j : j + 2, :] = rows


def pack_kernel(stress_ref, low_ref, high_ref, out1_ref, out2_ref, z1_ref, z2_ref, *y_refs):
    _, nz, ny, nx = stress_ref.shape
    of_x = (0, 3, 4)
    of_y = (3, 1, 5)
    z1_ref[...], z2_ref[...] = order("gz", stress_ref[:, nz - 2 : nz], stress_ref[:, 0:2])
    pack_sides(
        lambda c, k, t: stress_ref[of_x[c], k, SUB * t : SUB * t + SUB, :],
        nz, ny, nx, low_ref, high_ref, out1_ref, out2_ref,
    )
    pack_rows(lambda c, k, rows: stress_ref[of_y[c], k, rows, :], nz, ny, y_refs)


def y_send_kernel(slab_ref, *out_refs):
    ny = slab_ref.shape[0] - SUB
    both = order("gy", slab_ref[ny - 4 : ny, :], slab_ref[0:4, :])
    for ref, rows in zip(out_refs, both):
        ref[0:4, :] = rows
        ref[4:, :] = jnp.zeros_like(rows)


def x_send_kernel(n_gy, slab_ref, y1_ref, y2_ref, x1_ref, x2_ref, tall_ref, out1_ref, out2_ref):
    ny = slab_ref.shape[0] - SUB
    nx = slab_ref.shape[1]
    xs = x1_ref.shape[0]
    lane4 = lanes_of((SUB, nx)) // 4
    got = (y1_ref[0:4, :], y2_ref[0:4, :])
    tall_ref[: PAD - 4, :] = jnp.zeros((PAD - 4, nx), F32)
    tall_ref[PAD - 4 : PAD, :] = from_before("gy", got)
    tall_ref[PAD : PAD + ny, :] = slab_ref[:ny, :]
    tall_ref[PAD + ny : PAD + ny + 4, :] = from_after("gy", n_gy, got)
    tall_ref[PAD + ny + 4 :, :] = jnp.zeros((PAD - 4, nx), F32)
    lo = jnp.zeros((SUB, nx), F32)
    hi = jnp.zeros((SUB, nx), F32)
    for j in range((ny + 2 * PAD) // SUB):
        tile = tall_ref[SUB * j : SUB * j + SUB, :]
        lo = jnp.where(lane4 == j, pltpu.roll(tile, 4 * j, 1), lo)
        hi = jnp.where(lane4 == j, pltpu.roll(tile, (4 * j + 4) % nx, 1), hi)
    out1_ref[:xs, :] = x1_ref[...]
    out2_ref[:xs, :] = x2_ref[...]
    out1_ref[xs:, :], out2_ref[xs:, :] = order("gx", hi, lo)


def binomial(at):
    return (at(-2) + at(2) + 4.0 * (at(-1) + at(1)) + 6.0 * at(0)) / 16.0


def centred12(at):
    return 8.0 * (at(1) - at(-1)) - (at(2) - at(-2))


def metric_kernel(
    sizes, layers_ref, own, x1_ref, x2_ref, factor_ref, mz_ref, slope_ref, rim, sown,
):
    n_gx = sizes[0]
    gz = lax.axis_index("gz")
    nz, ny, nx = factor_ref.shape
    lane = lanes_of((SUB, nx))
    got = (x1_ref[...], x2_ref[...])
    left, right = from_before("gx", got), from_after("gx", n_gx, got)
    for j in range((ny + 2 * PAD) // SUB):
        rim[SUB * j : SUB * j + SUB, :] = jnp.where(
            lane < nx // 2,
            pltpu.roll(right, (nx - 4 * j) % nx, 1),
            pltpu.roll(left, nx - 4 - 4 * j, 1),
        )
    rows = ny + 4
    tall_own = binomial(lambda s: own[PAD - 2 + s : PAD - 2 + s + rows, :])
    tall_rim = binomial(lambda s: rim[PAD - 2 + s : PAD - 2 + s + rows, :])

    def shifted(a, b, s):
        ln = lanes_of(a.shape)
        cut = (ln < s) if s > 0 else (ln >= nx + s)
        if s > 0:
            mixed_a, mixed_b = jnp.where(cut, b, a), jnp.where(cut, a, b)
        elif s < 0:
            mixed_a, mixed_b = jnp.where(cut, b, a), jnp.where(cut, a, b)
        else:
            return a, b
        return pltpu.roll(mixed_a, (-s) % nx, 1), pltpu.roll(mixed_b, (-s) % nx, 1)

    def padded_rows(a):
        return jnp.concatenate([a, jnp.zeros((SUB - rows % SUB, nx), F32)], axis=0)

    tall_own, tall_rim = padded_rows(tall_own), padded_rows(tall_rim)
    pairs = {s: shifted(tall_own, tall_rim, s) for s in (-2, -1, 0, 1, 2)}
    surf_own = binomial(lambda s: pairs[s][0])
    surf_rim = binomial(lambda s: pairs[s][1])
    sown[...] = surf_own
    slope_ref[1] = centred12(lambda s: sown[2 + s : 2 + s + ny, :]) / 12.0
    pairs2 = {s: shifted(surf_own, surf_rim, s)[0] for s in (-2, -1, 1, 2)}
    along = centred12(lambda s: pairs2[s]) / 12.0
    surface = sown[2 : 2 + ny, :]
    sown[...] = along
    slope_ref[0] = sown[2 : 2 + ny, :]

    def above(slab, total):
        for k in range(nz):
            at = pl.ds(slab * nz + k, 1)
            s = layers_ref[1, at, :]
            total = total + (s * layers_ref[0, at, :]) * jnp.exp(s * surface)
        return total

    total = lax.fori_loop(0, gz, above, jnp.zeros((ny, nx), F32))
    for k in range(nz):
        at = pl.ds(gz * nz + k, 1)
        s = layers_ref[1, at, :]
        thickness = layers_ref[0, at, :] * jnp.exp(s * surface)
        weighted = s * thickness
        mz = 1.0 / thickness
        lift = total + 0.5 * weighted
        total = total + weighted
        mz_ref[k] = mz
        factor_ref[k] = (lift - 1.0) * mz

def edge_terms(got_left, got_right, low, high):
    dl = got_left - high
    dr = got_right - low
    nx = dl.shape[-1]
    lane = lanes_of(dl.shape)
    even = lane % 2 == 0
    dl = pltpu.roll(dl, 2, 1)
    dr = pltpu.roll(dr, nx - 2, 1)
    to_low = jnp.where(even, dl - 8.0 * pltpu.roll(dl, nx - 1, 1), dl)
    to_high = jnp.where(even, -dr, 8.0 * pltpu.roll(dr, 1, 1) - dr)
    second = (lane // 2) % 2 == 1
    return jnp.where(second, to_low, to_high), jnp.where(second, to_high, to_low)


def turned_left(edges, m):
    nx = edges.shape[-1]
    shift = (2 * nx - 2 - 2 * m) % nx if isinstance(m, int) else 2 * nx - 2 - 2 * m
    return pltpu.roll(edges, shift, 1)


def sides(lane):
    return (lane < 2) | (lane >= lane.shape[-1] - 2)


def x_weights(nx):
    ahead = (
        lax.broadcasted_iota(jnp.int32, (nx, nx), 0) - lax.broadcasted_iota(jnp.int32, (nx, nx), 1)
    )
    weights = jnp.zeros((nx, nx), F32)
    for offset, weight in ((1, 8.0), (-1, -8.0), (2, -1.0), (-2, 1.0)):
        weights = jnp.where((ahead == offset) | (ahead == offset + nx) | (ahead == offset - nx), weight, weights)
    weights = weights.astype(jnp.bfloat16)
    return jnp.concatenate([weights] * 3, axis=0)


def periodic_x(value, weights):
    high = value.astype(jnp.bfloat16)
    rest = value - high.astype(F32)
    middle = rest.astype(jnp.bfloat16)
    low = (rest - middle.astype(F32)).astype(jnp.bfloat16)
    return jnp.dot(
        jnp.concatenate([high, middle, low], axis=1), weights, preferred_element_type=F32
    )


def along_all(ref, comps, out_ref, group=16):
    _, nz, ny, nx = out_ref.shape
    group = next(d for d in range(group, 0, -1) if nz % d == 0)
    weights = x_weights(nx)

    @pl.loop(0, nz // group)
    def _(j):
        layers = pl.ds(j * group, group)
        rows = [ref[c, layers].reshape(group * ny, nx) for c in comps]
        result = periodic_x(jnp.concatenate(rows, axis=0), weights)
        for i in range(len(comps)):
            part = result[i * group * ny : (i + 1) * group * ny]
            out_ref[i, layers] = part.reshape(group, ny, nx)


def lookup(row, tile):
    table = jnp.broadcast_to(row, tile.shape)
    return jnp.take_along_axis(table, tile, axis=1, mode="promise_in_bounds")


def table_rows(refs, nx):
    n = refs[0].shape[1]
    return [jnp.concatenate([r, jnp.zeros((1, nx - n), F32)], axis=1) for r in refs]


def fill_edges(n_gx, edge_ref, x1_ref, x2_ref, low_ref, high_ref):
    for c in range(3):
        at = slice(SUB * c, SUB * c + SUB)
        got = (x1_ref[at, :], x2_ref[at, :])
        first, second = edge_terms(
            from_before("gx", got), from_after("gx", n_gx, got), low_ref[at, :], high_ref[at, :]
        )
        edge_ref[c, 0] = first
        edge_ref[c, 1] = second


def fill_rows(n_gy, tall, field, y1_ref, y2_ref, nz, ny, layers):
    for c in range(3):
        for spot, k in enumerate(layers):
            j = 2 * (c * nz + k)
            got = (y1_ref[j : j + 2, :], y2_ref[j : j + 2, :])
            tall[c, spot, PAD : PAD + ny, :] = field(c, k)
            tall[c, spot, PAD - 2 : PAD, :] = from_before("gy", got)
            tall[c, spot, PAD + ny : PAD + ny + 2, :] = from_after("gy", n_gy, got)


def depth_halos(n_gz, zb, za, z1_ref, z2_ref):
    got = (z1_ref[...], z2_ref[...])
    zb[...] = from_before("gz", got)
    za[...] = from_after("gz", n_gz, got)


def over(low, high, most, body):
    count = high - low
    group = next(d for d in range(most, 0, -1) if count % d == 0)

    @pl.loop(0, count // group)
    def _(j):
        for i in range(group):
            body(low + j * group + i)


def tile_rows(t):
    return slice(SUB * t, SUB * t + SUB)


def row_difference(tall, c, spot, t):
    return centred12(lambda s: tall[c, spot, PAD + SUB * t + s : PAD + SUB * t + s + SUB, :])


def inner_depth(ref, out_ref, comps, k, tiles):
    for t in range(tiles):
        for c in range(comps):
            out_ref[c, k - 2, tile_rows(t), :] = centred12(lambda s: ref[c, k + s, tile_rows(t), :])


def outer_depth(ref, zb, za, out_ref, comps, nz, tiles):
    for spot, k in enumerate((0, 1, nz - 2, nz - 1)):
        for t in range(tiles):
            for c in range(comps):

                def at(s):
                    if k + s < 0:
                        return zb[c, k + s + 2, tile_rows(t), :]
                    if k + s >= nz:
                        return za[c, k + s - nz, tile_rows(t), :]
                    return ref[c, k + s, tile_rows(t), :]

                out_ref[c, spot, tile_rows(t), :] = centred12(at)


def cell_kernel(
    layers_ref, material_ref, buoy_ref, lam_ref, mu_ref, relax_ref, weight_ref, cells_ref, spread_ref
):
    lane = lanes_of((SUB, layers_ref.shape[1]))
    sub = lax.broadcasted_iota(jnp.int32, lane.shape, 0)
    for i in range(2):
        row = jnp.broadcast_to(layers_ref[i : i + 1, :], lane.shape)
        for g in range(spread_ref.shape[1] // SUB):
            one = jnp.sum(jnp.where(lane == SUB * g + sub, row, 0.0), axis=1, keepdims=True)
            spread_ref[i, tile_rows(g), :] = jnp.broadcast_to(one, lane.shape)
    nz, ny, nx = material_ref.shape
    keep = jnp.exp(-step_size / relax_ref[...])
    tables = table_rows(
        [
            buoy_ref[...] * (step_size / 12.0), lam_ref[...] / 12.0, mu_ref[...] / 12.0, keep,
            (1.0 - keep) * weight_ref[...],
        ],
        nx,
    )

    def layer(k):
        for t in range(ny // SUB):
            kind = material_ref[k, tile_rows(t), :]
            for i, table in enumerate(tables):
                cells_ref[i, k, tile_rows(t), :] = lookup(table, kind)

    over(0, nz, 4, layer)


def depth_kernel(stress_ref, velocity_hbm, depth_ref, along_ref, velocity_ref, sem):
    load = pltpu.make_async_copy(velocity_hbm, velocity_ref, sem)
    load.start()
    _, nz, ny, _ = stress_ref.shape
    along_all(stress_ref, (0, 3, 4), along_ref)
    over(2, nz - 2, 4, lambda k: inner_depth(stress_ref, depth_ref, 6, k, ny // SUB))
    load.wait()


def plane_kernel(
    sizes, stress_ref, along_ref, y1_ref, y2_ref, z1_ref, z2_ref, plane_ref, outer_ref, tall, zb, za
):
    depth_halos(sizes[2], zb, za, z1_ref, z2_ref)
    outer_depth(stress_ref, zb, za, outer_ref, 6, stress_ref.shape[1], stress_ref.shape[2] // SUB)
    _, nz, ny, nx = stress_ref.shape
    tiles = ny // SUB
    of_y = (3, 1, 5)
    fill_rows(sizes[1], tall, lambda c, k: stress_ref[of_y[c], k], y1_ref, y2_ref, nz, ny, range(nz))

    def layer(k):
        for t in range(tiles):
            for c in range(3):
                plane_ref[c, k, tile_rows(t), :] = along_ref[
                    c, k, tile_rows(t), :
                ] + row_difference(tall, c, k, t)

    over(0, nz, 4, layer)


def velocity_kernel(
    sizes, velocity_ref, cells_ref, inner_ref, outer_ref, plane_ref, factor_ref, mz_ref, slope_ref,
    x1_ref, x2_ref, low_ref, high_ref, out_ref, vlow_ref, vhigh_ref, vx1_ref, vx2_ref, vz1_ref, vz2_ref,
    *rest,
):
    *vy_refs, edge = rest
    _, nz, ny, nx = velocity_ref.shape
    tiles = ny // SUB
    lane = lanes_of((SUB, nx))
    fill_edges(sizes[0], edge, x1_ref, x2_ref, low_ref, high_ref)

    def layer(k, depth_ref, spot):
        for t in range(tiles):
            rows = tile_rows(t)
            b = cells_ref[0, k, rows, :]
            factor = factor_ref[k, rows, :]
            mz = mz_ref[k, rows, :]
            mx = slope_ref[0, rows, :] * factor
            my = slope_ref[1, rows, :] * factor
            gk = [depth_ref[c, spot, rows, :] for c in range(6)]
            beside = [
                plane_ref[c, k, rows, :]
                + jnp.where(sides(lane), turned_left(edge[c, t % 2], k * tiles + t), 0.0)
                for c in range(3)
            ]
            accel = (
                beside[0] - mx * gk[0] - my * gk[3] + mz * gk[4],
                beside[1] - mx * gk[3] - my * gk[1] + mz * gk[5],
                beside[2] - mx * gk[4] - my * gk[5] + mz * gk[2],
            )
            for c in range(3):
                out_ref[c, k, rows, :] = velocity_ref[c, k, rows, :] + b * accel[c]

    for spot, k in enumerate((0, 1, nz - 2, nz - 1)):
        layer(k, outer_ref, spot)

    over(2, nz - 2, 4, lambda k: layer(k, inner_ref, k - 2))
    pack_sides(
        lambda c, k, t: out_ref[c, k, tile_rows(t), :], nz, ny, nx, vlow_ref, vhigh_ref, vx1_ref, vx2_ref
    )
    pack_rows(lambda c, k, rows: out_ref[c, k, rows, :], nz, ny, vy_refs)
    vz1_ref[...], vz2_ref[...] = order("gz", out_ref[:, nz - 2 : nz], out_ref[:, 0:2])


def velocity_inner_kernel(vel_ref, vel_hbm, depth_ref, along_ref, sem):
    store = pltpu.make_async_copy(vel_ref, vel_hbm, sem)
    store.start()
    _, nz, ny, nx = vel_ref.shape
    tiles = ny // SUB

    along_all(vel_ref, (0, 1, 2), along_ref)
    over(2, nz - 2, 4, lambda k: inner_depth(vel_ref, depth_ref, 3, k, tiles))
    store.wait()


def stress_kernel(
    sizes, vel_ref, stress_ref, memory_ref, cells_ref, inner_ref, along_ref, factor_ref, mz_ref, slope_ref,
    x1_ref, x2_ref, low_ref, high_ref, y1_ref, y2_ref, z1_ref, z2_ref,
    stress_hbm, memory_hbm, edge, tall, zb, za, outer, stress_out, memory_out, sems,
):
    n_gx, n_gy, n_gz = sizes
    _, nz, ny, nx = vel_ref.shape
    tiles = ny // SUB
    lane = lanes_of((SUB, nx))
    fill_edges(n_gx, edge, x1_ref, x2_ref, low_ref, high_ref)
    fill_rows(n_gy, tall, lambda c, k: vel_ref[c, k], y1_ref, y2_ref, nz, ny, range(nz))

    def layer(k, depth_ref, spot):
        for t in range(tiles):
            rows = tile_rows(t)
            factor = factor_ref[k, rows, :]
            mz = mz_ref[k, rows, :]
            mx = slope_ref[0, rows, :] * factor
            my = slope_ref[1, rows, :] * factor
            dk = [depth_ref[c, spot, rows, :] for c in range(3)]
            dx = [
                along_ref[c, k, rows, :]
                + jnp.where(sides(lane), turned_left(edge[c, t % 2], k * tiles + t), 0.0)
                - mx * dk[c]
                for c in range(3)
            ]
            dy = [row_difference(tall, c, k, t) - my * dk[c] for c in range(3)]
            dz = [mz * dk[c] for c in range(3)]
            lam, mu, keep, gain = (cells_ref[i, k, rows, :] for i in range(1, 5))
            volume = lam * (dx[0] + dy[1] + dz[2])
            mu2 = mu + mu
            rates = (
                volume + mu2 * dx[0],
                volume + mu2 * dy[1],
                volume + mu2 * dz[2],
                mu * (dy[0] + dx[1]),
                mu * (dz[0] + dx[2]),
                mu * (dz[1] + dy[2]),
            )
            for c in range(6):
                kept = keep * memory_ref[c, k, rows, :] + gain * rates[c]
                memory_out[c, k, rows, :] = kept
                stress_out[c, k, rows, :] = stress_ref[c, k, rows, :] + step_size * (
                    rates[c] - kept
                )

    def out_copies(first, count, spot):
        layers = pl.ds(first, count)
        return [
            pltpu.make_async_copy(a.at[:, layers], b.at[:, layers], sems.at[i, spot])
            for i, (a, b) in enumerate(((stress_out, stress_hbm), (memory_out, memory_hbm)))
        ]

    inner = nz - 4
    step = next(d for d in (4, 3, 2, 1) if inner % d == 0)
    chunks = inner // step

    @pl.loop(0, chunks)
    def _(j):
        for i in range(step):
            k = 2 + j * step + i
            layer(k, inner_ref, k - 2)

        for copy in out_copies(2 + j * step, step, 2 + j):
            copy.start()

    depth_halos(n_gz, zb, za, z1_ref, z2_ref)
    outer_depth(vel_ref, zb, za, outer, 3, nz, tiles)
    last = []
    for spot, k in enumerate((0, 1, nz - 2, nz - 1)):
        layer(k, outer, spot)
        if spot % 2 == 1:
            last += out_copies(k - 1, 2, spot // 2)
            for copy in last[-2:]:
                copy.start()

    @pl.loop(0, chunks)
    def _(j):
        for copy in out_copies(2 + j * step, step, 2 + j):
            copy.wait()

    for copy in last:
        copy.wait()


def in_hbm(value):
    return pltpu.with_memory_space_constraint(value, pltpu.HBM)


def call(kernel, outs, in_specs, scratch=(), name=None, out_specs=None, cost=0.0):
    return pl.pallas_call(
        kernel,
        out_shape=[jax.ShapeDtypeStruct(s, F32) for s in outs],
        in_specs=in_specs,
        out_specs=out_specs or [VM] * len(outs),
        scratch_shapes=list(scratch),
        compiler_params=params(),
        cost_estimate=pl.CostEstimate(flops=int(cost * 6e8), transcendentals=0, bytes_accessed=int(cost * 3.5e6)),
        name=name,
    )


def local(
    sizes, elevation, layer_base, stretch, material, buoyancy, lame_lambda, shear_modulus,
    relax_time, anelastic_weight, velocity, stress, memory,
):
    n_gx, n_gy, n_gz = counts = tuple(sizes[a] for a in ("gx", "gy", "gz"))
    _, nz, ny, nx = velocity.shape
    rows = ny + SUB
    rounds = pair_swaps(sizes, "gz")
    if n_gz == 4:
        piece = lax.ppermute(elevation, tuple(sizes), rounds[0])
    slab = call(
        terrain_piece_kernel,
        [(rows, nx)],
        [HB] * 3,
        [
            pltpu.VMEM(elevation.shape, jnp.int32),
            pltpu.VMEM((1, nz), F32),
            pltpu.VMEM((1, nz), F32),
            DMA((3,)),
        ],
        name="terrain_piece", cost=0.8,
    )(in_hbm(elevation), in_hbm(layer_base[None]), in_hbm(stretch[None]))[0]
    tied = lax.optimization_barrier
    faces = 2 * 3 * nz
    xs = 3 * SUB
    y_rounds = min(2, n_gy - 1) if n_gy > 1 else 1
    z_face = (6, 2, ny, nx)
    if n_gz == 4:
        slab = call(merge_kernel, [(rows, nx)], [VM] * 2, name="merge", cost=0.1)(slab, piece)[0]
        slab, stress = tied((slab, stress))
        slab = slab + lax.ppermute(slab, tuple(sizes), rounds[1])
        layers = slab[ny:]
    elif n_gz & (n_gz - 1):
        slab = lax.psum(slab, "gz")
        layers = slab[ny:]
    else:
        bit = 1
        while bit < n_gz:
            slab = slab + lax.ppermute(slab, "gz", [(i, i ^ bit) for i in range(n_gz)])
            if bit == 1:
                slab, stress = tied((slab, stress))
            bit *= 2
        layers = slab[ny:]
    stress_vm = stress
    low, high, x1, x2, z1, z2, *ys = call(
        pack_kernel,
        [(xs, nx)] * 4 + [z_face] * 2 + [(faces, nx)] * y_rounds,
        [VM],
        name="pack_stress", cost=0.5,
    )(stress)
    z1, z2 = exchange(sizes, "gz", z1, z2)
    ts = call(y_send_kernel, [(SUB, nx)] * y_rounds, [VM], name="y_send", cost=0.02)(slab)
    ts, ys, stress_vm, layers = tied((ts, ys, stress_vm, layers))
    t1, t2 = exchange(sizes, "gy", ts[0], ts[-1])
    y1, y2 = exchange(sizes, "gy", ys[0], ys[-1])
    if n_gz == 4:
        layers = layers + lax.ppermute(layers, tuple(sizes), rounds[0])
    inner_k, along, velocity_vm = call(
        depth_kernel,
        [(6, nz - 4, ny, nx), velocity.shape, velocity.shape],
        [VM, HB],
        [DMA],
        name="depth", cost=2.2,
    )(stress_vm, in_hbm(velocity))
    x1, x2, inner_k = tied((x1, x2, inner_k))
    terrain, x1, x2 = call(
        functools.partial(x_send_kernel, n_gy),
        [(ny + 2 * PAD, nx)] + [(xs + SUB, nx)] * 2,
        [VM] * 5,
        name="x_send", cost=0.1,
    )(slab, t1, t2, x1, x2)
    x1, x2, material = tied((x1, x2, material))
    x1, x2 = exchange(sizes, "gx", x1, x2, True)
    edge = pltpu.VMEM((3, 2, SUB, nx), F32)
    tall = pltpu.VMEM((3, nz, ny + 2 * PAD, nx), F32)

    def depth(comps):
        return [pltpu.VMEM((comps, 2, ny, nx), F32)] * 2

    tables = (buoyancy, lame_lambda, shear_modulus, relax_time, anelastic_weight)
    all_layers = -(-n_gz * nz // SUB) * SUB
    cells, spread = call(
        cell_kernel, [(5, nz, ny, nx), (2, all_layers, nx)], [VM] * 7, name="cells", cost=0.8
    )(layers, material, *[table[None] for table in tables])
    plane, outer_k = call(
        functools.partial(plane_kernel, counts),
        [velocity.shape, (6, 4, ny, nx)],
        [VM] * 6,
        [tall] + depth(6),
        name="planes", cost=0.6,
    )(stress_vm, along, y1, y2, z1, z2)
    plane, cells, x1, x2 = tied((plane, cells, x1, x2))
    factor, mz, slope = call(
        functools.partial(metric_kernel, counts),
        [(nz, ny, nx), (nz, ny, nx), (2, ny, nx)],
        [VM] * 4,
        [pltpu.VMEM((ny + 2 * PAD, nx), F32), pltpu.VMEM((ny + PAD, nx), F32)],
        name="metrics", cost=1.1,
    )(spread, terrain, x1[xs:], x2[xs:])
    vel, vlow, vhigh, vx1, vx2, vz1, vz2, *vys = call(
        functools.partial(velocity_kernel, counts),
        [velocity.shape] + [(xs, nx)] * 4 + [(3, 2, ny, nx)] * 2 + [(faces, nx)] * y_rounds,
        [VM] * 12,
        [edge],
        name="velocity", cost=1.5,
    )(velocity_vm, cells, inner_k, outer_k, plane, factor, mz, slope, x1, x2, low, high)
    vz1, vz2 = exchange(sizes, "gz", vz1, vz2)
    vy1, vy2 = exchange(sizes, "gy", vys[0], vys[-1])
    vx1, vx2 = exchange(sizes, "gx", vx1, vx2)
    vel_next, vel_k, vel_x = call(
        velocity_inner_kernel,
        [velocity.shape, (3, nz - 4, ny, nx), velocity.shape],
        [VM],
        [DMA],
        name="velocity_inner", cost=0.1,
        out_specs=[HB, VM, VM],
    )(vel)
    stress_next, memory_next = call(
        functools.partial(stress_kernel, counts),
        [stress.shape, stress.shape],
        [VM] * 17,
        [edge, tall] + depth(3)
        + [pltpu.VMEM((3, 4, ny, nx), F32), pltpu.VMEM(stress.shape, F32), pltpu.VMEM(stress.shape, F32)]
        + [DMA((2, nz))],
        name="stress", cost=2.8,
        out_specs=[HB] * 2,
    )(
        vel, stress_vm, memory, cells, vel_k, vel_x, factor, mz, slope, vx1, vx2, vlow, vhigh, vy1, vy2,
        vz1, vz2,
    )
    return vel_next, stress_next, memory_next


def solution(mesh):
    sizes = {a: mesh.shape[a] for a in ("gx", "gy", "gz")}
    field = P(None, "gz", "gy", "gx")
    return jax.shard_map(
        functools.partial(local, sizes),
        mesh=mesh,
        in_specs=(
            P("gy", ("gx", "gz")), P("gz"), P("gz"), P("gz", "gy", "gx"),
            P(), P(), P(), P(), P(), field, field, field,
        ),
        out_specs=(field, field, field),
        check_vma=False,
    )
```

```python
import functools
import jax
import jax.numpy as jnp
import numpy as np
from jax import lax
from jax.experimental import pallas as pl
from jax.experimental.pallas import tpu as pltpu
from jax.sharding import PartitionSpec as P

step_size = 0.3
SUB = 8
PAD = 8
F32 = jnp.float32
params = functools.partial(pltpu.CompilerParams, vmem_limit_bytes=20 * 1024 * 1024)
VM = pl.BlockSpec(memory_space=pltpu.VMEM)
SM = pl.BlockSpec(memory_space=pltpu.SMEM)
HB = pl.BlockSpec(memory_space=pltpu.HBM)
DMA = pltpu.SemaphoreType.DMA


def pair_swaps(sizes, axis):
    names = tuple(sizes)
    shape = tuple(sizes.values())
    index = names.index(axis)
    n = shape[index]
    others = [d for d in (2, 1, 0) if d != index and shape[d] % 2 == 0]
    rounds = []
    for first in (0, 1)[: max(0, min(2, n - 1))]:
        table = []
        for spot in np.ndindex(*shape):
            mate = spot[index] + 1 if spot[index] % 2 == first else spot[index] - 1
            target = list(spot)
            if 0 <= mate < n or axis == "gz":
                target[index] = mate % n
            elif others:
                target[others[0]] ^= 1
            else:
                continue
            table.append((int(np.ravel_multi_index(spot, shape)), int(np.ravel_multi_index(tuple(target), shape))))
        rounds.append(table)
    return rounds


def exchange(sizes, axis, first, second, second_first=False):
    rounds = list(zip((first, second), pair_swaps(sizes, axis)))
    if second_first:
        rounds = rounds[::-1]
    got = [lax.ppermute(v, tuple(sizes), r) for v, r in rounds]
    if second_first:
        got = got[::-1]
    return (got[0], got[-1]) if got else (first, second)


def even(axis):
    return lax.axis_index(axis) % 2 == 0


def from_before(axis, got):
    value = jnp.where(even(axis), got[1], got[0])
    return jnp.where(lax.axis_index(axis) > 0, value, 0.0)


def from_after(axis, n, got):
    value = jnp.where(even(axis), got[0], got[1])
    return jnp.where(lax.axis_index(axis) < n - 1, value, 0.0)


def order(axis, to_after, to_before):
    e = even(axis)
    return jnp.where(e, to_after, to_before), jnp.where(e, to_before, to_after)


def lanes_of(shape):
    return lax.broadcasted_iota(jnp.int32, shape, len(shape) - 1)


def terrain_piece_kernel(elev_hbm, base_hbm, stretch_hbm, out_ref, elev_ref, base_ref, stretch_ref, sems):
    mine = lax.axis_index("gz")
    pairs = ((elev_hbm, elev_ref), (base_hbm, base_ref), (stretch_hbm, stretch_ref))
    copies = [pltpu.make_async_copy(a, b, sems.at[i]) for i, (a, b) in enumerate(pairs)]
    for copy in copies:
        copy.start()
    for copy in copies:
        copy.wait()
    ny, width = elev_ref.shape
    nx = out_ref.shape[1]
    nz = base_ref.shape[1]
    height = elev_ref[...].astype(F32) / 200.0
    wide = jnp.concatenate([height, jnp.zeros((ny, nx - width), F32)], axis=1)
    out_ref[:ny, :] = pltpu.roll(wide, mine * width, 1)
    row = lax.broadcasted_iota(jnp.int32, (SUB, nx), 0)
    fill = jnp.zeros((1, nx - nz), F32)
    base = jnp.concatenate([base_ref[...], fill], axis=1)
    stretch = jnp.concatenate([stretch_ref[...], fill], axis=1)
    both = jnp.where(row == 0, base, jnp.where(row == 1, stretch, 0.0))
    out_ref[ny:, :] = pltpu.roll(both, mine * nz, 1)


def merge_kernel(first_ref, elev_ref, out_ref):
    ny, width = elev_ref.shape
    nx = out_ref.shape[1]
    height = elev_ref[...].astype(F32) / 200.0
    wide = jnp.concatenate([height, jnp.zeros((ny, nx - width), F32)], axis=1)
    mate = lax.axis_index("gz") + jnp.where(even("gz"), 1, -1)
    out_ref[:ny, :] = first_ref[:ny, :] + pltpu.roll(wide, mate * width, 1)
    out_ref[ny:, :] = first_ref[ny:, :]


def pack_sides(field, nz, ny, nx, low_ref, high_ref, out1_ref, out2_ref):
    tiles = ny // SUB
    lane2 = lanes_of((SUB, nx)) // 2
    for c in range(3):
        lo = jnp.zeros((SUB, nx), F32)
        hi = jnp.zeros((SUB, nx), F32)
        for k in range(nz):
            for t in range(tiles):
                m = k * tiles + t
                turned = pltpu.roll(field(c, k, t), (2 * m + 2) % nx, 1)
                hi = jnp.where(lane2 == m, turned, hi)
                lo = jnp.where(lane2 == (m + 1) % (nx // 2), turned, lo)
        at = slice(SUB * c, SUB * c + SUB)
        low_ref[at, :] = lo
        high_ref[at, :] = hi
        out1_ref[at, :], out2_ref[at, :] = order("gx", hi, lo)


def pack_rows(field, nz, ny, y_refs):
    for c in range(3):
        for k in range(nz):
            j = 2 * (c * nz + k)
            both = order("gy", field(c, k, slice(ny - 2, ny)), field(c, k, slice(0, 2)))
            for ref, rows in zip(y_refs, both):
                ref[j : j + 2, :] = rows


def pack_kernel(stress_ref, low_ref, high_ref, out1_ref, out2_ref, z1_ref, z2_ref, *y_refs):
    _, nz, ny, nx = stress_ref.shape
    of_x = (0, 3, 4)
    of_y = (3, 1, 5)
    z1_ref[...], z2_ref[...] = order("gz", stress_ref[:, nz - 2 : nz], stress_ref[:, 0:2])
    pack_sides(
        lambda c, k, t: stress_ref[of_x[c], k, SUB * t : SUB * t + SUB, :],
        nz, ny, nx, low_ref, high_ref, out1_ref, out2_ref,
    )
    pack_rows(lambda c, k, rows: stress_ref[of_y[c], k, rows, :], nz, ny, y_refs)


def y_send_kernel(slab_ref, *out_refs):
    ny = slab_ref.shape[0] - SUB
    both = order("gy", slab_ref[ny - 4 : ny, :], slab_ref[0:4, :])
    for ref, rows in zip(out_refs, both):
        ref[0:4, :] = rows
        ref[4:, :] = jnp.zeros_like(rows)


def x_send_kernel(n_gy, slab_ref, y1_ref, y2_ref, x1_ref, x2_ref, tall_ref, out1_ref, out2_ref):
    ny = slab_ref.shape[0] - SUB
    nx = slab_ref.shape[1]
    xs = x1_ref.shape[0]
    lane4 = lanes_of((SUB, nx)) // 4
    got = (y1_ref[0:4, :], y2_ref[0:4, :])
    tall_ref[: PAD - 4, :] = jnp.zeros((PAD - 4, nx), F32)
    tall_ref[PAD - 4 : PAD, :] = from_before("gy", got)
    tall_ref[PAD : PAD + ny, :] = slab_ref[:ny, :]
    tall_ref[PAD + ny : PAD + ny + 4, :] = from_after("gy", n_gy, got)
    tall_ref[PAD + ny + 4 :, :] = jnp.zeros((PAD - 4, nx), F32)
    lo = jnp.zeros((SUB, nx), F32)
    hi = jnp.zeros((SUB, nx), F32)
    for j in range((ny + 2 * PAD) // SUB):
        tile = tall_ref[SUB * j : SUB * j + SUB, :]
        lo = jnp.where(lane4 == j, pltpu.roll(tile, 4 * j, 1), lo)
        hi = jnp.where(lane4 == j, pltpu.roll(tile, (4 * j + 4) % nx, 1), hi)
    out1_ref[:xs, :] = x1_ref[...]
    out2_ref[:xs, :] = x2_ref[...]
    out1_ref[xs:, :], out2_ref[xs:, :] = order("gx", hi, lo)


def binomial(at):
    return (at(-2) + at(2) + 4.0 * (at(-1) + at(1)) + 6.0 * at(0)) / 16.0


def centred12(at):
    return 8.0 * (at(1) - at(-1)) - (at(2) - at(-2))


def metric_kernel(
    sizes, layers_ref, own, x1_ref, x2_ref, factor_ref, mz_ref, slope_ref, rim, sown,
):
    n_gx = sizes[0]
    gz = lax.axis_index("gz")
    nz, ny, nx = factor_ref.shape
    lane = lanes_of((SUB, nx))
    got = (x1_ref[...], x2_ref[...])
    left, right = from_before("gx", got), from_after("gx", n_gx, got)
    for j in range((ny + 2 * PAD) // SUB):
        rim[SUB * j : SUB * j + SUB, :] = jnp.where(
            lane < nx // 2,
            pltpu.roll(right, (nx - 4 * j) % nx, 1),
            pltpu.roll(left, nx - 4 - 4 * j, 1),
        )
    rows = ny + 4
    tall_own = binomial(lambda s: own[PAD - 2 + s : PAD - 2 + s + rows, :])
    tall_rim = binomial(lambda s: rim[PAD - 2 + s : PAD - 2 + s + rows, :])

    def shifted(a, b, s):
        ln = lanes_of(a.shape)
        cut = (ln < s) if s > 0 else (ln >= nx + s)
        if s > 0:
            mixed_a, mixed_b = jnp.where(cut, b, a), jnp.where(cut, a, b)
        elif s < 0:
            mixed_a, mixed_b = jnp.where(cut, b, a), jnp.where(cut, a, b)
        else:
            return a, b
        return pltpu.roll(mixed_a, (-s) % nx, 1), pltpu.roll(mixed_b, (-s) % nx, 1)

    def padded_rows(a):
        return jnp.concatenate([a, jnp.zeros((SUB - rows % SUB, nx), F32)], axis=0)

    tall_own, tall_rim = padded_rows(tall_own), padded_rows(tall_rim)
    pairs = {s: shifted(tall_own, tall_rim, s) for s in (-2, -1, 0, 1, 2)}
    surf_own = binomial(lambda s: pairs[s][0])
    surf_rim = binomial(lambda s: pairs[s][1])
    sown[...] = surf_own
    slope_ref[1] = centred12(lambda s: sown[2 + s : 2 + s + ny, :]) / 12.0
    pairs2 = {s: shifted(surf_own, surf_rim, s)[0] for s in (-2, -1, 1, 2)}
    along = centred12(lambda s: pairs2[s]) / 12.0
    surface = sown[2 : 2 + ny, :]
    sown[...] = along
    slope_ref[0] = sown[2 : 2 + ny, :]

    def above(slab, total):
        for k in range(nz):
            at = pl.ds(slab * nz + k, 1)
            s = layers_ref[1, at, :]
            total = total + (s * layers_ref[0, at, :]) * jnp.exp(s * surface)
        return total

    total = lax.fori_loop(0, gz, above, jnp.zeros((ny, nx), F32))
    for k in range(nz):
        at = pl.ds(gz * nz + k, 1)
        s = layers_ref[1, at, :]
        thickness = layers_ref[0, at, :] * jnp.exp(s * surface)
        weighted = s * thickness
        mz = 1.0 / thickness
        lift = total + 0.5 * weighted
        total = total + weighted
        mz_ref[k] = mz
        factor_ref[k] = (lift - 1.0) * mz

def edge_terms(got_left, got_right, low, high):
    dl = got_left - high
    dr = got_right - low
    nx = dl.shape[-1]
    lane = lanes_of(dl.shape)
    even = lane % 2 == 0
    dl = pltpu.roll(dl, 2, 1)
    dr = pltpu.roll(dr, nx - 2, 1)
    to_low = jnp.where(even, dl - 8.0 * pltpu.roll(dl, nx - 1, 1), dl)
    to_high = jnp.where(even, -dr, 8.0 * pltpu.roll(dr, 1, 1) - dr)
    second = (lane // 2) % 2 == 1
    return jnp.where(second, to_low, to_high), jnp.where(second, to_high, to_low)


def turned_left(edges, m):
    nx = edges.shape[-1]
    shift = (2 * nx - 2 - 2 * m) % nx if isinstance(m, int) else 2 * nx - 2 - 2 * m
    return pltpu.roll(edges, shift, 1)


def sides(lane):
    return (lane < 2) | (lane >= lane.shape[-1] - 2)


def x_weights(nx):
    ahead = (
        lax.broadcasted_iota(jnp.int32, (nx, nx), 0) - lax.broadcasted_iota(jnp.int32, (nx, nx), 1)
    )
    weights = jnp.zeros((nx, nx), F32)
    for offset, weight in ((1, 8.0), (-1, -8.0), (2, -1.0), (-2, 1.0)):
        weights = jnp.where((ahead == offset) | (ahead == offset + nx) | (ahead == offset - nx), weight, weights)
    weights = weights.astype(jnp.bfloat16)
    return jnp.concatenate([weights] * 3, axis=0)


def periodic_x(value, weights):
    high = value.astype(jnp.bfloat16)
    rest = value - high.astype(F32)
    middle = rest.astype(jnp.bfloat16)
    low = (rest - middle.astype(F32)).astype(jnp.bfloat16)
    return jnp.dot(
        jnp.concatenate([high, middle, low], axis=1), weights, preferred_element_type=F32
    )


def along_all(ref, comps, out_ref, group=16):
    _, nz, ny, nx = out_ref.shape
    group = next(d for d in range(group, 0, -1) if nz % d == 0)
    weights = x_weights(nx)

    @pl.loop(0, nz // group)
    def _(j):
        layers = pl.ds(j * group, group)
        rows = [ref[c, layers].reshape(group * ny, nx) for c in comps]
        result = periodic_x(jnp.concatenate(rows, axis=0), weights)
        for i in range(len(comps)):
            part = result[i * group * ny : (i + 1) * group * ny]
            out_ref[i, layers] = part.reshape(group, ny, nx)


def lookup(row, tile):
    table = jnp.broadcast_to(row, tile.shape)
    return jnp.take_along_axis(table, tile, axis=1, mode="promise_in_bounds")


def table_rows(refs, nx):
    n = refs[0].shape[1]
    return [jnp.concatenate([r, jnp.zeros((1, nx - n), F32)], axis=1) for r in refs]


def fill_edges(n_gx, edge_ref, x1_ref, x2_ref, low_ref, high_ref):
    for c in range(3):
        at = slice(SUB * c, SUB * c + SUB)
        got = (x1_ref[at, :], x2_ref[at, :])
        first, second = edge_terms(
            from_before("gx", got), from_after("gx", n_gx, got), low_ref[at, :], high_ref[at, :]
        )
        edge_ref[c, 0] = first
        edge_ref[c, 1] = second


def fill_rows(n_gy, tall, field, y1_ref, y2_ref, nz, ny, layers):
    for c in range(3):
        for spot, k in enumerate(layers):
            j = 2 * (c * nz + k)
            got = (y1_ref[j : j + 2, :], y2_ref[j : j + 2, :])
            tall[c, spot, PAD : PAD + ny, :] = field(c, k)
            tall[c, spot, PAD - 2 : PAD, :] = from_before("gy", got)
            tall[c, spot, PAD + ny : PAD + ny + 2, :] = from_after("gy", n_gy, got)


def depth_halos(n_gz, zb, za, z1_ref, z2_ref):
    got = (z1_ref[...], z2_ref[...])
    zb[...] = from_before("gz", got)
    za[...] = from_after("gz", n_gz, got)


def over(low, high, most, body):
    count = high - low
    group = next(d for d in range(most, 0, -1) if count % d == 0)

    @pl.loop(0, count // group)
    def _(j):
        for i in range(group):
            body(low + j * group + i)


def tile_rows(t):
    return slice(SUB * t, SUB * t + SUB)


def row_difference(tall, c, spot, t):
    return centred12(lambda s: tall[c, spot, PAD + SUB * t + s : PAD + SUB * t + s + SUB, :])


def inner_depth(ref, out_ref, comps, k, tiles):
    for t in range(tiles):
        for c in range(comps):
            out_ref[c, k - 2, tile_rows(t), :] = centred12(lambda s: ref[c, k + s, tile_rows(t), :])


def outer_depth(ref, zb, za, out_ref, comps, nz, tiles):
    for spot, k in enumerate((0, 1, nz - 2, nz - 1)):
        for t in range(tiles):
            for c in range(comps):

                def at(s):
                    if k + s < 0:
                        return zb[c, k + s + 2, tile_rows(t), :]
                    if k + s >= nz:
                        return za[c, k + s - nz, tile_rows(t), :]
                    return ref[c, k + s, tile_rows(t), :]

                out_ref[c, spot, tile_rows(t), :] = centred12(at)


def cell_kernel(
    layers_ref, material_ref, buoy_ref, lam_ref, mu_ref, relax_ref, weight_ref, cells_ref, spread_ref
):
    lane = lanes_of((SUB, layers_ref.shape[1]))
    sub = lax.broadcasted_iota(jnp.int32, lane.shape, 0)
    for i in range(2):
        row = jnp.broadcast_to(layers_ref[i : i + 1, :], lane.shape)
        for g in range(spread_ref.shape[1] // SUB):
            one = jnp.sum(jnp.where(lane == SUB * g + sub, row, 0.0), axis=1, keepdims=True)
            spread_ref[i, tile_rows(g), :] = jnp.broadcast_to(one, lane.shape)
    nz, ny, nx = material_ref.shape
    keep = jnp.exp(-step_size / relax_ref[...])
    tables = table_rows(
        [
            buoy_ref[...] * (step_size / 12.0), lam_ref[...] / 12.0, mu_ref[...] / 12.0, keep,
            (1.0 - keep) * weight_ref[...],
        ],
        nx,
    )

    def layer(k):
        for t in range(ny // SUB):
            kind = material_ref[k, tile_rows(t), :]
            for i, table in enumerate(tables):
                cells_ref[i, k, tile_rows(t), :] = lookup(table, kind)

    over(0, nz, 4, layer)


def depth_kernel(stress_ref, velocity_hbm, depth_ref, along_ref, velocity_ref, sem):
    load = pltpu.make_async_copy(velocity_hbm, velocity_ref, sem)
    load.start()
    _, nz, ny, _ = stress_ref.shape
    along_all(stress_ref, (0, 3, 4), along_ref)
    over(2, nz - 2, 4, lambda k: inner_depth(stress_ref, depth_ref, 6, k, ny // SUB))
    load.wait()


def plane_kernel(
    sizes, stress_ref, along_ref, y1_ref, y2_ref, z1_ref, z2_ref, plane_ref, outer_ref, tall, zb, za
):
    depth_halos(sizes[2], zb, za, z1_ref, z2_ref)
    outer_depth(stress_ref, zb, za, outer_ref, 6, stress_ref.shape[1], stress_ref.shape[2] // SUB)
    _, nz, ny, nx = stress_ref.shape
    tiles = ny // SUB
    of_y = (3, 1, 5)
    fill_rows(sizes[1], tall, lambda c, k: stress_ref[of_y[c], k], y1_ref, y2_ref, nz, ny, range(nz))

    def layer(k):
        for t in range(tiles):
            for c in range(3):
                plane_ref[c, k, tile_rows(t), :] = along_ref[
                    c, k, tile_rows(t), :
                ] + row_difference(tall, c, k, t)

    over(0, nz, 4, layer)


def velocity_kernel(
    sizes, velocity_ref, cells_ref, inner_ref, outer_ref, plane_ref, factor_ref, mz_ref, slope_ref,
    x1_ref, x2_ref, low_ref, high_ref, out_ref, vlow_ref, vhigh_ref, vx1_ref, vx2_ref, vz1_ref, vz2_ref,
    *rest,
):
    *vy_refs, edge = rest
    _, nz, ny, nx = velocity_ref.shape
    tiles = ny // SUB
    lane = lanes_of((SUB, nx))
    fill_edges(sizes[0], edge, x1_ref, x2_ref, low_ref, high_ref)

    def layer(k, depth_ref, spot):
        for t in range(tiles):
            rows = tile_rows(t)
            b = cells_ref[0, k, rows, :]
            factor = factor_ref[k, rows, :]
            mz = mz_ref[k, rows, :]
            mx = slope_ref[0, rows, :] * factor
            my = slope_ref[1, rows, :] * factor
            gk = [depth_ref[c, spot, rows, :] for c in range(6)]
            beside = [
                plane_ref[c, k, rows, :]
                + jnp.where(sides(lane), turned_left(edge[c, t % 2], k * tiles + t), 0.0)
                for c in range(3)
            ]
            accel = (
                beside[0] - mx * gk[0] - my * gk[3] + mz * gk[4],
                beside[1] - mx * gk[3] - my * gk[1] + mz * gk[5],
                beside[2] - mx * gk[4] - my * gk[5] + mz * gk[2],
            )
            for c in range(3):
                out_ref[c, k, rows, :] = velocity_ref[c, k, rows, :] + b * accel[c]

    for spot, k in enumerate((0, 1, nz - 2, nz - 1)):
        layer(k, outer_ref, spot)

    over(2, nz - 2, 4, lambda k: layer(k, inner_ref, k - 2))
    pack_sides(
        lambda c, k, t: out_ref[c, k, tile_rows(t), :], nz, ny, nx, vlow_ref, vhigh_ref, vx1_ref, vx2_ref
    )
    pack_rows(lambda c, k, rows: out_ref[c, k, rows, :], nz, ny, vy_refs)
    vz1_ref[...], vz2_ref[...] = order("gz", out_ref[:, nz - 2 : nz], out_ref[:, 0:2])


def velocity_inner_kernel(vel_ref, vel_hbm, depth_ref, along_ref, across_ref, tall, sem):
    store = pltpu.make_async_copy(vel_ref, vel_hbm, sem)
    store.start()
    _, nz, ny, nx = vel_ref.shape
    tiles = ny // SUB

    along_all(vel_ref, (0, 1, 2), along_ref)
    over(2, nz - 2, 4, lambda k: inner_depth(vel_ref, depth_ref, 3, k, tiles))
    nothing = jnp.zeros((2, nx), F32)
    for c in range(3):
        for k in range(nz):
            tall[c, k, PAD : PAD + ny, :] = vel_ref[c, k]
            tall[c, k, PAD - 2 : PAD, :] = nothing
            tall[c, k, PAD + ny : PAD + ny + 2, :] = nothing

    def across(k):
        for t in range(tiles):
            for c in range(3):
                across_ref[c, k, tile_rows(t), :] = row_difference(tall, c, k, t)

    over(0, nz, 4, across)
    store.wait()


def fill_sides(n_gy, top, bottom, y1_ref, y2_ref):
    count = y1_ref.shape[0]
    got = (y1_ref[...], y2_ref[...])
    even_row = lax.broadcasted_iota(jnp.int32, got[0].shape, 0) % 2 == 0
    empty = jnp.zeros((SUB, y1_ref.shape[1]), F32)
    before, after = from_before("gy", got), from_after("gy", n_gy, got)
    top[:count, :] = before
    top[count:, :] = empty
    bottom[:SUB, :] = empty
    bottom[SUB:, :] = after
    top[:count, :] = jnp.where(even_row, before - 8.0 * top[1 : count + 1, :], before)
    bottom[SUB:, :] = jnp.where(even_row, -after, 8.0 * bottom[SUB - 1 : SUB + count - 1, :] - after)


def beside_rows(top, bottom, c, k, t, nz, tiles):
    j = 2 * (c * nz + k)
    row = lax.broadcasted_iota(jnp.int32, (SUB, top.shape[1]), 0)
    added = 0.0
    if t == 0:
        added = jnp.where(row < 2, top[pl.ds(j, SUB), :], 0.0)
    if t == tiles - 1:
        added = added + jnp.where(row >= SUB - 2, bottom[pl.ds(j + 2, SUB), :], 0.0)
    return added


def stress_kernel(
    sizes, vel_ref, stress_ref, memory_ref, cells_ref, inner_ref, along_ref, across_ref, factor_ref, mz_ref,
    slope_ref, x1_ref, x2_ref, low_ref, high_ref, y1_ref, y2_ref, z1_ref, z2_ref,
    stress_hbm, memory_hbm, edge, top, bottom, zb, za, outer, stress_out, memory_out, sems,
):
    n_gx, n_gy, n_gz = sizes
    _, nz, ny, nx = vel_ref.shape
    tiles = ny // SUB
    lane = lanes_of((SUB, nx))
    fill_edges(n_gx, edge, x1_ref, x2_ref, low_ref, high_ref)
    fill_sides(n_gy, top, bottom, y1_ref, y2_ref)

    def layer(k, depth_ref, spot):
        for t in range(tiles):
            rows = tile_rows(t)
            factor = factor_ref[k, rows, :]
            mz = mz_ref[k, rows, :]
            mx = slope_ref[0, rows, :] * factor
            my = slope_ref[1, rows, :] * factor
            dk = [depth_ref[c, spot, rows, :] for c in range(3)]
            dx = [
                along_ref[c, k, rows, :]
                + jnp.where(sides(lane), turned_left(edge[c, t % 2], k * tiles + t), 0.0)
                - mx * dk[c]
                for c in range(3)
            ]
            dy = [
                across_ref[c, k, rows, :] + beside_rows(top, bottom, c, k, t, nz, tiles) - my * dk[c]
                for c in range(3)
            ]
            dz = [mz * dk[c] for c in range(3)]
            lam, mu, keep, gain = (cells_ref[i, k, rows, :] for i in range(1, 5))
            volume = lam * (dx[0] + dy[1] + dz[2])
            mu2 = mu + mu
            rates = (
                volume + mu2 * dx[0],
                volume + mu2 * dy[1],
                volume + mu2 * dz[2],
                mu * (dy[0] + dx[1]),
                mu * (dz[0] + dx[2]),
                mu * (dz[1] + dy[2]),
            )
            for c in range(6):
                kept = keep * memory_ref[c, k, rows, :] + gain * rates[c]
                memory_out[c, k, rows, :] = kept
                stress_out[c, k, rows, :] = stress_ref[c, k, rows, :] + step_size * (
                    rates[c] - kept
                )

    pairs = ((stress_out, stress_hbm), (memory_out, memory_hbm))

    def send(first, count):
        layers = pl.ds(first, count)
        for i, (a, b) in enumerate(pairs):
            pltpu.make_async_copy(a.at[:, layers], b.at[:, layers], sems.at[i]).start()

    inner = nz - 4
    step = next(d for d in (4, 3, 2, 1) if inner % d == 0)

    @pl.loop(0, inner // step)
    def _(j):
        for i in range(step):
            k = 2 + j * step + i
            layer(k, inner_ref, k - 2)
        send(2 + j * step, step)

    depth_halos(n_gz, zb, za, z1_ref, z2_ref)
    outer_depth(vel_ref, zb, za, outer, 3, nz, tiles)
    for spot, k in enumerate((0, 1, nz - 2, nz - 1)):
        layer(k, outer, spot)
        if spot % 2 == 1:
            send(k - 1, 2)
    for i, (a, b) in enumerate(pairs):
        pltpu.make_async_copy(a, b, sems.at[i]).wait()


def in_hbm(value):
    return pltpu.with_memory_space_constraint(value, pltpu.HBM)


def call(kernel, outs, in_specs, scratch=(), name=None, out_specs=None, cost=0.0):
    return pl.pallas_call(
        kernel,
        out_shape=[jax.ShapeDtypeStruct(s, F32) for s in outs],
        in_specs=in_specs,
        out_specs=out_specs or [VM] * len(outs),
        scratch_shapes=list(scratch),
        compiler_params=params(),
        cost_estimate=pl.CostEstimate(flops=int(cost * 6e8), transcendentals=0, bytes_accessed=int(cost * 3.5e6)),
        name=name,
    )


def local(
    sizes, elevation, layer_base, stretch, material, buoyancy, lame_lambda, shear_modulus,
    relax_time, anelastic_weight, velocity, stress, memory,
):
    n_gx, n_gy, n_gz = counts = tuple(sizes[a] for a in ("gx", "gy", "gz"))
    _, nz, ny, nx = velocity.shape
    rows = ny + SUB
    rounds = pair_swaps(sizes, "gz")
    if n_gz == 4:
        piece = lax.ppermute(elevation, tuple(sizes), rounds[0])
    slab = call(
        terrain_piece_kernel,
        [(rows, nx)],
        [HB] * 3,
        [
            pltpu.VMEM(elevation.shape, jnp.int32),
            pltpu.VMEM((1, nz), F32),
            pltpu.VMEM((1, nz), F32),
            DMA((3,)),
        ],
        name="terrain_piece", cost=0.8,
    )(in_hbm(elevation), in_hbm(layer_base[None]), in_hbm(stretch[None]))[0]
    tied = lax.optimization_barrier
    faces = 2 * 3 * nz
    xs = 3 * SUB
    y_rounds = min(2, n_gy - 1) if n_gy > 1 else 1
    z_face = (6, 2, ny, nx)
    if n_gz == 4:
        slab = call(merge_kernel, [(rows, nx)], [VM] * 2, name="merge", cost=0.1)(slab, piece)[0]
        slab, stress = tied((slab, stress))
        slab = slab + lax.ppermute(slab, tuple(sizes), rounds[1])
        layers = slab[ny:]
    elif n_gz & (n_gz - 1):
        slab = lax.psum(slab, "gz")
        layers = slab[ny:]
    else:
        bit = 1
        while bit < n_gz:
            slab = slab + lax.ppermute(slab, "gz", [(i, i ^ bit) for i in range(n_gz)])
            if bit == 1:
                slab, stress = tied((slab, stress))
            bit *= 2
        layers = slab[ny:]
    stress_vm = stress
    low, high, x1, x2, z1, z2, *ys = call(
        pack_kernel,
        [(xs, nx)] * 4 + [z_face] * 2 + [(faces, nx)] * y_rounds,
        [VM],
        name="pack_stress", cost=0.5,
    )(stress)
    z1, z2 = exchange(sizes, "gz", z1, z2)
    ts = call(y_send_kernel, [(SUB, nx)] * y_rounds, [VM], name="y_send", cost=0.02)(slab)
    ts, ys, stress_vm, layers = tied((ts, ys, stress_vm, layers))
    t1, t2 = exchange(sizes, "gy", ts[0], ts[-1])
    y1, y2 = exchange(sizes, "gy", ys[0], ys[-1])
    if n_gz == 4:
        layers = layers + lax.ppermute(layers, tuple(sizes), rounds[0])
    inner_k, along, velocity_vm = call(
        depth_kernel,
        [(6, nz - 4, ny, nx), velocity.shape, velocity.shape],
        [VM, HB],
        [DMA],
        name="depth", cost=2.2,
    )(stress_vm, in_hbm(velocity))
    x1, x2, inner_k = tied((x1, x2, inner_k))
    terrain, x1, x2 = call(
        functools.partial(x_send_kernel, n_gy),
        [(ny + 2 * PAD, nx)] + [(xs + SUB, nx)] * 2,
        [VM] * 5,
        name="x_send", cost=0.1,
    )(slab, t1, t2, x1, x2)
    x1, x2, material = tied((x1, x2, material))
    x1, x2 = exchange(sizes, "gx", x1, x2, True)
    edge = pltpu.VMEM((3, 2, SUB, nx), F32)
    tall = pltpu.VMEM((3, nz, ny + 2 * PAD, nx), F32)

    def depth(comps):
        return [pltpu.VMEM((comps, 2, ny, nx), F32)] * 2

    tables = (buoyancy, lame_lambda, shear_modulus, relax_time, anelastic_weight)
    all_layers = -(-n_gz * nz // SUB) * SUB
    cells, spread = call(
        cell_kernel, [(5, nz, ny, nx), (2, all_layers, nx)], [VM] * 7, name="cells", cost=0.8
    )(layers, material, *[table[None] for table in tables])
    plane, outer_k = call(
        functools.partial(plane_kernel, counts),
        [velocity.shape, (6, 4, ny, nx)],
        [VM] * 6,
        [tall] + depth(6),
        name="planes", cost=0.6,
    )(stress_vm, along, y1, y2, z1, z2)
    plane, cells, x1, x2 = tied((plane, cells, x1, x2))
    factor, mz, slope = call(
        functools.partial(metric_kernel, counts),
        [(nz, ny, nx), (nz, ny, nx), (2, ny, nx)],
        [VM] * 4,
        [pltpu.VMEM((ny + 2 * PAD, nx), F32), pltpu.VMEM((ny + PAD, nx), F32)],
        name="metrics", cost=1.1,
    )(spread, terrain, x1[xs:], x2[xs:])
    vel, vlow, vhigh, vx1, vx2, vz1, vz2, *vys = call(
        functools.partial(velocity_kernel, counts),
        [velocity.shape] + [(xs, nx)] * 4 + [(3, 2, ny, nx)] * 2 + [(faces, nx)] * y_rounds,
        [VM] * 12,
        [edge],
        name="velocity", cost=1.5,
    )(velocity_vm, cells, inner_k, outer_k, plane, factor, mz, slope, x1, x2, low, high)
    vz1, vz2 = exchange(sizes, "gz", vz1, vz2)
    vy1, vy2 = exchange(sizes, "gy", vys[0], vys[-1])
    vx1, vx2 = exchange(sizes, "gx", vx1, vx2)
    vel_next, vel_k, vel_x, vel_y = call(
        velocity_inner_kernel,
        [velocity.shape, (3, nz - 4, ny, nx), velocity.shape, velocity.shape],
        [VM],
        [tall, DMA],
        name="velocity_inner", cost=0.1,
        out_specs=[HB, VM, VM, VM],
    )(vel)
    stress_next, memory_next = call(
        functools.partial(stress_kernel, counts),
        [stress.shape, stress.shape],
        [VM] * 18,
        [edge, pltpu.VMEM((faces + SUB, nx), F32), pltpu.VMEM((faces + SUB, nx), F32)]
        + depth(3)
        + [pltpu.VMEM((3, 4, ny, nx), F32), pltpu.VMEM(stress.shape, F32), pltpu.VMEM(stress.shape, F32)]
        + [DMA((2,))],
        name="stress", cost=2.8,
        out_specs=[HB] * 2,
    )(
        vel, stress_vm, memory, cells, vel_k, vel_x, vel_y, factor, mz, slope, vx1, vx2, vlow, vhigh, vy1, vy2,
        vz1, vz2,
    )
    return vel_next, stress_next, memory_next


def solution(mesh):
    sizes = {a: mesh.shape[a] for a in ("gx", "gy", "gz")}
    field = P(None, "gz", "gy", "gx")
    return jax.shard_map(
        functools.partial(local, sizes),
        mesh=mesh,
        in_specs=(
            P("gy", ("gx", "gz")), P("gz"), P("gz"), P("gz", "gy", "gx"),
            P(), P(), P(), P(), P(), field, field, field,
        ),
        out_specs=(field, field, field),
        check_vma=False,
    )
```

```python
import functools
import jax
import jax.numpy as jnp
import numpy as np
from jax import lax
from jax.experimental import pallas as pl
from jax.experimental.pallas import tpu as pltpu
from jax.sharding import PartitionSpec as P

step_size = 0.3
SUB = 8
PAD = 8
F32 = jnp.float32
params = functools.partial(pltpu.CompilerParams, vmem_limit_bytes=20 * 1024 * 1024)
VM = pl.BlockSpec(memory_space=pltpu.VMEM)
SM = pl.BlockSpec(memory_space=pltpu.SMEM)
HB = pl.BlockSpec(memory_space=pltpu.HBM)
DMA = pltpu.SemaphoreType.DMA


def pair_swaps(sizes, axis):
    names = tuple(sizes)
    shape = tuple(sizes.values())
    index = names.index(axis)
    n = shape[index]
    others = [d for d in (2, 1, 0) if d != index and shape[d] % 2 == 0]
    rounds = []
    for first in (0, 1)[: max(0, min(2, n - 1))]:
        table = []
        for spot in np.ndindex(*shape):
            mate = spot[index] + 1 if spot[index] % 2 == first else spot[index] - 1
            target = list(spot)
            if 0 <= mate < n or axis == "gz":
                target[index] = mate % n
            elif others:
                target[others[0]] ^= 1
            else:
                continue
            table.append((int(np.ravel_multi_index(spot, shape)), int(np.ravel_multi_index(tuple(target), shape))))
        rounds.append(table)
    return rounds


def exchange(sizes, axis, first, second, second_first=False):
    rounds = list(zip((first, second), pair_swaps(sizes, axis)))
    if second_first:
        rounds = rounds[::-1]
    got = [lax.ppermute(v, tuple(sizes), r) for v, r in rounds]
    if second_first:
        got = got[::-1]
    return (got[0], got[-1]) if got else (first, second)


def even(axis):
    return lax.axis_index(axis) % 2 == 0


def from_before(axis, got):
    value = jnp.where(even(axis), got[1], got[0])
    return jnp.where(lax.axis_index(axis) > 0, value, 0.0)


def from_after(axis, n, got):
    value = jnp.where(even(axis), got[0], got[1])
    return jnp.where(lax.axis_index(axis) < n - 1, value, 0.0)


def order(axis, to_after, to_before):
    e = even(axis)
    return jnp.where(e, to_after, to_before), jnp.where(e, to_before, to_after)


def lanes_of(shape):
    return lax.broadcasted_iota(jnp.int32, shape, len(shape) - 1)


def terrain_piece_kernel(elev_hbm, base_hbm, stretch_hbm, out_ref, elev_ref, base_ref, stretch_ref, sems):
    mine = lax.axis_index("gz")
    pairs = ((elev_hbm, elev_ref), (base_hbm, base_ref), (stretch_hbm, stretch_ref))
    copies = [pltpu.make_async_copy(a, b, sems.at[i]) for i, (a, b) in enumerate(pairs)]
    for copy in copies:
        copy.start()
    for copy in copies:
        copy.wait()
    ny, width = elev_ref.shape
    nx = out_ref.shape[1]
    nz = base_ref.shape[1]
    height = elev_ref[...].astype(F32) / 200.0
    wide = jnp.concatenate([height, jnp.zeros((ny, nx - width), F32)], axis=1)
    out_ref[:ny, :] = pltpu.roll(wide, mine * width, 1)
    row = lax.broadcasted_iota(jnp.int32, (SUB, nx), 0)
    fill = jnp.zeros((1, nx - nz), F32)
    base = jnp.concatenate([base_ref[...], fill], axis=1)
    stretch = jnp.concatenate([stretch_ref[...], fill], axis=1)
    both = jnp.where(row == 0, base, jnp.where(row == 1, stretch, 0.0))
    out_ref[ny:, :] = pltpu.roll(both, mine * nz, 1)


def merge_kernel(first_ref, elev_ref, out_ref):
    ny, width = elev_ref.shape
    nx = out_ref.shape[1]
    height = elev_ref[...].astype(F32) / 200.0
    wide = jnp.concatenate([height, jnp.zeros((ny, nx - width), F32)], axis=1)
    mate = lax.axis_index("gz") + jnp.where(even("gz"), 1, -1)
    out_ref[:ny, :] = first_ref[:ny, :] + pltpu.roll(wide, mate * width, 1)
    out_ref[ny:, :] = first_ref[ny:, :]


def pack_sides(field, nz, ny, nx, low_ref, high_ref, out1_ref, out2_ref):
    tiles = ny // SUB
    lane2 = lanes_of((SUB, nx)) // 2
    for c in range(3):
        lo = jnp.zeros((SUB, nx), F32)
        hi = jnp.zeros((SUB, nx), F32)
        for k in range(nz):
            for t in range(tiles):
                m = k * tiles + t
                turned = pltpu.roll(field(c, k, t), (2 * m + 2) % nx, 1)
                hi = jnp.where(lane2 == m, turned, hi)
                lo = jnp.where(lane2 == (m + 1) % (nx // 2), turned, lo)
        at = slice(SUB * c, SUB * c + SUB)
        low_ref[at, :] = lo
        high_ref[at, :] = hi
        out1_ref[at, :], out2_ref[at, :] = order("gx", hi, lo)


def pack_rows(field, nz, ny, y_refs):
    for c in range(3):
        for k in range(nz):
            j = 2 * (c * nz + k)
            both = order("gy", field(c, k, slice(ny - 2, ny)), field(c, k, slice(0, 2)))
            for ref, rows in zip(y_refs, both):
                ref[j : j + 2, :] = rows


def pack_kernel(stress_ref, low_ref, high_ref, out1_ref, out2_ref, z1_ref, z2_ref, *y_refs):
    _, nz, ny, nx = stress_ref.shape
    of_x = (0, 3, 4)
    of_y = (3, 1, 5)
    z1_ref[...], z2_ref[...] = order("gz", stress_ref[:, nz - 2 : nz], stress_ref[:, 0:2])
    pack_sides(
        lambda c, k, t: stress_ref[of_x[c], k, SUB * t : SUB * t + SUB, :],
        nz, ny, nx, low_ref, high_ref, out1_ref, out2_ref,
    )
    pack_rows(lambda c, k, rows: stress_ref[of_y[c], k, rows, :], nz, ny, y_refs)


def y_send_kernel(slab_ref, *out_refs):
    ny = slab_ref.shape[0] - SUB
    both = order("gy", slab_ref[ny - 4 : ny, :], slab_ref[0:4, :])
    for ref, rows in zip(out_refs, both):
        ref[0:4, :] = rows
        ref[4:, :] = jnp.zeros_like(rows)


def x_send_kernel(n_gy, slab_ref, y1_ref, y2_ref, x1_ref, x2_ref, tall_ref, out1_ref, out2_ref):
    ny = slab_ref.shape[0] - SUB
    nx = slab_ref.shape[1]
    xs = x1_ref.shape[0]
    lane4 = lanes_of((SUB, nx)) // 4
    got = (y1_ref[0:4, :], y2_ref[0:4, :])
    tall_ref[: PAD - 4, :] = jnp.zeros((PAD - 4, nx), F32)
    tall_ref[PAD - 4 : PAD, :] = from_before("gy", got)
    tall_ref[PAD : PAD + ny, :] = slab_ref[:ny, :]
    tall_ref[PAD + ny : PAD + ny + 4, :] = from_after("gy", n_gy, got)
    tall_ref[PAD + ny + 4 :, :] = jnp.zeros((PAD - 4, nx), F32)
    lo = jnp.zeros((SUB, nx), F32)
    hi = jnp.zeros((SUB, nx), F32)
    for j in range((ny + 2 * PAD) // SUB):
        tile = tall_ref[SUB * j : SUB * j + SUB, :]
        lo = jnp.where(lane4 == j, pltpu.roll(tile, 4 * j, 1), lo)
        hi = jnp.where(lane4 == j, pltpu.roll(tile, (4 * j + 4) % nx, 1), hi)
    out1_ref[:xs, :] = x1_ref[...]
    out2_ref[:xs, :] = x2_ref[...]
    out1_ref[xs:, :], out2_ref[xs:, :] = order("gx", hi, lo)


def binomial(at):
    return (at(-2) + at(2) + 4.0 * (at(-1) + at(1)) + 6.0 * at(0)) / 16.0


def centred12(at):
    return 8.0 * (at(1) - at(-1)) - (at(2) - at(-2))


def metric_kernel(
    sizes, layers_ref, own, x1_ref, x2_ref, factor_ref, mz_ref, slope_ref, rim, sown,
):
    n_gx = sizes[0]
    gz = lax.axis_index("gz")
    nz, ny, nx = factor_ref.shape
    lane = lanes_of((SUB, nx))
    got = (x1_ref[...], x2_ref[...])
    left, right = from_before("gx", got), from_after("gx", n_gx, got)
    for j in range((ny + 2 * PAD) // SUB):
        rim[SUB * j : SUB * j + SUB, :] = jnp.where(
            lane < nx // 2,
            pltpu.roll(right, (nx - 4 * j) % nx, 1),
            pltpu.roll(left, nx - 4 - 4 * j, 1),
        )
    rows = ny + 4
    tall_own = binomial(lambda s: own[PAD - 2 + s : PAD - 2 + s + rows, :])
    tall_rim = binomial(lambda s: rim[PAD - 2 + s : PAD - 2 + s + rows, :])

    def shifted(a, b, s):
        ln = lanes_of(a.shape)
        cut = (ln < s) if s > 0 else (ln >= nx + s)
        if s > 0:
            mixed_a, mixed_b = jnp.where(cut, b, a), jnp.where(cut, a, b)
        elif s < 0:
            mixed_a, mixed_b = jnp.where(cut, b, a), jnp.where(cut, a, b)
        else:
            return a, b
        return pltpu.roll(mixed_a, (-s) % nx, 1), pltpu.roll(mixed_b, (-s) % nx, 1)

    def padded_rows(a):
        return jnp.concatenate([a, jnp.zeros((SUB - rows % SUB, nx), F32)], axis=0)

    tall_own, tall_rim = padded_rows(tall_own), padded_rows(tall_rim)
    pairs = {s: shifted(tall_own, tall_rim, s) for s in (-2, -1, 0, 1, 2)}
    surf_own = binomial(lambda s: pairs[s][0])
    surf_rim = binomial(lambda s: pairs[s][1])
    sown[...] = surf_own
    slope_ref[1] = centred12(lambda s: sown[2 + s : 2 + s + ny, :]) / 12.0
    pairs2 = {s: shifted(surf_own, surf_rim, s)[0] for s in (-2, -1, 1, 2)}
    along = centred12(lambda s: pairs2[s]) / 12.0
    surface = sown[2 : 2 + ny, :]
    sown[...] = along
    slope_ref[0] = sown[2 : 2 + ny, :]

    def above(slab, total):
        for k in range(nz):
            at = pl.ds(slab * nz + k, 1)
            s = layers_ref[1, at, :]
            total = total + (s * layers_ref[0, at, :]) * jnp.exp(s * surface)
        return total

    total = lax.fori_loop(0, gz, above, jnp.zeros((ny, nx), F32))
    for k in range(nz):
        at = pl.ds(gz * nz + k, 1)
        s = layers_ref[1, at, :]
        thickness = layers_ref[0, at, :] * jnp.exp(s * surface)
        weighted = s * thickness
        mz = 1.0 / thickness
        lift = total + 0.5 * weighted
        total = total + weighted
        mz_ref[k] = mz
        factor_ref[k] = (lift - 1.0) * mz

def edge_terms(got_left, got_right, low, high):
    dl = got_left - high
    dr = got_right - low
    nx = dl.shape[-1]
    lane = lanes_of(dl.shape)
    even = lane % 2 == 0
    dl = pltpu.roll(dl, 2, 1)
    dr = pltpu.roll(dr, nx - 2, 1)
    to_low = jnp.where(even, dl - 8.0 * pltpu.roll(dl, nx - 1, 1), dl)
    to_high = jnp.where(even, -dr, 8.0 * pltpu.roll(dr, 1, 1) - dr)
    second = (lane // 2) % 2 == 1
    return jnp.where(second, to_low, to_high), jnp.where(second, to_high, to_low)


def turned_left(edges, m):
    nx = edges.shape[-1]
    shift = (2 * nx - 2 - 2 * m) % nx if isinstance(m, int) else 2 * nx - 2 - 2 * m
    return pltpu.roll(edges, shift, 1)


def sides(lane):
    return (lane < 2) | (lane >= lane.shape[-1] - 2)


def x_weights(nx):
    ahead = (
        lax.broadcasted_iota(jnp.int32, (nx, nx), 0) - lax.broadcasted_iota(jnp.int32, (nx, nx), 1)
    )
    weights = jnp.zeros((nx, nx), F32)
    for offset, weight in ((1, 8.0), (-1, -8.0), (2, -1.0), (-2, 1.0)):
        weights = jnp.where((ahead == offset) | (ahead == offset + nx) | (ahead == offset - nx), weight, weights)
    weights = weights.astype(jnp.bfloat16)
    return jnp.concatenate([weights] * 3, axis=0)


def periodic_x(value, weights):
    high = value.astype(jnp.bfloat16)
    rest = value - high.astype(F32)
    middle = rest.astype(jnp.bfloat16)
    low = (rest - middle.astype(F32)).astype(jnp.bfloat16)
    return jnp.dot(
        jnp.concatenate([high, middle, low], axis=1), weights, preferred_element_type=F32
    )


def along_all(ref, comps, out_ref, group=16):
    _, nz, ny, nx = out_ref.shape
    group = next(d for d in range(group, 0, -1) if nz % d == 0)
    weights = x_weights(nx)

    @pl.loop(0, nz // group)
    def _(j):
        layers = pl.ds(j * group, group)
        rows = [ref[c, layers].reshape(group * ny, nx) for c in comps]
        result = periodic_x(jnp.concatenate(rows, axis=0), weights)
        for i in range(len(comps)):
            part = result[i * group * ny : (i + 1) * group * ny]
            out_ref[i, layers] = part.reshape(group, ny, nx)


def lookup(row, tile):
    table = jnp.broadcast_to(row, tile.shape)
    return jnp.take_along_axis(table, tile, axis=1, mode="promise_in_bounds")


def table_rows(refs, nx):
    n = refs[0].shape[1]
    return [jnp.concatenate([r, jnp.zeros((1, nx - n), F32)], axis=1) for r in refs]


def fill_edges(n_gx, edge_ref, x1_ref, x2_ref, low_ref, high_ref):
    for c in range(3):
        at = slice(SUB * c, SUB * c + SUB)
        got = (x1_ref[at, :], x2_ref[at, :])
        first, second = edge_terms(
            from_before("gx", got), from_after("gx", n_gx, got), low_ref[at, :], high_ref[at, :]
        )
        edge_ref[c, 0] = first
        edge_ref[c, 1] = second


def fill_rows(n_gy, tall, field, y1_ref, y2_ref, nz, ny, layers):
    for c in range(3):
        for spot, k in enumerate(layers):
            j = 2 * (c * nz + k)
            got = (y1_ref[j : j + 2, :], y2_ref[j : j + 2, :])
            tall[c, spot, PAD : PAD + ny, :] = field(c, k)
            tall[c, spot, PAD - 2 : PAD, :] = from_before("gy", got)
            tall[c, spot, PAD + ny : PAD + ny + 2, :] = from_after("gy", n_gy, got)


def depth_halos(n_gz, zb, za, z1_ref, z2_ref):
    got = (z1_ref[...], z2_ref[...])
    zb[...] = from_before("gz", got)
    za[...] = from_after("gz", n_gz, got)


def over(low, high, most, body):
    count = high - low
    group = next(d for d in range(most, 0, -1) if count % d == 0)

    @pl.loop(0, count // group)
    def _(j):
        for i in range(group):
            body(low + j * group + i)


def tile_rows(t):
    return slice(SUB * t, SUB * t + SUB)


def row_difference(tall, c, spot, t):
    return centred12(lambda s: tall[c, spot, PAD + SUB * t + s : PAD + SUB * t + s + SUB, :])


def inner_depth(ref, out_ref, comps, k, tiles):
    for t in range(tiles):
        for c in range(comps):
            out_ref[c, k - 2, tile_rows(t), :] = centred12(lambda s: ref[c, k + s, tile_rows(t), :])


def outer_depth(ref, zb, za, out_ref, comps, nz, tiles):
    for spot, k in enumerate((0, 1, nz - 2, nz - 1)):
        for t in range(tiles):
            for c in range(comps):

                def at(s):
                    if k + s < 0:
                        return zb[c, k + s + 2, tile_rows(t), :]
                    if k + s >= nz:
                        return za[c, k + s - nz, tile_rows(t), :]
                    return ref[c, k + s, tile_rows(t), :]

                out_ref[c, spot, tile_rows(t), :] = centred12(at)


def cell_kernel(
    layers_ref, material_ref, buoy_ref, lam_ref, mu_ref, relax_ref, weight_ref, cells_ref, spread_ref
):
    lane = lanes_of((SUB, layers_ref.shape[1]))
    sub = lax.broadcasted_iota(jnp.int32, lane.shape, 0)
    for i in range(2):
        row = jnp.broadcast_to(layers_ref[i : i + 1, :], lane.shape)
        for g in range(spread_ref.shape[1] // SUB):
            one = jnp.sum(jnp.where(lane == SUB * g + sub, row, 0.0), axis=1, keepdims=True)
            spread_ref[i, tile_rows(g), :] = jnp.broadcast_to(one, lane.shape)
    nz, ny, nx = material_ref.shape
    keep = jnp.exp(-step_size / relax_ref[...])
    tables = table_rows(
        [
            buoy_ref[...] * (step_size / 12.0), lam_ref[...] / 12.0, mu_ref[...] / 12.0, keep,
            (1.0 - keep) * weight_ref[...],
        ],
        nx,
    )

    def layer(k):
        for t in range(ny // SUB):
            kind = material_ref[k, tile_rows(t), :]
            for i, table in enumerate(tables):
                cells_ref[i, k, tile_rows(t), :] = lookup(table, kind)

    over(0, nz, 8, layer)


def depth_kernel(stress_ref, velocity_hbm, depth_ref, along_ref, velocity_ref, sem):
    load = pltpu.make_async_copy(velocity_hbm, velocity_ref, sem)
    load.start()
    _, nz, ny, _ = stress_ref.shape
    along_all(stress_ref, (0, 3, 4), along_ref)
    over(2, nz - 2, 4, lambda k: inner_depth(stress_ref, depth_ref, 6, k, ny // SUB))
    load.wait()


def plane_kernel(
    sizes, stress_ref, along_ref, y1_ref, y2_ref, z1_ref, z2_ref, plane_ref, outer_ref, tall, zb, za
):
    depth_halos(sizes[2], zb, za, z1_ref, z2_ref)
    outer_depth(stress_ref, zb, za, outer_ref, 6, stress_ref.shape[1], stress_ref.shape[2] // SUB)
    _, nz, ny, nx = stress_ref.shape
    tiles = ny // SUB
    of_y = (3, 1, 5)
    fill_rows(sizes[1], tall, lambda c, k: stress_ref[of_y[c], k], y1_ref, y2_ref, nz, ny, range(nz))

    def layer(k):
        for t in range(tiles):
            for c in range(3):
                plane_ref[c, k, tile_rows(t), :] = along_ref[
                    c, k, tile_rows(t), :
                ] + row_difference(tall, c, k, t)

    over(0, nz, 4, layer)


def velocity_kernel(
    sizes, velocity_ref, cells_ref, inner_ref, outer_ref, plane_ref, factor_ref, mz_ref, slope_ref,
    x1_ref, x2_ref, low_ref, high_ref, out_ref, vlow_ref, vhigh_ref, vx1_ref, vx2_ref, vz1_ref, vz2_ref,
    *rest,
):
    *vy_refs, edge = rest
    _, nz, ny, nx = velocity_ref.shape
    tiles = ny // SUB
    lane = lanes_of((SUB, nx))
    fill_edges(sizes[0], edge, x1_ref, x2_ref, low_ref, high_ref)

    def layer(k, depth_ref, spot):
        for t in range(tiles):
            rows = tile_rows(t)
            b = cells_ref[0, k, rows, :]
            factor = factor_ref[k, rows, :]
            mz = mz_ref[k, rows, :]
            mx = slope_ref[0, rows, :] * factor
            my = slope_ref[1, rows, :] * factor
            gk = [depth_ref[c, spot, rows, :] for c in range(6)]
            beside = [
                plane_ref[c, k, rows, :]
                + jnp.where(sides(lane), turned_left(edge[c, t % 2], k * tiles + t), 0.0)
                for c in range(3)
            ]
            accel = (
                beside[0] - mx * gk[0] - my * gk[3] + mz * gk[4],
                beside[1] - mx * gk[3] - my * gk[1] + mz * gk[5],
                beside[2] - mx * gk[4] - my * gk[5] + mz * gk[2],
            )
            for c in range(3):
                out_ref[c, k, rows, :] = velocity_ref[c, k, rows, :] + b * accel[c]

    for spot, k in enumerate((0, 1, nz - 2, nz - 1)):
        layer(k, outer_ref, spot)

    over(2, nz - 2, 12, lambda k: layer(k, inner_ref, k - 2))
    pack_sides(
        lambda c, k, t: out_ref[c, k, tile_rows(t), :], nz, ny, nx, vlow_ref, vhigh_ref, vx1_ref, vx2_ref
    )
    pack_rows(lambda c, k, rows: out_ref[c, k, rows, :], nz, ny, vy_refs)
    vz1_ref[...], vz2_ref[...] = order("gz", out_ref[:, nz - 2 : nz], out_ref[:, 0:2])


def velocity_inner_kernel(vel_ref, vel_hbm, depth_ref, along_ref, across_ref, tall, sem):
    store = pltpu.make_async_copy(vel_ref, vel_hbm, sem)
    store.start()
    _, nz, ny, nx = vel_ref.shape
    tiles = ny // SUB

    along_all(vel_ref, (0, 1, 2), along_ref)
    over(2, nz - 2, 4, lambda k: inner_depth(vel_ref, depth_ref, 3, k, tiles))
    nothing = jnp.zeros((2, nx), F32)
    for c in range(3):
        for k in range(nz):
            tall[c, k, PAD : PAD + ny, :] = vel_ref[c, k]
            tall[c, k, PAD - 2 : PAD, :] = nothing
            tall[c, k, PAD + ny : PAD + ny + 2, :] = nothing

    def across(k):
        for t in range(tiles):
            for c in range(3):
                across_ref[c, k, tile_rows(t), :] = row_difference(tall, c, k, t)

    over(0, nz, 4, across)
    store.wait()


def fill_sides(n_gy, top, bottom, y1_ref, y2_ref):
    count = y1_ref.shape[0]
    got = (y1_ref[...], y2_ref[...])
    even_row = lax.broadcasted_iota(jnp.int32, got[0].shape, 0) % 2 == 0
    empty = jnp.zeros((SUB, y1_ref.shape[1]), F32)
    before, after = from_before("gy", got), from_after("gy", n_gy, got)
    top[:count, :] = before
    top[count:, :] = empty
    bottom[:SUB, :] = empty
    bottom[SUB:, :] = after
    top[:count, :] = jnp.where(even_row, before - 8.0 * top[1 : count + 1, :], before)
    bottom[SUB:, :] = jnp.where(even_row, -after, 8.0 * bottom[SUB - 1 : SUB + count - 1, :] - after)


def beside_rows(top, bottom, c, k, t, nz, tiles):
    j = 2 * (c * nz + k)
    row = lax.broadcasted_iota(jnp.int32, (SUB, top.shape[1]), 0)
    added = 0.0
    if t == 0:
        added = jnp.where(row < 2, top[pl.ds(j, SUB), :], 0.0)
    if t == tiles - 1:
        added = added + jnp.where(row >= SUB - 2, bottom[pl.ds(j + 2, SUB), :], 0.0)
    return added


def stress_kernel(
    sizes, vel_ref, stress_ref, memory_ref, cells_ref, inner_ref, along_ref, across_ref, factor_ref, mz_ref,
    slope_ref, x1_ref, x2_ref, low_ref, high_ref, y1_ref, y2_ref, z1_ref, z2_ref,
    stress_hbm, memory_hbm, edge, top, bottom, zb, za, outer, stress_out, memory_out, sems,
):
    n_gx, n_gy, n_gz = sizes
    _, nz, ny, nx = vel_ref.shape
    tiles = ny // SUB
    lane = lanes_of((SUB, nx))
    fill_edges(n_gx, edge, x1_ref, x2_ref, low_ref, high_ref)
    fill_sides(n_gy, top, bottom, y1_ref, y2_ref)

    def layer(k, depth_ref, spot):
        for t in range(tiles):
            rows = tile_rows(t)
            factor = factor_ref[k, rows, :]
            mz = mz_ref[k, rows, :]
            mx = slope_ref[0, rows, :] * factor
            my = slope_ref[1, rows, :] * factor
            dk = [depth_ref[c, spot, rows, :] for c in range(3)]
            dx = [
                along_ref[c, k, rows, :]
                + jnp.where(sides(lane), turned_left(edge[c, t % 2], k * tiles + t), 0.0)
                - mx * dk[c]
                for c in range(3)
            ]
            dy = [
                across_ref[c, k, rows, :] + beside_rows(top, bottom, c, k, t, nz, tiles) - my * dk[c]
                for c in range(3)
            ]
            dz = [mz * dk[c] for c in range(3)]
            lam, mu, keep, gain = (cells_ref[i, k, rows, :] for i in range(1, 5))
            volume = lam * (dx[0] + dy[1] + dz[2])
            mu2 = mu + mu
            rates = (
                volume + mu2 * dx[0],
                volume + mu2 * dy[1],
                volume + mu2 * dz[2],
                mu * (dy[0] + dx[1]),
                mu * (dz[0] + dx[2]),
                mu * (dz[1] + dy[2]),
            )
            for c in range(6):
                kept = keep * memory_ref[c, k, rows, :] + gain * rates[c]
                memory_out[c, k, rows, :] = kept
                stress_out[c, k, rows, :] = stress_ref[c, k, rows, :] + step_size * (
                    rates[c] - kept
                )

    pairs = ((stress_out, stress_hbm), (memory_out, memory_hbm))

    def send(first, count):
        layers = pl.ds(first, count)
        for i, (a, b) in enumerate(pairs):
            pltpu.make_async_copy(a.at[:, layers], b.at[:, layers], sems.at[i]).start()

    inner = nz - 4
    step = next(d for d in (4, 3, 2, 1) if inner % d == 0)

    for k in range(2, nz - 2):
        layer(k, inner_ref, k - 2)
        if (k - 1) % 2 == 0 or k == nz - 3:
            count = (k - 2) % 2 + 1
            send(k + 1 - count, count)

    depth_halos(n_gz, zb, za, z1_ref, z2_ref)
    outer_depth(vel_ref, zb, za, outer, 3, nz, tiles)
    for spot, k in enumerate((0, 1, nz - 2, nz - 1)):
        layer(k, outer, spot)
        if spot % 2 == 1:
            send(k - 1, 2)
    for i, (a, b) in enumerate(pairs):
        pltpu.make_async_copy(a, b, sems.at[i]).wait()


def in_hbm(value):
    return pltpu.with_memory_space_constraint(value, pltpu.HBM)


def call(kernel, outs, in_specs, scratch=(), name=None, out_specs=None, cost=0.0):
    return pl.pallas_call(
        kernel,
        out_shape=[jax.ShapeDtypeStruct(s, F32) for s in outs],
        in_specs=in_specs,
        out_specs=out_specs or [VM] * len(outs),
        scratch_shapes=list(scratch),
        compiler_params=params(),
        cost_estimate=pl.CostEstimate(flops=int(cost * 6e8), transcendentals=0, bytes_accessed=int(cost * 3.5e6)),
        name=name,
    )


def local(
    sizes, elevation, layer_base, stretch, material, buoyancy, lame_lambda, shear_modulus,
    relax_time, anelastic_weight, velocity, stress, memory,
):
    n_gx, n_gy, n_gz = counts = tuple(sizes[a] for a in ("gx", "gy", "gz"))
    _, nz, ny, nx = velocity.shape
    rows = ny + SUB
    rounds = pair_swaps(sizes, "gz")
    if n_gz == 4:
        piece = lax.ppermute(elevation, tuple(sizes), rounds[0])
    slab = call(
        terrain_piece_kernel,
        [(rows, nx)],
        [HB] * 3,
        [
            pltpu.VMEM(elevation.shape, jnp.int32),
            pltpu.VMEM((1, nz), F32),
            pltpu.VMEM((1, nz), F32),
            DMA((3,)),
        ],
        name="terrain_piece", cost=0.8,
    )(in_hbm(elevation), in_hbm(layer_base[None]), in_hbm(stretch[None]))[0]
    tied = lax.optimization_barrier
    faces = 2 * 3 * nz
    xs = 3 * SUB
    y_rounds = min(2, n_gy - 1) if n_gy > 1 else 1
    z_face = (6, 2, ny, nx)
    if n_gz == 4:
        slab = call(merge_kernel, [(rows, nx)], [VM] * 2, name="merge", cost=0.1)(slab, piece)[0]
        slab, stress = tied((slab, stress))
        slab = slab + lax.ppermute(slab, tuple(sizes), rounds[1])
        layers = slab[ny:]
    elif n_gz & (n_gz - 1):
        slab = lax.psum(slab, "gz")
        layers = slab[ny:]
    else:
        bit = 1
        while bit < n_gz:
            slab = slab + lax.ppermute(slab, "gz", [(i, i ^ bit) for i in range(n_gz)])
            if bit == 1:
                slab, stress = tied((slab, stress))
            bit *= 2
        layers = slab[ny:]
    stress_vm = stress
    low, high, x1, x2, z1, z2, *ys = call(
        pack_kernel,
        [(xs, nx)] * 4 + [z_face] * 2 + [(faces, nx)] * y_rounds,
        [VM],
        name="pack_stress", cost=0.5,
    )(stress)
    z1, z2 = exchange(sizes, "gz", z1, z2)
    ts = call(y_send_kernel, [(SUB, nx)] * y_rounds, [VM], name="y_send", cost=0.02)(slab)
    ts, ys, stress_vm, layers = tied((ts, ys, stress_vm, layers))
    t1, t2 = exchange(sizes, "gy", ts[0], ts[-1])
    y1, y2 = exchange(sizes, "gy", ys[0], ys[-1])
    if n_gz == 4:
        layers = layers + lax.ppermute(layers, tuple(sizes), rounds[0])
    inner_k, along, velocity_vm = call(
        depth_kernel,
        [(6, nz - 4, ny, nx), velocity.shape, velocity.shape],
        [VM, HB],
        [DMA],
        name="depth", cost=2.2,
    )(stress_vm, in_hbm(velocity))
    x1, x2, inner_k = tied((x1, x2, inner_k))
    terrain, x1, x2 = call(
        functools.partial(x_send_kernel, n_gy),
        [(ny + 2 * PAD, nx)] + [(xs + SUB, nx)] * 2,
        [VM] * 5,
        name="x_send", cost=0.1,
    )(slab, t1, t2, x1, x2)
    x1, x2, material = tied((x1, x2, material))
    x1, x2 = exchange(sizes, "gx", x1, x2, True)
    edge = pltpu.VMEM((3, 2, SUB, nx), F32)
    tall = pltpu.VMEM((3, nz, ny + 2 * PAD, nx), F32)

    def depth(comps):
        return [pltpu.VMEM((comps, 2, ny, nx), F32)] * 2

    tables = (buoyancy, lame_lambda, shear_modulus, relax_time, anelastic_weight)
    all_layers = -(-n_gz * nz // SUB) * SUB
    cells, spread = call(
        cell_kernel, [(5, nz, ny, nx), (2, all_layers, nx)], [VM] * 7, name="cells", cost=0.8
    )(layers, material, *[table[None] for table in tables])
    plane, outer_k = call(
        functools.partial(plane_kernel, counts),
        [velocity.shape, (6, 4, ny, nx)],
        [VM] * 6,
        [tall] + depth(6),
        name="planes", cost=0.6,
    )(stress_vm, along, y1, y2, z1, z2)
    plane, cells, x1, x2 = tied((plane, cells, x1, x2))
    factor, mz, slope = call(
        functools.partial(metric_kernel, counts),
        [(nz, ny, nx), (nz, ny, nx), (2, ny, nx)],
        [VM] * 4,
        [pltpu.VMEM((ny + 2 * PAD, nx), F32), pltpu.VMEM((ny + PAD, nx), F32)],
        name="metrics", cost=1.1,
    )(spread, terrain, x1[xs:], x2[xs:])
    vel, vlow, vhigh, vx1, vx2, vz1, vz2, *vys = call(
        functools.partial(velocity_kernel, counts),
        [velocity.shape] + [(xs, nx)] * 4 + [(3, 2, ny, nx)] * 2 + [(faces, nx)] * y_rounds,
        [VM] * 12,
        [edge],
        name="velocity", cost=1.5,
    )(velocity_vm, cells, inner_k, outer_k, plane, factor, mz, slope, x1, x2, low, high)
    vz1, vz2 = exchange(sizes, "gz", vz1, vz2)
    vy1, vy2 = exchange(sizes, "gy", vys[0], vys[-1])
    vx1, vx2 = exchange(sizes, "gx", vx1, vx2)
    vel_next, vel_k, vel_x, vel_y = call(
        velocity_inner_kernel,
        [velocity.shape, (3, nz - 4, ny, nx), velocity.shape, velocity.shape],
        [VM],
        [tall, DMA],
        name="velocity_inner", cost=0.1,
        out_specs=[HB, VM, VM, VM],
    )(vel)
    stress_next, memory_next = call(
        functools.partial(stress_kernel, counts),
        [stress.shape, stress.shape],
        [VM] * 18,
        [edge, pltpu.VMEM((faces + SUB, nx), F32), pltpu.VMEM((faces + SUB, nx), F32)]
        + depth(3)
        + [pltpu.VMEM((3, 4, ny, nx), F32), pltpu.VMEM(stress.shape, F32), pltpu.VMEM(stress.shape, F32)]
        + [DMA((2,))],
        name="stress", cost=2.8,
        out_specs=[HB] * 2,
    )(
        vel, stress_vm, memory, cells, vel_k, vel_x, vel_y, factor, mz, slope, vx1, vx2, vlow, vhigh, vy1, vy2,
        vz1, vz2,
    )
    return vel_next, stress_next, memory_next


def solution(mesh):
    sizes = {a: mesh.shape[a] for a in ("gx", "gy", "gz")}
    field = P(None, "gz", "gy", "gx")
    return jax.shard_map(
        functools.partial(local, sizes),
        mesh=mesh,
        in_specs=(
            P("gy", ("gx", "gz")), P("gz"), P("gz"), P("gz", "gy", "gx"),
            P(), P(), P(), P(), P(), field, field, field,
        ),
        out_specs=(field, field, field),
        check_vma=False,
    )
```

```python
import functools
import jax
import jax.numpy as jnp
import numpy as np
from jax import lax
from jax.experimental import pallas as pl
from jax.experimental.pallas import tpu as pltpu
from jax.sharding import PartitionSpec as P

step_size = 0.3
SUB = 8
PAD = 8
F32 = jnp.float32
params = functools.partial(pltpu.CompilerParams, vmem_limit_bytes=20 * 1024 * 1024)
VM = pl.BlockSpec(memory_space=pltpu.VMEM)
SM = pl.BlockSpec(memory_space=pltpu.SMEM)
HB = pl.BlockSpec(memory_space=pltpu.HBM)
DMA = pltpu.SemaphoreType.DMA


def pair_swaps(sizes, axis):
    names = tuple(sizes)
    shape = tuple(sizes.values())
    index = names.index(axis)
    n = shape[index]
    others = [d for d in (2, 1, 0) if d != index and shape[d] % 2 == 0]
    rounds = []
    for first in (0, 1)[: max(0, min(2, n - 1))]:
        table = []
        for spot in np.ndindex(*shape):
            mate = spot[index] + 1 if spot[index] % 2 == first else spot[index] - 1
            target = list(spot)
            if 0 <= mate < n or axis == "gz":
                target[index] = mate % n
            elif others:
                target[others[0]] ^= 1
            else:
                continue
            table.append((int(np.ravel_multi_index(spot, shape)), int(np.ravel_multi_index(tuple(target), shape))))
        rounds.append(table)
    return rounds


def exchange(sizes, axis, first, second, second_first=False):
    rounds = list(zip((first, second), pair_swaps(sizes, axis)))
    if second_first:
        rounds = rounds[::-1]
    got = [lax.ppermute(v, tuple(sizes), r) for v, r in rounds]
    if second_first:
        got = got[::-1]
    return (got[0], got[-1]) if got else (first, second)


def even(axis):
    return lax.axis_index(axis) % 2 == 0


def from_before(axis, got):
    value = jnp.where(even(axis), got[1], got[0])
    return jnp.where(lax.axis_index(axis) > 0, value, 0.0)


def from_after(axis, n, got):
    value = jnp.where(even(axis), got[0], got[1])
    return jnp.where(lax.axis_index(axis) < n - 1, value, 0.0)


def order(axis, to_after, to_before):
    e = even(axis)
    return jnp.where(e, to_after, to_before), jnp.where(e, to_before, to_after)


def lanes_of(shape):
    return lax.broadcasted_iota(jnp.int32, shape, len(shape) - 1)


def terrain_piece_kernel(elev_hbm, base_hbm, stretch_hbm, out_ref, elev_ref, base_ref, stretch_ref, sems):
    mine = lax.axis_index("gz")
    pairs = ((elev_hbm, elev_ref), (base_hbm, base_ref), (stretch_hbm, stretch_ref))
    copies = [pltpu.make_async_copy(a, b, sems.at[i]) for i, (a, b) in enumerate(pairs)]
    for copy in copies:
        copy.start()
    for copy in copies:
        copy.wait()
    ny, width = elev_ref.shape
    nx = out_ref.shape[1]
    nz = base_ref.shape[1]
    height = elev_ref[...].astype(F32) / 200.0
    wide = jnp.concatenate([height, jnp.zeros((ny, nx - width), F32)], axis=1)
    out_ref[:ny, :] = pltpu.roll(wide, mine * width, 1)
    row = lax.broadcasted_iota(jnp.int32, (SUB, nx), 0)
    fill = jnp.zeros((1, nx - nz), F32)
    base = jnp.concatenate([base_ref[...], fill], axis=1)
    stretch = jnp.concatenate([stretch_ref[...], fill], axis=1)
    both = jnp.where(row == 0, base, jnp.where(row == 1, stretch, 0.0))
    out_ref[ny:, :] = pltpu.roll(both, mine * nz, 1)


def merge_kernel(first_ref, elev_ref, out_ref):
    ny, width = elev_ref.shape
    nx = out_ref.shape[1]
    height = elev_ref[...].astype(F32) / 200.0
    wide = jnp.concatenate([height, jnp.zeros((ny, nx - width), F32)], axis=1)
    mate = lax.axis_index("gz") + jnp.where(even("gz"), 1, -1)
    out_ref[:ny, :] = first_ref[:ny, :] + pltpu.roll(wide, mate * width, 1)
    out_ref[ny:, :] = first_ref[ny:, :]


def pack_sides(field, nz, ny, nx, low_ref, high_ref, out1_ref, out2_ref):
    tiles = ny // SUB
    lane2 = lanes_of((SUB, nx)) // 2
    for c in range(3):
        lo = jnp.zeros((SUB, nx), F32)
        hi = jnp.zeros((SUB, nx), F32)
        for k in range(nz):
            for t in range(tiles):
                m = k * tiles + t
                turned = pltpu.roll(field(c, k, t), (2 * m + 2) % nx, 1)
                hi = jnp.where(lane2 == m, turned, hi)
                lo = jnp.where(lane2 == (m + 1) % (nx // 2), turned, lo)
        at = slice(SUB * c, SUB * c + SUB)
        low_ref[at, :] = lo
        high_ref[at, :] = hi
        out1_ref[at, :], out2_ref[at, :] = order("gx", hi, lo)


def pack_rows(field, nz, ny, y_refs):
    for c in range(3):
        for k in range(nz):
            j = 2 * (c * nz + k)
            both = order("gy", field(c, k, slice(ny - 2, ny)), field(c, k, slice(0, 2)))
            for ref, rows in zip(y_refs, both):
                ref[j : j + 2, :] = rows


def pack_kernel(stress_ref, low_ref, high_ref, out1_ref, out2_ref, z1_ref, z2_ref, *y_refs):
    _, nz, ny, nx = stress_ref.shape
    of_x = (0, 3, 4)
    of_y = (3, 1, 5)
    z1_ref[...], z2_ref[...] = order("gz", stress_ref[:, nz - 2 : nz], stress_ref[:, 0:2])
    pack_sides(
        lambda c, k, t: stress_ref[of_x[c], k, SUB * t : SUB * t + SUB, :],
        nz, ny, nx, low_ref, high_ref, out1_ref, out2_ref,
    )
    pack_rows(lambda c, k, rows: stress_ref[of_y[c], k, rows, :], nz, ny, y_refs)


def y_send_kernel(slab_ref, *out_refs):
    ny = slab_ref.shape[0] - SUB
    both = order("gy", slab_ref[ny - 4 : ny, :], slab_ref[0:4, :])
    for ref, rows in zip(out_refs, both):
        ref[0:4, :] = rows
        ref[4:, :] = jnp.zeros_like(rows)


def x_send_kernel(n_gy, slab_ref, y1_ref, y2_ref, x1_ref, x2_ref, tall_ref, out1_ref, out2_ref):
    ny = slab_ref.shape[0] - SUB
    nx = slab_ref.shape[1]
    xs = x1_ref.shape[0]
    lane4 = lanes_of((SUB, nx)) // 4
    got = (y1_ref[0:4, :], y2_ref[0:4, :])
    tall_ref[: PAD - 4, :] = jnp.zeros((PAD - 4, nx), F32)
    tall_ref[PAD - 4 : PAD, :] = from_before("gy", got)
    tall_ref[PAD : PAD + ny, :] = slab_ref[:ny, :]
    tall_ref[PAD + ny : PAD + ny + 4, :] = from_after("gy", n_gy, got)
    tall_ref[PAD + ny + 4 :, :] = jnp.zeros((PAD - 4, nx), F32)
    lo = jnp.zeros((SUB, nx), F32)
    hi = jnp.zeros((SUB, nx), F32)
    for j in range((ny + 2 * PAD) // SUB):
        tile = tall_ref[SUB * j : SUB * j + SUB, :]
        lo = jnp.where(lane4 == j, pltpu.roll(tile, 4 * j, 1), lo)
        hi = jnp.where(lane4 == j, pltpu.roll(tile, (4 * j + 4) % nx, 1), hi)
    out1_ref[:xs, :] = x1_ref[...]
    out2_ref[:xs, :] = x2_ref[...]
    out1_ref[xs:, :], out2_ref[xs:, :] = order("gx", hi, lo)


def binomial(at):
    return (at(-2) + at(2) + 4.0 * (at(-1) + at(1)) + 6.0 * at(0)) / 16.0


def centred12(at):
    return 8.0 * (at(1) - at(-1)) - (at(2) - at(-2))


def metric_kernel(
    sizes, layers_ref, own, x1_ref, x2_ref, factor_ref, mz_ref, slope_ref, rim, sown,
):
    n_gx = sizes[0]
    gz = lax.axis_index("gz")
    nz, ny, nx = factor_ref.shape
    lane = lanes_of((SUB, nx))
    got = (x1_ref[...], x2_ref[...])
    left, right = from_before("gx", got), from_after("gx", n_gx, got)
    for j in range((ny + 2 * PAD) // SUB):
        rim[SUB * j : SUB * j + SUB, :] = jnp.where(
            lane < nx // 2,
            pltpu.roll(right, (nx - 4 * j) % nx, 1),
            pltpu.roll(left, nx - 4 - 4 * j, 1),
        )
    rows = ny + 4
    tall_own = binomial(lambda s: own[PAD - 2 + s : PAD - 2 + s + rows, :])
    tall_rim = binomial(lambda s: rim[PAD - 2 + s : PAD - 2 + s + rows, :])

    def shifted(a, b, s):
        ln = lanes_of(a.shape)
        cut = (ln < s) if s > 0 else (ln >= nx + s)
        if s > 0:
            mixed_a, mixed_b = jnp.where(cut, b, a), jnp.where(cut, a, b)
        elif s < 0:
            mixed_a, mixed_b = jnp.where(cut, b, a), jnp.where(cut, a, b)
        else:
            return a, b
        return pltpu.roll(mixed_a, (-s) % nx, 1), pltpu.roll(mixed_b, (-s) % nx, 1)

    def padded_rows(a):
        return jnp.concatenate([a, jnp.zeros((SUB - rows % SUB, nx), F32)], axis=0)

    tall_own, tall_rim = padded_rows(tall_own), padded_rows(tall_rim)
    pairs = {s: shifted(tall_own, tall_rim, s) for s in (-2, -1, 0, 1, 2)}
    surf_own = binomial(lambda s: pairs[s][0])
    surf_rim = binomial(lambda s: pairs[s][1])
    sown[...] = surf_own
    slope_ref[1] = centred12(lambda s: sown[2 + s : 2 + s + ny, :]) / 12.0
    pairs2 = {s: shifted(surf_own, surf_rim, s)[0] for s in (-2, -1, 1, 2)}
    along = centred12(lambda s: pairs2[s]) / 12.0
    surface = sown[2 : 2 + ny, :]
    sown[...] = along
    slope_ref[0] = sown[2 : 2 + ny, :]

    def above(slab, total):
        for k in range(nz):
            at = pl.ds(slab * nz + k, 1)
            s = layers_ref[1, at, :]
            total = total + (s * layers_ref[0, at, :]) * jnp.exp(s * surface)
        return total

    total = lax.fori_loop(0, gz, above, jnp.zeros((ny, nx), F32))
    for k in range(nz):
        at = pl.ds(gz * nz + k, 1)
        s = layers_ref[1, at, :]
        thickness = layers_ref[0, at, :] * jnp.exp(s * surface)
        weighted = s * thickness
        mz = 1.0 / thickness
        lift = total + 0.5 * weighted
        total = total + weighted
        mz_ref[k] = mz
        factor_ref[k] = (lift - 1.0) * mz

def edge_terms(got_left, got_right, low, high):
    dl = got_left - high
    dr = got_right - low
    nx = dl.shape[-1]
    lane = lanes_of(dl.shape)
    even = lane % 2 == 0
    dl = pltpu.roll(dl, 2, 1)
    dr = pltpu.roll(dr, nx - 2, 1)
    to_low = jnp.where(even, dl - 8.0 * pltpu.roll(dl, nx - 1, 1), dl)
    to_high = jnp.where(even, -dr, 8.0 * pltpu.roll(dr, 1, 1) - dr)
    second = (lane // 2) % 2 == 1
    return jnp.where(second, to_low, to_high), jnp.where(second, to_high, to_low)


def turned_left(edges, m):
    nx = edges.shape[-1]
    shift = (2 * nx - 2 - 2 * m) % nx if isinstance(m, int) else 2 * nx - 2 - 2 * m
    return pltpu.roll(edges, shift, 1)


def sides(lane):
    return (lane < 2) | (lane >= lane.shape[-1] - 2)


def x_weights(nx):
    ahead = (
        lax.broadcasted_iota(jnp.int32, (nx, nx), 0) - lax.broadcasted_iota(jnp.int32, (nx, nx), 1)
    )
    weights = jnp.zeros((nx, nx), F32)
    for offset, weight in ((1, 8.0), (-1, -8.0), (2, -1.0), (-2, 1.0)):
        weights = jnp.where((ahead == offset) | (ahead == offset + nx) | (ahead == offset - nx), weight, weights)
    weights = weights.astype(jnp.bfloat16)
    return jnp.concatenate([weights] * 3, axis=0)


def periodic_x(value, weights):
    high = value.astype(jnp.bfloat16)
    rest = value - high.astype(F32)
    middle = rest.astype(jnp.bfloat16)
    low = (rest - middle.astype(F32)).astype(jnp.bfloat16)
    return jnp.dot(
        jnp.concatenate([high, middle, low], axis=1), weights, preferred_element_type=F32
    )


def along_all(ref, comps, out_ref, group=16):
    _, nz, ny, nx = out_ref.shape
    group = next(d for d in range(group, 0, -1) if nz % d == 0)
    weights = x_weights(nx)

    @pl.loop(0, nz // group)
    def _(j):
        layers = pl.ds(j * group, group)
        rows = [ref[c, layers].reshape(group * ny, nx) for c in comps]
        result = periodic_x(jnp.concatenate(rows, axis=0), weights)
        for i in range(len(comps)):
            part = result[i * group * ny : (i + 1) * group * ny]
            out_ref[i, layers] = part.reshape(group, ny, nx)


def lookup(row, tile):
    table = jnp.broadcast_to(row, tile.shape)
    return jnp.take_along_axis(table, tile, axis=1, mode="promise_in_bounds")


def table_rows(refs, nx):
    n = refs[0].shape[1]
    return [jnp.concatenate([r, jnp.zeros((1, nx - n), F32)], axis=1) for r in refs]


def fill_edges(n_gx, edge_ref, x1_ref, x2_ref, low_ref, high_ref):
    for c in range(3):
        at = slice(SUB * c, SUB * c + SUB)
        got = (x1_ref[at, :], x2_ref[at, :])
        first, second = edge_terms(
            from_before("gx", got), from_after("gx", n_gx, got), low_ref[at, :], high_ref[at, :]
        )
        edge_ref[c, 0] = first
        edge_ref[c, 1] = second


def fill_rows(n_gy, tall, field, y1_ref, y2_ref, nz, ny, layers):
    for c in range(3):
        for spot, k in enumerate(layers):
            j = 2 * (c * nz + k)
            got = (y1_ref[j : j + 2, :], y2_ref[j : j + 2, :])
            tall[c, spot, PAD : PAD + ny, :] = field(c, k)
            tall[c, spot, PAD - 2 : PAD, :] = from_before("gy", got)
            tall[c, spot, PAD + ny : PAD + ny + 2, :] = from_after("gy", n_gy, got)


def depth_halos(n_gz, zb, za, z1_ref, z2_ref):
    got = (z1_ref[...], z2_ref[...])
    zb[...] = from_before("gz", got)
    za[...] = from_after("gz", n_gz, got)


def over(low, high, most, body):
    count = high - low
    group = next(d for d in range(most, 0, -1) if count % d == 0)

    @pl.loop(0, count // group)
    def _(j):
        for i in range(group):
            body(low + j * group + i)


def tile_rows(t):
    return slice(SUB * t, SUB * t + SUB)


def row_difference(tall, c, spot, t):
    return centred12(lambda s: tall[c, spot, PAD + SUB * t + s : PAD + SUB * t + s + SUB, :])


def inner_depth(ref, out_ref, comps, k, tiles):
    for t in range(tiles):
        for c in range(comps):
            out_ref[c, k - 2, tile_rows(t), :] = centred12(lambda s: ref[c, k + s, tile_rows(t), :])


def outer_depth(ref, zb, za, out_ref, comps, nz, tiles):
    for spot, k in enumerate((0, 1, nz - 2, nz - 1)):
        for t in range(tiles):
            for c in range(comps):

                def at(s):
                    if k + s < 0:
                        return zb[c, k + s + 2, tile_rows(t), :]
                    if k + s >= nz:
                        return za[c, k + s - nz, tile_rows(t), :]
                    return ref[c, k + s, tile_rows(t), :]

                out_ref[c, spot, tile_rows(t), :] = centred12(at)


def cell_kernel(
    layers_ref, material_ref, buoy_ref, lam_ref, mu_ref, relax_ref, weight_ref, cells_ref, spread_ref
):
    lane = lanes_of((SUB, layers_ref.shape[1]))
    sub = lax.broadcasted_iota(jnp.int32, lane.shape, 0)
    for i in range(2):
        row = jnp.broadcast_to(layers_ref[i : i + 1, :], lane.shape)
        for g in range(spread_ref.shape[1] // SUB):
            one = jnp.sum(jnp.where(lane == SUB * g + sub, row, 0.0), axis=1, keepdims=True)
            spread_ref[i, tile_rows(g), :] = jnp.broadcast_to(one, lane.shape)
    nz, ny, nx = material_ref.shape
    keep = jnp.exp(-step_size / relax_ref[...])
    tables = table_rows(
        [
            buoy_ref[...] * (step_size / 12.0), lam_ref[...] / 12.0, mu_ref[...] / 12.0, keep,
            (1.0 - keep) * weight_ref[...],
        ],
        nx,
    )

    def layer(k):
        for t in range(ny // SUB):
            kind = material_ref[k, tile_rows(t), :]
            for i, table in enumerate(tables):
                cells_ref[i, k, tile_rows(t), :] = lookup(table, kind)

    over(0, nz, 8, layer)


def depth_kernel(stress_ref, velocity_hbm, depth_ref, along_ref, velocity_ref, sem):
    load = pltpu.make_async_copy(velocity_hbm, velocity_ref, sem)
    load.start()
    _, nz, ny, _ = stress_ref.shape
    along_all(stress_ref, (0, 3, 4), along_ref)
    over(2, nz - 2, 4, lambda k: inner_depth(stress_ref, depth_ref, 6, k, ny // SUB))
    load.wait()


def plane_kernel(
    sizes, stress_ref, along_ref, y1_ref, y2_ref, z1_ref, z2_ref, plane_ref, outer_ref, tall, zb, za
):
    depth_halos(sizes[2], zb, za, z1_ref, z2_ref)
    outer_depth(stress_ref, zb, za, outer_ref, 6, stress_ref.shape[1], stress_ref.shape[2] // SUB)
    _, nz, ny, nx = stress_ref.shape
    tiles = ny // SUB
    of_y = (3, 1, 5)
    fill_rows(sizes[1], tall, lambda c, k: stress_ref[of_y[c], k], y1_ref, y2_ref, nz, ny, range(nz))

    def layer(k):
        for t in range(tiles):
            for c in range(3):
                plane_ref[c, k, tile_rows(t), :] = along_ref[
                    c, k, tile_rows(t), :
                ] + row_difference(tall, c, k, t)

    over(0, nz, 4, layer)


def velocity_kernel(
    sizes, velocity_ref, cells_ref, inner_ref, outer_ref, plane_ref, factor_ref, mz_ref, slope_ref,
    x1_ref, x2_ref, low_ref, high_ref, out_ref, vlow_ref, vhigh_ref, vx1_ref, vx2_ref, vz1_ref, vz2_ref,
    *rest,
):
    *vy_refs, edge = rest
    _, nz, ny, nx = velocity_ref.shape
    tiles = ny // SUB
    lane = lanes_of((SUB, nx))
    fill_edges(sizes[0], edge, x1_ref, x2_ref, low_ref, high_ref)

    def layer(k, depth_ref, spot):
        for t in range(tiles):
            rows = tile_rows(t)
            b = cells_ref[0, k, rows, :]
            factor = factor_ref[k, rows, :]
            mz = mz_ref[k, rows, :]
            mx = slope_ref[0, rows, :] * factor
            my = slope_ref[1, rows, :] * factor
            gk = [depth_ref[c, spot, rows, :] for c in range(6)]
            beside = [
                plane_ref[c, k, rows, :]
                + jnp.where(sides(lane), turned_left(edge[c, t % 2], k * tiles + t), 0.0)
                for c in range(3)
            ]
            accel = (
                beside[0] - mx * gk[0] - my * gk[3] + mz * gk[4],
                beside[1] - mx * gk[3] - my * gk[1] + mz * gk[5],
                beside[2] - mx * gk[4] - my * gk[5] + mz * gk[2],
            )
            for c in range(3):
                out_ref[c, k, rows, :] = velocity_ref[c, k, rows, :] + b * accel[c]

    for spot, k in enumerate((0, 1, nz - 2, nz - 1)):
        layer(k, outer_ref, spot)

    over(2, nz - 2, 12, lambda k: layer(k, inner_ref, k - 2))
    pack_sides(
        lambda c, k, t: out_ref[c, k, tile_rows(t), :], nz, ny, nx, vlow_ref, vhigh_ref, vx1_ref, vx2_ref
    )
    pack_rows(lambda c, k, rows: out_ref[c, k, rows, :], nz, ny, vy_refs)
    vz1_ref[...], vz2_ref[...] = order("gz", out_ref[:, nz - 2 : nz], out_ref[:, 0:2])


def velocity_inner_kernel(vel_ref, vel_hbm, depth_ref, along_ref, across_ref, tall, sem):
    store = pltpu.make_async_copy(vel_ref, vel_hbm, sem)
    store.start()
    _, nz, ny, nx = vel_ref.shape
    tiles = ny // SUB

    along_all(vel_ref, (0, 1, 2), along_ref)
    over(2, nz - 2, 4, lambda k: inner_depth(vel_ref, depth_ref, 3, k, tiles))
    nothing = jnp.zeros((2, nx), F32)
    for c in range(3):
        for k in range(nz):
            tall[c, k, PAD : PAD + ny, :] = vel_ref[c, k]
            tall[c, k, PAD - 2 : PAD, :] = nothing
            tall[c, k, PAD + ny : PAD + ny + 2, :] = nothing

    def across(k):
        for t in range(tiles):
            for c in range(3):
                across_ref[c, k, tile_rows(t), :] = row_difference(tall, c, k, t)

    over(0, nz, 4, across)
    store.wait()


def fill_sides(n_gy, top, bottom, y1_ref, y2_ref):
    count = y1_ref.shape[0]
    got = (y1_ref[...], y2_ref[...])
    even_row = lax.broadcasted_iota(jnp.int32, got[0].shape, 0) % 2 == 0
    empty = jnp.zeros((SUB, y1_ref.shape[1]), F32)
    before, after = from_before("gy", got), from_after("gy", n_gy, got)
    top[:count, :] = before
    top[count:, :] = empty
    bottom[:SUB, :] = empty
    bottom[SUB:, :] = after
    top[:count, :] = jnp.where(even_row, before - 8.0 * top[1 : count + 1, :], before)
    bottom[SUB:, :] = jnp.where(even_row, -after, 8.0 * bottom[SUB - 1 : SUB + count - 1, :] - after)


def beside_rows(top, bottom, c, k, t, nz, tiles):
    j = 2 * (c * nz + k)
    row = lax.broadcasted_iota(jnp.int32, (SUB, top.shape[1]), 0)
    added = 0.0
    if t == 0:
        added = jnp.where(row < 2, top[pl.ds(j, SUB), :], 0.0)
    if t == tiles - 1:
        added = added + jnp.where(row >= SUB - 2, bottom[pl.ds(j + 2, SUB), :], 0.0)
    return added


def stress_kernel(
    sizes, vel_ref, stress_ref, memory_ref, cells_ref, inner_ref, along_ref, across_ref, factor_ref, mz_ref,
    slope_ref, x1_ref, x2_ref, low_ref, high_ref, y1_ref, y2_ref, z1_ref, z2_ref,
    stress_hbm, memory_hbm, edge, top, bottom, zb, za, outer, stress_out, memory_out, sems,
):
    n_gx, n_gy, n_gz = sizes
    _, nz, ny, nx = vel_ref.shape
    tiles = ny // SUB
    lane = lanes_of((SUB, nx))
    fill_edges(n_gx, edge, x1_ref, x2_ref, low_ref, high_ref)
    fill_sides(n_gy, top, bottom, y1_ref, y2_ref)

    def layer(k, depth_ref, spot):
        for t in range(tiles):
            rows = tile_rows(t)
            factor = factor_ref[k, rows, :]
            mz = mz_ref[k, rows, :]
            mx = slope_ref[0, rows, :] * factor
            my = slope_ref[1, rows, :] * factor
            dk = [depth_ref[c, spot, rows, :] for c in range(3)]
            dx = [
                along_ref[c, k, rows, :]
                + jnp.where(sides(lane), turned_left(edge[c, t % 2], k * tiles + t), 0.0)
                - mx * dk[c]
                for c in range(3)
            ]
            dy = [
                across_ref[c, k, rows, :] + beside_rows(top, bottom, c, k, t, nz, tiles) - my * dk[c]
                for c in range(3)
            ]
            dz = [mz * dk[c] for c in range(3)]
            lam, mu, keep, gain = (cells_ref[i, k, rows, :] for i in range(1, 5))
            volume = lam * (dx[0] + dy[1] + dz[2])
            mu2 = mu + mu
            rates = (
                volume + mu2 * dx[0],
                volume + mu2 * dy[1],
                volume + mu2 * dz[2],
                mu * (dy[0] + dx[1]),
                mu * (dz[0] + dx[2]),
                mu * (dz[1] + dy[2]),
            )
            for c in range(6):
                kept = keep * memory_ref[c, k, rows, :] + gain * rates[c]
                memory_out[c, k, rows, :] = kept
                stress_out[c, k, rows, :] = stress_ref[c, k, rows, :] + step_size * (
                    rates[c] - kept
                )

    pairs = ((stress_out, stress_hbm), (memory_out, memory_hbm))

    def send(first, count):
        layers = pl.ds(first, count)
        for i, (a, b) in enumerate(pairs):
            pltpu.make_async_copy(a.at[:, layers], b.at[:, layers], sems.at[i]).start()

    inner = nz - 4
    step = next(d for d in (4, 3, 2, 1) if inner % d == 0)

    for k in range(2, nz - 2):
        layer(k, inner_ref, k - 2)
        send(k, 1)

    depth_halos(n_gz, zb, za, z1_ref, z2_ref)
    outer_depth(vel_ref, zb, za, outer, 3, nz, tiles)
    for spot, k in enumerate((0, 1, nz - 2, nz - 1)):
        layer(k, outer, spot)
        send(k, 1)
    for i, (a, b) in enumerate(pairs):
        pltpu.make_async_copy(a, b, sems.at[i]).wait()


def in_hbm(value):
    return pltpu.with_memory_space_constraint(value, pltpu.HBM)


def call(kernel, outs, in_specs, scratch=(), name=None, out_specs=None, cost=0.0):
    return pl.pallas_call(
        kernel,
        out_shape=[jax.ShapeDtypeStruct(s, F32) for s in outs],
        in_specs=in_specs,
        out_specs=out_specs or [VM] * len(outs),
        scratch_shapes=list(scratch),
        compiler_params=params(),
        cost_estimate=pl.CostEstimate(flops=int(cost * 6e8), transcendentals=0, bytes_accessed=int(cost * 3.5e6)),
        name=name,
    )


def local(
    sizes, elevation, layer_base, stretch, material, buoyancy, lame_lambda, shear_modulus,
    relax_time, anelastic_weight, velocity, stress, memory,
):
    n_gx, n_gy, n_gz = counts = tuple(sizes[a] for a in ("gx", "gy", "gz"))
    _, nz, ny, nx = velocity.shape
    rows = ny + SUB
    rounds = pair_swaps(sizes, "gz")
    if n_gz == 4:
        piece = lax.ppermute(elevation, tuple(sizes), rounds[0])
    slab = call(
        terrain_piece_kernel,
        [(rows, nx)],
        [HB] * 3,
        [
            pltpu.VMEM(elevation.shape, jnp.int32),
            pltpu.VMEM((1, nz), F32),
            pltpu.VMEM((1, nz), F32),
            DMA((3,)),
        ],
        name="terrain_piece", cost=0.8,
    )(in_hbm(elevation), in_hbm(layer_base[None]), in_hbm(stretch[None]))[0]
    tied = lax.optimization_barrier
    faces = 2 * 3 * nz
    xs = 3 * SUB
    y_rounds = min(2, n_gy - 1) if n_gy > 1 else 1
    z_face = (6, 2, ny, nx)
    if n_gz == 4:
        slab = call(merge_kernel, [(rows, nx)], [VM] * 2, name="merge", cost=0.1)(slab, piece)[0]
        slab, stress = tied((slab, stress))
        slab = slab + lax.ppermute(slab, tuple(sizes), rounds[1])
        layers = slab[ny:]
    elif n_gz & (n_gz - 1):
        slab = lax.psum(slab, "gz")
        layers = slab[ny:]
    else:
        bit = 1
        while bit < n_gz:
            slab = slab + lax.ppermute(slab, "gz", [(i, i ^ bit) for i in range(n_gz)])
            if bit == 1:
                slab, stress = tied((slab, stress))
            bit *= 2
        layers = slab[ny:]
    stress_vm = stress
    low, high, x1, x2, z1, z2, *ys = call(
        pack_kernel,
        [(xs, nx)] * 4 + [z_face] * 2 + [(faces, nx)] * y_rounds,
        [VM],
        name="pack_stress", cost=0.5,
    )(stress)
    z1, z2 = exchange(sizes, "gz", z1, z2)
    ts = call(y_send_kernel, [(SUB, nx)] * y_rounds, [VM], name="y_send", cost=0.02)(slab)
    ts, ys, stress_vm, layers = tied((ts, ys, stress_vm, layers))
    t1, t2 = exchange(sizes, "gy", ts[0], ts[-1])
    y1, y2 = exchange(sizes, "gy", ys[0], ys[-1])
    if n_gz == 4:
        layers = layers + lax.ppermute(layers, tuple(sizes), rounds[0])
    inner_k, along, velocity_vm = call(
        depth_kernel,
        [(6, nz - 4, ny, nx), velocity.shape, velocity.shape],
        [VM, HB],
        [DMA],
        name="depth", cost=2.2,
    )(stress_vm, in_hbm(velocity))
    x1, x2, inner_k = tied((x1, x2, inner_k))
    terrain, x1, x2 = call(
        functools.partial(x_send_kernel, n_gy),
        [(ny + 2 * PAD, nx)] + [(xs + SUB, nx)] * 2,
        [VM] * 5,
        name="x_send", cost=0.1,
    )(slab, t1, t2, x1, x2)
    x1, x2, material = tied((x1, x2, material))
    x1, x2 = exchange(sizes, "gx", x1, x2, True)
    edge = pltpu.VMEM((3, 2, SUB, nx), F32)
    tall = pltpu.VMEM((3, nz, ny + 2 * PAD, nx), F32)

    def depth(comps):
        return [pltpu.VMEM((comps, 2, ny, nx), F32)] * 2

    tables = (buoyancy, lame_lambda, shear_modulus, relax_time, anelastic_weight)
    all_layers = -(-n_gz * nz // SUB) * SUB
    cells, spread = call(
        cell_kernel, [(5, nz, ny, nx), (2, all_layers, nx)], [VM] * 7, name="cells", cost=0.8
    )(layers, material, *[table[None] for table in tables])
    plane, outer_k = call(
        functools.partial(plane_kernel, counts),
        [velocity.shape, (6, 4, ny, nx)],
        [VM] * 6,
        [tall] + depth(6),
        name="planes", cost=0.6,
    )(stress_vm, along, y1, y2, z1, z2)
    plane, cells, x1, x2 = tied((plane, cells, x1, x2))
    factor, mz, slope = call(
        functools.partial(metric_kernel, counts),
        [(nz, ny, nx), (nz, ny, nx), (2, ny, nx)],
        [VM] * 4,
        [pltpu.VMEM((ny + 2 * PAD, nx), F32), pltpu.VMEM((ny + PAD, nx), F32)],
        name="metrics", cost=1.1,
    )(spread, terrain, x1[xs:], x2[xs:])
    vel, vlow, vhigh, vx1, vx2, vz1, vz2, *vys = call(
        functools.partial(velocity_kernel, counts),
        [velocity.shape] + [(xs, nx)] * 4 + [(3, 2, ny, nx)] * 2 + [(faces, nx)] * y_rounds,
        [VM] * 12,
        [edge],
        name="velocity", cost=1.5,
    )(velocity_vm, cells, inner_k, outer_k, plane, factor, mz, slope, x1, x2, low, high)
    vz1, vz2 = exchange(sizes, "gz", vz1, vz2)
    vy1, vy2 = exchange(sizes, "gy", vys[0], vys[-1])
    vx1, vx2 = exchange(sizes, "gx", vx1, vx2)
    vel_next, vel_k, vel_x, vel_y = call(
        velocity_inner_kernel,
        [velocity.shape, (3, nz - 4, ny, nx), velocity.shape, velocity.shape],
        [VM],
        [tall, DMA],
        name="velocity_inner", cost=0.1,
        out_specs=[HB, VM, VM, VM],
    )(vel)
    stress_next, memory_next = call(
        functools.partial(stress_kernel, counts),
        [stress.shape, stress.shape],
        [VM] * 18,
        [edge, pltpu.VMEM((faces + SUB, nx), F32), pltpu.VMEM((faces + SUB, nx), F32)]
        + depth(3)
        + [pltpu.VMEM((3, 4, ny, nx), F32), pltpu.VMEM(stress.shape, F32), pltpu.VMEM(stress.shape, F32)]
        + [DMA((2,))],
        name="stress", cost=2.8,
        out_specs=[HB] * 2,
    )(
        vel, stress_vm, memory, cells, vel_k, vel_x, vel_y, factor, mz, slope, vx1, vx2, vlow, vhigh, vy1, vy2,
        vz1, vz2,
    )
    return vel_next, stress_next, memory_next


def solution(mesh):
    sizes = {a: mesh.shape[a] for a in ("gx", "gy", "gz")}
    field = P(None, "gz", "gy", "gx")
    return jax.shard_map(
        functools.partial(local, sizes),
        mesh=mesh,
        in_specs=(
            P("gy", ("gx", "gz")), P("gz"), P("gz"), P("gz", "gy", "gx"),
            P(), P(), P(), P(), P(), field, field, field,
        ),
        out_specs=(field, field, field),
        check_vma=False,
    )
```

```python
import functools
import jax
import jax.numpy as jnp
import numpy as np
from jax import lax
from jax.experimental import pallas as pl
from jax.experimental.pallas import tpu as pltpu
from jax.sharding import PartitionSpec as P

step_size = 0.3
SUB = 8
PAD = 8
F32 = jnp.float32
params = functools.partial(pltpu.CompilerParams, vmem_limit_bytes=20 * 1024 * 1024)
VM = pl.BlockSpec(memory_space=pltpu.VMEM)
SM = pl.BlockSpec(memory_space=pltpu.SMEM)
HB = pl.BlockSpec(memory_space=pltpu.HBM)
DMA = pltpu.SemaphoreType.DMA


def pair_swaps(sizes, axis):
    names = tuple(sizes)
    shape = tuple(sizes.values())
    index = names.index(axis)
    n = shape[index]
    others = [d for d in (2, 1, 0) if d != index and shape[d] % 2 == 0]
    rounds = []
    for first in (0, 1)[: max(0, min(2, n - 1))]:
        table = []
        for spot in np.ndindex(*shape):
            mate = spot[index] + 1 if spot[index] % 2 == first else spot[index] - 1
            target = list(spot)
            if 0 <= mate < n or axis == "gz":
                target[index] = mate % n
            elif others:
                target[others[0]] ^= 1
            else:
                continue
            table.append((int(np.ravel_multi_index(spot, shape)), int(np.ravel_multi_index(tuple(target), shape))))
        rounds.append(table)
    return rounds


def exchange(sizes, axis, first, second, second_first=False):
    rounds = list(zip((first, second), pair_swaps(sizes, axis)))
    if second_first:
        rounds = rounds[::-1]
    got = [lax.ppermute(v, tuple(sizes), r) for v, r in rounds]
    if second_first:
        got = got[::-1]
    return (got[0], got[-1]) if got else (first, second)


def even(axis):
    return lax.axis_index(axis) % 2 == 0


def from_before(axis, got):
    value = jnp.where(even(axis), got[1], got[0])
    return jnp.where(lax.axis_index(axis) > 0, value, 0.0)


def from_after(axis, n, got):
    value = jnp.where(even(axis), got[0], got[1])
    return jnp.where(lax.axis_index(axis) < n - 1, value, 0.0)


def order(axis, to_after, to_before):
    e = even(axis)
    return jnp.where(e, to_after, to_before), jnp.where(e, to_before, to_after)


def lanes_of(shape):
    return lax.broadcasted_iota(jnp.int32, shape, len(shape) - 1)


def terrain_piece_kernel(elev_hbm, base_hbm, stretch_hbm, out_ref, elev_ref, base_ref, stretch_ref, sems):
    mine = lax.axis_index("gz")
    pairs = ((elev_hbm, elev_ref), (base_hbm, base_ref), (stretch_hbm, stretch_ref))
    copies = [pltpu.make_async_copy(a, b, sems.at[i]) for i, (a, b) in enumerate(pairs)]
    for copy in copies:
        copy.start()
    for copy in copies:
        copy.wait()
    ny, width = elev_ref.shape
    nx = out_ref.shape[1]
    nz = base_ref.shape[1]
    height = elev_ref[...].astype(F32) / 200.0
    wide = jnp.concatenate([height, jnp.zeros((ny, nx - width), F32)], axis=1)
    out_ref[:ny, :] = pltpu.roll(wide, mine * width, 1)
    row = lax.broadcasted_iota(jnp.int32, (SUB, nx), 0)
    fill = jnp.zeros((1, nx - nz), F32)
    base = jnp.concatenate([base_ref[...], fill], axis=1)
    stretch = jnp.concatenate([stretch_ref[...], fill], axis=1)
    both = jnp.where(row == 0, base, jnp.where(row == 1, stretch, 0.0))
    out_ref[ny:, :] = pltpu.roll(both, mine * nz, 1)


def merge_kernel(first_ref, elev_ref, out_ref):
    ny, width = elev_ref.shape
    nx = out_ref.shape[1]
    height = elev_ref[...].astype(F32) / 200.0
    wide = jnp.concatenate([height, jnp.zeros((ny, nx - width), F32)], axis=1)
    mate = lax.axis_index("gz") + jnp.where(even("gz"), 1, -1)
    out_ref[:ny, :] = first_ref[:ny, :] + pltpu.roll(wide, mate * width, 1)
    out_ref[ny:, :] = first_ref[ny:, :]


def pack_sides(field, nz, ny, nx, low_ref, high_ref, out1_ref, out2_ref):
    tiles = ny // SUB
    lane2 = lanes_of((SUB, nx)) // 2
    for c in range(3):
        lo = jnp.zeros((SUB, nx), F32)
        hi = jnp.zeros((SUB, nx), F32)
        for k in range(nz):
            for t in range(tiles):
                m = k * tiles + t
                turned = pltpu.roll(field(c, k, t), (2 * m + 2) % nx, 1)
                hi = jnp.where(lane2 == m, turned, hi)
                lo = jnp.where(lane2 == (m + 1) % (nx // 2), turned, lo)
        at = slice(SUB * c, SUB * c + SUB)
        low_ref[at, :] = lo
        high_ref[at, :] = hi
        out1_ref[at, :], out2_ref[at, :] = order("gx", hi, lo)


def pack_rows(field, nz, ny, y_refs):
    for c in range(3):
        for k in range(nz):
            j = 2 * (c * nz + k)
            both = order("gy", field(c, k, slice(ny - 2, ny)), field(c, k, slice(0, 2)))
            for ref, rows in zip(y_refs, both):
                ref[j : j + 2, :] = rows


def pack_kernel(stress_ref, low_ref, high_ref, out1_ref, out2_ref, z1_ref, z2_ref, *y_refs):
    _, nz, ny, nx = stress_ref.shape
    of_x = (0, 3, 4)
    of_y = (3, 1, 5)
    z1_ref[...], z2_ref[...] = order("gz", stress_ref[:, nz - 2 : nz], stress_ref[:, 0:2])
    pack_sides(
        lambda c, k, t: stress_ref[of_x[c], k, SUB * t : SUB * t + SUB, :],
        nz, ny, nx, low_ref, high_ref, out1_ref, out2_ref,
    )
    pack_rows(lambda c, k, rows: stress_ref[of_y[c], k, rows, :], nz, ny, y_refs)


def y_send_kernel(slab_ref, *out_refs):
    ny = slab_ref.shape[0] - SUB
    both = order("gy", slab_ref[ny - 4 : ny, :], slab_ref[0:4, :])
    for ref, rows in zip(out_refs, both):
        ref[0:4, :] = rows
        ref[4:, :] = jnp.zeros_like(rows)


def x_send_kernel(n_gy, slab_ref, y1_ref, y2_ref, x1_ref, x2_ref, tall_ref, out1_ref, out2_ref):
    ny = slab_ref.shape[0] - SUB
    nx = slab_ref.shape[1]
    xs = x1_ref.shape[0]
    lane4 = lanes_of((SUB, nx)) // 4
    got = (y1_ref[0:4, :], y2_ref[0:4, :])
    tall_ref[: PAD - 4, :] = jnp.zeros((PAD - 4, nx), F32)
    tall_ref[PAD - 4 : PAD, :] = from_before("gy", got)
    tall_ref[PAD : PAD + ny, :] = slab_ref[:ny, :]
    tall_ref[PAD + ny : PAD + ny + 4, :] = from_after("gy", n_gy, got)
    tall_ref[PAD + ny + 4 :, :] = jnp.zeros((PAD - 4, nx), F32)
    lo = jnp.zeros((SUB, nx), F32)
    hi = jnp.zeros((SUB, nx), F32)
    for j in range((ny + 2 * PAD) // SUB):
        tile = tall_ref[SUB * j : SUB * j + SUB, :]
        lo = jnp.where(lane4 == j, pltpu.roll(tile, 4 * j, 1), lo)
        hi = jnp.where(lane4 == j, pltpu.roll(tile, (4 * j + 4) % nx, 1), hi)
    out1_ref[:xs, :] = x1_ref[...]
    out2_ref[:xs, :] = x2_ref[...]
    out1_ref[xs:, :], out2_ref[xs:, :] = order("gx", hi, lo)


def binomial(at):
    return (at(-2) + at(2) + 4.0 * (at(-1) + at(1)) + 6.0 * at(0)) / 16.0


def centred12(at):
    return 8.0 * (at(1) - at(-1)) - (at(2) - at(-2))


def metric_kernel(
    sizes, layers_ref, own, x1_ref, x2_ref, factor_ref, mz_ref, slope_ref, rim, sown,
):
    n_gx = sizes[0]
    gz = lax.axis_index("gz")
    nz, ny, nx = factor_ref.shape
    lane = lanes_of((SUB, nx))
    got = (x1_ref[...], x2_ref[...])
    left, right = from_before("gx", got), from_after("gx", n_gx, got)
    for j in range((ny + 2 * PAD) // SUB):
        rim[SUB * j : SUB * j + SUB, :] = jnp.where(
            lane < nx // 2,
            pltpu.roll(right, (nx - 4 * j) % nx, 1),
            pltpu.roll(left, nx - 4 - 4 * j, 1),
        )
    rows = ny + 4
    tall_own = binomial(lambda s: own[PAD - 2 + s : PAD - 2 + s + rows, :])
    tall_rim = binomial(lambda s: rim[PAD - 2 + s : PAD - 2 + s + rows, :])

    def shifted(a, b, s):
        ln = lanes_of(a.shape)
        cut = (ln < s) if s > 0 else (ln >= nx + s)
        if s > 0:
            mixed_a, mixed_b = jnp.where(cut, b, a), jnp.where(cut, a, b)
        elif s < 0:
            mixed_a, mixed_b = jnp.where(cut, b, a), jnp.where(cut, a, b)
        else:
            return a, b
        return pltpu.roll(mixed_a, (-s) % nx, 1), pltpu.roll(mixed_b, (-s) % nx, 1)

    def padded_rows(a):
        return jnp.concatenate([a, jnp.zeros((SUB - rows % SUB, nx), F32)], axis=0)

    tall_own, tall_rim = padded_rows(tall_own), padded_rows(tall_rim)
    pairs = {s: shifted(tall_own, tall_rim, s) for s in (-2, -1, 0, 1, 2)}
    surf_own = binomial(lambda s: pairs[s][0])
    surf_rim = binomial(lambda s: pairs[s][1])
    sown[...] = surf_own
    slope_ref[1] = centred12(lambda s: sown[2 + s : 2 + s + ny, :]) / 12.0
    pairs2 = {s: shifted(surf_own, surf_rim, s)[0] for s in (-2, -1, 1, 2)}
    along = centred12(lambda s: pairs2[s]) / 12.0
    surface = sown[2 : 2 + ny, :]
    sown[...] = along
    slope_ref[0] = sown[2 : 2 + ny, :]

    def above(slab, total):
        for k in range(nz):
            at = pl.ds(slab * nz + k, 1)
            s = layers_ref[1, at, :]
            total = total + (s * layers_ref[0, at, :]) * jnp.exp(s * surface)
        return total

    total = lax.fori_loop(0, gz, above, jnp.zeros((ny, nx), F32))
    for k in range(nz):
        at = pl.ds(gz * nz + k, 1)
        s = layers_ref[1, at, :]
        thickness = layers_ref[0, at, :] * jnp.exp(s * surface)
        weighted = s * thickness
        mz = 1.0 / thickness
        lift = total + 0.5 * weighted
        total = total + weighted
        mz_ref[k] = mz
        factor_ref[k] = (lift - 1.0) * mz

def edge_terms(got_left, got_right, low, high):
    dl = got_left - high
    dr = got_right - low
    nx = dl.shape[-1]
    lane = lanes_of(dl.shape)
    even = lane % 2 == 0
    dl = pltpu.roll(dl, 2, 1)
    dr = pltpu.roll(dr, nx - 2, 1)
    to_low = jnp.where(even, dl - 8.0 * pltpu.roll(dl, nx - 1, 1), dl)
    to_high = jnp.where(even, -dr, 8.0 * pltpu.roll(dr, 1, 1) - dr)
    second = (lane // 2) % 2 == 1
    return jnp.where(second, to_low, to_high), jnp.where(second, to_high, to_low)


def turned_left(edges, m):
    nx = edges.shape[-1]
    shift = (2 * nx - 2 - 2 * m) % nx if isinstance(m, int) else 2 * nx - 2 - 2 * m
    return pltpu.roll(edges, shift, 1)


def sides(lane):
    return (lane < 2) | (lane >= lane.shape[-1] - 2)


def x_weights(nx):
    ahead = (
        lax.broadcasted_iota(jnp.int32, (nx, nx), 0) - lax.broadcasted_iota(jnp.int32, (nx, nx), 1)
    )
    weights = jnp.zeros((nx, nx), F32)
    for offset, weight in ((1, 8.0), (-1, -8.0), (2, -1.0), (-2, 1.0)):
        weights = jnp.where((ahead == offset) | (ahead == offset + nx) | (ahead == offset - nx), weight, weights)
    weights = weights.astype(jnp.bfloat16)
    return jnp.concatenate([weights] * 3, axis=0)


def periodic_x(value, weights):
    high = value.astype(jnp.bfloat16)
    rest = value - high.astype(F32)
    middle = rest.astype(jnp.bfloat16)
    low = (rest - middle.astype(F32)).astype(jnp.bfloat16)
    return jnp.dot(
        jnp.concatenate([high, middle, low], axis=1), weights, preferred_element_type=F32
    )


def along_all(ref, comps, out_ref, group=16):
    _, nz, ny, nx = out_ref.shape
    group = next(d for d in range(group, 0, -1) if nz % d == 0)
    weights = x_weights(nx)

    @pl.loop(0, nz // group)
    def _(j):
        layers = pl.ds(j * group, group)
        rows = [ref[c, layers].reshape(group * ny, nx) for c in comps]
        result = periodic_x(jnp.concatenate(rows, axis=0), weights)
        for i in range(len(comps)):
            part = result[i * group * ny : (i + 1) * group * ny]
            out_ref[i, layers] = part.reshape(group, ny, nx)


def lookup(row, tile):
    table = jnp.broadcast_to(row, tile.shape)
    return jnp.take_along_axis(table, tile, axis=1, mode="promise_in_bounds")


def table_rows(refs, nx):
    n = refs[0].shape[1]
    return [jnp.concatenate([r, jnp.zeros((1, nx - n), F32)], axis=1) for r in refs]


def fill_edges(n_gx, edge_ref, x1_ref, x2_ref, low_ref, high_ref):
    for c in range(3):
        at = slice(SUB * c, SUB * c + SUB)
        got = (x1_ref[at, :], x2_ref[at, :])
        first, second = edge_terms(
            from_before("gx", got), from_after("gx", n_gx, got), low_ref[at, :], high_ref[at, :]
        )
        edge_ref[c, 0] = first
        edge_ref[c, 1] = second


def fill_rows(n_gy, tall, field, y1_ref, y2_ref, nz, ny, layers):
    for c in range(3):
        for spot, k in enumerate(layers):
            j = 2 * (c * nz + k)
            got = (y1_ref[j : j + 2, :], y2_ref[j : j + 2, :])
            tall[c, spot, PAD : PAD + ny, :] = field(c, k)
            tall[c, spot, PAD - 2 : PAD, :] = from_before("gy", got)
            tall[c, spot, PAD + ny : PAD + ny + 2, :] = from_after("gy", n_gy, got)


def depth_halos(n_gz, zb, za, z1_ref, z2_ref):
    got = (z1_ref[...], z2_ref[...])
    zb[...] = from_before("gz", got)
    za[...] = from_after("gz", n_gz, got)


def over(low, high, most, body):
    count = high - low
    group = next(d for d in range(most, 0, -1) if count % d == 0)

    @pl.loop(0, count // group)
    def _(j):
        for i in range(group):
            body(low + j * group + i)


def tile_rows(t):
    return slice(SUB * t, SUB * t + SUB)


def row_difference(tall, c, spot, t):
    return centred12(lambda s: tall[c, spot, PAD + SUB * t + s : PAD + SUB * t + s + SUB, :])


def inner_depth(ref, out_ref, comps, k, tiles):
    for t in range(tiles):
        for c in range(comps):
            out_ref[c, k - 2, tile_rows(t), :] = centred12(lambda s: ref[c, k + s, tile_rows(t), :])


def outer_depth(ref, zb, za, out_ref, comps, nz, tiles):
    for spot, k in enumerate((0, 1, nz - 2, nz - 1)):
        for t in range(tiles):
            for c in range(comps):

                def at(s):
                    if k + s < 0:
                        return zb[c, k + s + 2, tile_rows(t), :]
                    if k + s >= nz:
                        return za[c, k + s - nz, tile_rows(t), :]
                    return ref[c, k + s, tile_rows(t), :]

                out_ref[c, spot, tile_rows(t), :] = centred12(at)


def cell_kernel(
    layers_ref, material_ref, buoy_ref, lam_ref, mu_ref, relax_ref, weight_ref, cells_ref, spread_ref
):
    lane = lanes_of((SUB, layers_ref.shape[1]))
    sub = lax.broadcasted_iota(jnp.int32, lane.shape, 0)
    for i in range(2):
        row = jnp.broadcast_to(layers_ref[i : i + 1, :], lane.shape)
        for g in range(spread_ref.shape[1] // SUB):
            one = jnp.sum(jnp.where(lane == SUB * g + sub, row, 0.0), axis=1, keepdims=True)
            spread_ref[i, tile_rows(g), :] = jnp.broadcast_to(one, lane.shape)
    nz, ny, nx = material_ref.shape
    keep = jnp.exp(-step_size / relax_ref[...])
    tables = table_rows(
        [
            buoy_ref[...] * (step_size / 12.0), lam_ref[...] / 12.0, mu_ref[...] / 12.0, keep,
            (1.0 - keep) * weight_ref[...],
        ],
        nx,
    )

    def layer(k):
        for t in range(ny // SUB):
            kind = material_ref[k, tile_rows(t), :]
            for i, table in enumerate(tables):
                cells_ref[i, k, tile_rows(t), :] = lookup(table, kind)

    over(0, nz, 8, layer)


def depth_kernel(stress_ref, velocity_hbm, depth_ref, along_ref, velocity_ref, sem):
    load = pltpu.make_async_copy(velocity_hbm, velocity_ref, sem)
    load.start()
    _, nz, ny, _ = stress_ref.shape
    along_all(stress_ref, (0, 3, 4), along_ref)
    over(2, nz - 2, 4, lambda k: inner_depth(stress_ref, depth_ref, 6, k, ny // SUB))
    load.wait()


def plane_kernel(
    sizes, stress_ref, along_ref, y1_ref, y2_ref, z1_ref, z2_ref, plane_ref, outer_ref, tall, zb, za
):
    depth_halos(sizes[2], zb, za, z1_ref, z2_ref)
    outer_depth(stress_ref, zb, za, outer_ref, 6, stress_ref.shape[1], stress_ref.shape[2] // SUB)
    _, nz, ny, nx = stress_ref.shape
    tiles = ny // SUB
    of_y = (3, 1, 5)
    fill_rows(sizes[1], tall, lambda c, k: stress_ref[of_y[c], k], y1_ref, y2_ref, nz, ny, range(nz))

    def layer(k):
        for t in range(tiles):
            for c in range(3):
                plane_ref[c, k, tile_rows(t), :] = along_ref[
                    c, k, tile_rows(t), :
                ] + row_difference(tall, c, k, t)

    over(0, nz, 16, layer)


def velocity_kernel(
    sizes, velocity_ref, cells_ref, inner_ref, outer_ref, plane_ref, factor_ref, mz_ref, slope_ref,
    x1_ref, x2_ref, low_ref, high_ref, out_ref, vlow_ref, vhigh_ref, vx1_ref, vx2_ref, vz1_ref, vz2_ref,
    *rest,
):
    *vy_refs, edge = rest
    _, nz, ny, nx = velocity_ref.shape
    tiles = ny // SUB
    lane = lanes_of((SUB, nx))
    fill_edges(sizes[0], edge, x1_ref, x2_ref, low_ref, high_ref)

    def layer(k, depth_ref, spot):
        for t in range(tiles):
            rows = tile_rows(t)
            b = cells_ref[0, k, rows, :]
            factor = factor_ref[k, rows, :]
            mz = mz_ref[k, rows, :]
            mx = slope_ref[0, rows, :] * factor
            my = slope_ref[1, rows, :] * factor
            gk = [depth_ref[c, spot, rows, :] for c in range(6)]
            beside = [
                plane_ref[c, k, rows, :]
                + jnp.where(sides(lane), turned_left(edge[c, t % 2], k * tiles + t), 0.0)
                for c in range(3)
            ]
            accel = (
                beside[0] - mx * gk[0] - my * gk[3] + mz * gk[4],
                beside[1] - mx * gk[3] - my * gk[1] + mz * gk[5],
                beside[2] - mx * gk[4] - my * gk[5] + mz * gk[2],
            )
            for c in range(3):
                out_ref[c, k, rows, :] = velocity_ref[c, k, rows, :] + b * accel[c]

    for spot, k in enumerate((0, 1, nz - 2, nz - 1)):
        layer(k, outer_ref, spot)

    over(2, nz - 2, 12, lambda k: layer(k, inner_ref, k - 2))
    pack_sides(
        lambda c, k, t: out_ref[c, k, tile_rows(t), :], nz, ny, nx, vlow_ref, vhigh_ref, vx1_ref, vx2_ref
    )
    pack_rows(lambda c, k, rows: out_ref[c, k, rows, :], nz, ny, vy_refs)
    vz1_ref[...], vz2_ref[...] = order("gz", out_ref[:, nz - 2 : nz], out_ref[:, 0:2])


def velocity_inner_kernel(vel_ref, vel_hbm, depth_ref, along_ref, across_ref, tall, sem):
    store = pltpu.make_async_copy(vel_ref, vel_hbm, sem)
    store.start()
    _, nz, ny, nx = vel_ref.shape
    tiles = ny // SUB

    along_all(vel_ref, (0, 1, 2), along_ref)
    over(2, nz - 2, 4, lambda k: inner_depth(vel_ref, depth_ref, 3, k, tiles))
    nothing = jnp.zeros((2, nx), F32)
    for c in range(3):
        for k in range(nz):
            tall[c, k, PAD : PAD + ny, :] = vel_ref[c, k]
            tall[c, k, PAD - 2 : PAD, :] = nothing
            tall[c, k, PAD + ny : PAD + ny + 2, :] = nothing

    def across(k):
        for t in range(tiles):
            for c in range(3):
                across_ref[c, k, tile_rows(t), :] = row_difference(tall, c, k, t)

    over(0, nz, 4, across)
    store.wait()


def fill_sides(n_gy, top, bottom, y1_ref, y2_ref):
    count = y1_ref.shape[0]
    got = (y1_ref[...], y2_ref[...])
    even_row = lax.broadcasted_iota(jnp.int32, got[0].shape, 0) % 2 == 0
    empty = jnp.zeros((SUB, y1_ref.shape[1]), F32)
    before, after = from_before("gy", got), from_after("gy", n_gy, got)
    top[:count, :] = before
    top[count:, :] = empty
    bottom[:SUB, :] = empty
    bottom[SUB:, :] = after
    top[:count, :] = jnp.where(even_row, before - 8.0 * top[1 : count + 1, :], before)
    bottom[SUB:, :] = jnp.where(even_row, -after, 8.0 * bottom[SUB - 1 : SUB + count - 1, :] - after)


def beside_rows(top, bottom, c, k, t, nz, tiles):
    j = 2 * (c * nz + k)
    row = lax.broadcasted_iota(jnp.int32, (SUB, top.shape[1]), 0)
    added = 0.0
    if t == 0:
        added = jnp.where(row < 2, top[pl.ds(j, SUB), :], 0.0)
    if t == tiles - 1:
        added = added + jnp.where(row >= SUB - 2, bottom[pl.ds(j + 2, SUB), :], 0.0)
    return added


def stress_kernel(
    sizes, vel_ref, stress_ref, memory_ref, cells_ref, inner_ref, along_ref, across_ref, factor_ref, mz_ref,
    slope_ref, x1_ref, x2_ref, low_ref, high_ref, y1_ref, y2_ref, z1_ref, z2_ref,
    stress_hbm, memory_hbm, edge, top, bottom, zb, za, outer, stress_out, memory_out, sems,
):
    n_gx, n_gy, n_gz = sizes
    _, nz, ny, nx = vel_ref.shape
    tiles = ny // SUB
    lane = lanes_of((SUB, nx))
    fill_edges(n_gx, edge, x1_ref, x2_ref, low_ref, high_ref)
    fill_sides(n_gy, top, bottom, y1_ref, y2_ref)

    def layer(k, depth_ref, spot):
        for t in range(tiles):
            rows = tile_rows(t)
            factor = factor_ref[k, rows, :]
            mz = mz_ref[k, rows, :]
            mx = slope_ref[0, rows, :] * factor
            my = slope_ref[1, rows, :] * factor
            dk = [depth_ref[c, spot, rows, :] for c in range(3)]
            dx = [
                along_ref[c, k, rows, :]
                + jnp.where(sides(lane), turned_left(edge[c, t % 2], k * tiles + t), 0.0)
                - mx * dk[c]
                for c in range(3)
            ]
            dy = [
                across_ref[c, k, rows, :] + beside_rows(top, bottom, c, k, t, nz, tiles) - my * dk[c]
                for c in range(3)
            ]
            dz = [mz * dk[c] for c in range(3)]
            lam, mu, keep, gain = (cells_ref[i, k, rows, :] for i in range(1, 5))
            volume = lam * (dx[0] + dy[1] + dz[2])
            mu2 = mu + mu
            rates = (
                volume + mu2 * dx[0],
                volume + mu2 * dy[1],
                volume + mu2 * dz[2],
                mu * (dy[0] + dx[1]),
                mu * (dz[0] + dx[2]),
                mu * (dz[1] + dy[2]),
            )
            for c in range(6):
                kept = keep * memory_ref[c, k, rows, :] + gain * rates[c]
                memory_out[c, k, rows, :] = kept
                stress_out[c, k, rows, :] = stress_ref[c, k, rows, :] + step_size * (
                    rates[c] - kept
                )

    pairs = ((stress_out, stress_hbm), (memory_out, memory_hbm))

    def send(first, count):
        layers = pl.ds(first, count)
        for i, (a, b) in enumerate(pairs):
            pltpu.make_async_copy(a.at[:, layers], b.at[:, layers], sems.at[i]).start()

    inner = nz - 4
    step = next(d for d in (4, 3, 2, 1) if inner % d == 0)

    for k in range(2, nz - 2):
        layer(k, inner_ref, k - 2)
        send(k, 1)

    depth_halos(n_gz, zb, za, z1_ref, z2_ref)
    outer_depth(vel_ref, zb, za, outer, 3, nz, tiles)
    for spot, k in enumerate((0, 1, nz - 2, nz - 1)):
        layer(k, outer, spot)
        send(k, 1)
    for i, (a, b) in enumerate(pairs):
        pltpu.make_async_copy(a, b, sems.at[i]).wait()


def in_hbm(value):
    return pltpu.with_memory_space_constraint(value, pltpu.HBM)


def call(kernel, outs, in_specs, scratch=(), name=None, out_specs=None, cost=0.0):
    return pl.pallas_call(
        kernel,
        out_shape=[jax.ShapeDtypeStruct(s, F32) for s in outs],
        in_specs=in_specs,
        out_specs=out_specs or [VM] * len(outs),
        scratch_shapes=list(scratch),
        compiler_params=params(),
        cost_estimate=pl.CostEstimate(flops=int(cost * 6e8), transcendentals=0, bytes_accessed=int(cost * 3.5e6)),
        name=name,
    )


def local(
    sizes, elevation, layer_base, stretch, material, buoyancy, lame_lambda, shear_modulus,
    relax_time, anelastic_weight, velocity, stress, memory,
):
    n_gx, n_gy, n_gz = counts = tuple(sizes[a] for a in ("gx", "gy", "gz"))
    _, nz, ny, nx = velocity.shape
    rows = ny + SUB
    rounds = pair_swaps(sizes, "gz")
    if n_gz == 4:
        piece = lax.ppermute(elevation, tuple(sizes), rounds[0])
    slab = call(
        terrain_piece_kernel,
        [(rows, nx)],
        [HB] * 3,
        [
            pltpu.VMEM(elevation.shape, jnp.int32),
            pltpu.VMEM((1, nz), F32),
            pltpu.VMEM((1, nz), F32),
            DMA((3,)),
        ],
        name="terrain_piece", cost=0.8,
    )(in_hbm(elevation), in_hbm(layer_base[None]), in_hbm(stretch[None]))[0]
    tied = lax.optimization_barrier
    faces = 2 * 3 * nz
    xs = 3 * SUB
    y_rounds = min(2, n_gy - 1) if n_gy > 1 else 1
    z_face = (6, 2, ny, nx)
    if n_gz == 4:
        slab = call(merge_kernel, [(rows, nx)], [VM] * 2, name="merge", cost=0.1)(slab, piece)[0]
        slab, stress = tied((slab, stress))
        slab = slab + lax.ppermute(slab, tuple(sizes), rounds[1])
        layers = slab[ny:]
    elif n_gz & (n_gz - 1):
        slab = lax.psum(slab, "gz")
        layers = slab[ny:]
    else:
        bit = 1
        while bit < n_gz:
            slab = slab + lax.ppermute(slab, "gz", [(i, i ^ bit) for i in range(n_gz)])
            if bit == 1:
                slab, stress = tied((slab, stress))
            bit *= 2
        layers = slab[ny:]
    stress_vm = stress
    low, high, x1, x2, z1, z2, *ys = call(
        pack_kernel,
        [(xs, nx)] * 4 + [z_face] * 2 + [(faces, nx)] * y_rounds,
        [VM],
        name="pack_stress", cost=0.5,
    )(stress)
    z1, z2 = exchange(sizes, "gz", z1, z2)
    ts = call(y_send_kernel, [(SUB, nx)] * y_rounds, [VM], name="y_send", cost=0.02)(slab)
    ts, ys, stress_vm, layers = tied((ts, ys, stress_vm, layers))
    t1, t2 = exchange(sizes, "gy", ts[0], ts[-1])
    y1, y2 = exchange(sizes, "gy", ys[0], ys[-1])
    if n_gz == 4:
        layers = layers + lax.ppermute(layers, tuple(sizes), rounds[0])
    inner_k, along, velocity_vm = call(
        depth_kernel,
        [(6, nz - 4, ny, nx), velocity.shape, velocity.shape],
        [VM, HB],
        [DMA],
        name="depth", cost=2.2,
    )(stress_vm, in_hbm(velocity))
    x1, x2, inner_k = tied((x1, x2, inner_k))
    terrain, x1, x2 = call(
        functools.partial(x_send_kernel, n_gy),
        [(ny + 2 * PAD, nx)] + [(xs + SUB, nx)] * 2,
        [VM] * 5,
        name="x_send", cost=0.1,
    )(slab, t1, t2, x1, x2)
    x1, x2, material = tied((x1, x2, material))
    x1, x2 = exchange(sizes, "gx", x1, x2, True)
    edge = pltpu.VMEM((3, 2, SUB, nx), F32)
    tall = pltpu.VMEM((3, nz, ny + 2 * PAD, nx), F32)

    def depth(comps):
        return [pltpu.VMEM((comps, 2, ny, nx), F32)] * 2

    tables = (buoyancy, lame_lambda, shear_modulus, relax_time, anelastic_weight)
    all_layers = -(-n_gz * nz // SUB) * SUB
    cells, spread = call(
        cell_kernel, [(5, nz, ny, nx), (2, all_layers, nx)], [VM] * 7, name="cells", cost=0.8
    )(layers, material, *[table[None] for table in tables])
    plane, outer_k = call(
        functools.partial(plane_kernel, counts),
        [velocity.shape, (6, 4, ny, nx)],
        [VM] * 6,
        [tall] + depth(6),
        name="planes", cost=0.6,
    )(stress_vm, along, y1, y2, z1, z2)
    plane, cells, x1, x2 = tied((plane, cells, x1, x2))
    factor, mz, slope = call(
        functools.partial(metric_kernel, counts),
        [(nz, ny, nx), (nz, ny, nx), (2, ny, nx)],
        [VM] * 4,
        [pltpu.VMEM((ny + 2 * PAD, nx), F32), pltpu.VMEM((ny + PAD, nx), F32)],
        name="metrics", cost=1.1,
    )(spread, terrain, x1[xs:], x2[xs:])
    vel, vlow, vhigh, vx1, vx2, vz1, vz2, *vys = call(
        functools.partial(velocity_kernel, counts),
        [velocity.shape] + [(xs, nx)] * 4 + [(3, 2, ny, nx)] * 2 + [(faces, nx)] * y_rounds,
        [VM] * 12,
        [edge],
        name="velocity", cost=1.5,
    )(velocity_vm, cells, inner_k, outer_k, plane, factor, mz, slope, x1, x2, low, high)
    vz1, vz2 = exchange(sizes, "gz", vz1, vz2)
    vy1, vy2 = exchange(sizes, "gy", vys[0], vys[-1])
    vx1, vx2 = exchange(sizes, "gx", vx1, vx2)
    vel_next, vel_k, vel_x, vel_y = call(
        velocity_inner_kernel,
        [velocity.shape, (3, nz - 4, ny, nx), velocity.shape, velocity.shape],
        [VM],
        [tall, DMA],
        name="velocity_inner", cost=0.1,
        out_specs=[HB, VM, VM, VM],
    )(vel)
    stress_next, memory_next = call(
        functools.partial(stress_kernel, counts),
        [stress.shape, stress.shape],
        [VM] * 18,
        [edge, pltpu.VMEM((faces + SUB, nx), F32), pltpu.VMEM((faces + SUB, nx), F32)]
        + depth(3)
        + [pltpu.VMEM((3, 4, ny, nx), F32), pltpu.VMEM(stress.shape, F32), pltpu.VMEM(stress.shape, F32)]
        + [DMA((2,))],
        name="stress", cost=2.8,
        out_specs=[HB] * 2,
    )(
        vel, stress_vm, memory, cells, vel_k, vel_x, vel_y, factor, mz, slope, vx1, vx2, vlow, vhigh, vy1, vy2,
        vz1, vz2,
    )
    return vel_next, stress_next, memory_next


def solution(mesh):
    sizes = {a: mesh.shape[a] for a in ("gx", "gy", "gz")}
    field = P(None, "gz", "gy", "gx")
    return jax.shard_map(
        functools.partial(local, sizes),
        mesh=mesh,
        in_specs=(
            P("gy", ("gx", "gz")), P("gz"), P("gz"), P("gz", "gy", "gx"),
            P(), P(), P(), P(), P(), field, field, field,
        ),
        out_specs=(field, field, field),
        check_vma=False,
    )
```
